256 devices in a mesh: dp: 64 (over y, z, core), tensor: 4 (over x).
Axes of the slice: x: 4, y: 4, z: 8, core: 2. Of those that a mesh axis runs over, the one named last changes fastest.
Arguments:
- activations: bfloat16 [65536, 4096], P(('dp', 'tensor')), may hold values from -6 to 6
- cotangent: bfloat16 [2, 65536, 1024], P(None, 'dp', 'tensor'), may hold values from -0.19921875 to 0.19921875
- error_memory: bfloat16 [2, 64, 4096, 1024], P(None, 'dp', None, 'tensor'), may hold values from -3 to 3
- right_factor: float32 [2, 1024, 32], P(None, 'tensor'), may hold values from -6 to 6
Outputs:
- new_error: bfloat16 [2, 64, 4096, 1024], P(None, 'dp', None, 'tensor')
- left_factor: float32 [2, 4, 4096, 32], P(None, 'tensor')
- mean_right: float32 [2, 1024, 32], P(None, 'tensor')
The draws below stay inside these ranges and needn't reach their ends.
All inputs are finite; a program needn't handle non-finite values.
Results may differ from the reference program's by a relative error of at most 0.00045.
Values may be sent and summed in bfloat16 or wider, within the bound.
A program may use at most 128 MiB of HBM per device.

```python
import jax
import jax.numpy as jnp
from jax import lax

DW = 4096
KVW = 1024
RANK = 32
TOK_DEV = 256
TOKENS = 65536
N_DP = 64
N_TENSOR = 4


def steps_of(rng, shape, shards, least, largest):
    loudness, own = 1.0, jax.random.fold_in(rng, 6)
    for dim, shards_of in shards:
        draws = jnp.exp(jax.random.uniform(jax.random.fold_in(own, dim), (shards_of,), jnp.float32, least / len(shards), largest / len(shards)))
        loudness = loudness * jnp.repeat(draws, shape[dim] // shards_of).reshape([-1 if axis == dim else 1 for axis in range(len(shape))])
    return loudness


def noise(stream_key, extent, spread, reach, shards=(), held_as=jnp.bfloat16):
    factor_of = steps_of(stream_key, extent, shards, -0.22, 0.18) if shards else 1.0
    drawn = jax.random.normal(stream_key, extent, jnp.float32) * spread * factor_of
    return jnp.minimum(jnp.maximum(drawn, -reach), reach).astype(held_as)


def setup_inputs(seed: int = 0) -> dict:
    keys = jax.random.split(jax.random.key(seed), 5)
    activations = noise(keys[0], (TOKENS, DW), 1.0, 6.0, ((0, 256),))
    cotangent = noise(keys[1], (2, TOKENS, KVW), 0.03125, 0.19921875, ((1, 64), (2, 4)))
    error_memory = noise(keys[2], (2, N_DP, DW, KVW), 0.5, 3.0, ((1, 64), (3, 4)))
    right_factor = noise(keys[3], (2, KVW, RANK), 1.0, 6.0, ((1, 4),), jnp.float32)
    return dict(activations=activations, cotangent=cotangent, error_memory=error_memory, right_factor=right_factor)


def orthonormal(summed):
    gram = jnp.dot(summed.T, summed, precision=lax.Precision.HIGHEST)
    lower = jnp.linalg.cholesky(gram)
    return lax.linalg.triangular_solve(lower, summed, left_side=False, lower=True, transpose_a=True)

def reference(activations, cotangent, error_memory, right_factor):
    tok_rep = TOK_DEV * N_TENSOR
    kv_cols = KVW // N_TENSOR
    x_groups = activations.reshape(N_DP, tok_rep, DW)
    errors_out = []
    lefts_out = []
    rights_out = []
    for matrix in range(2):
        dy_all = cotangent[matrix].reshape(N_DP, tok_rep, KVW)
        err_cols = []
        left_cols = []
        right_cols = []
        for column in range(N_TENSOR):
            lo_col = column * kv_cols
            dy_block = dy_all[:, :, lo_col:lo_col + kv_cols]
            err_block = error_memory[matrix, :, :, lo_col:lo_col + kv_cols]
            right_in = right_factor[matrix, lo_col:lo_col + kv_cols]

            def merged(items):
                xs, dys, errs = items
                return jnp.dot(xs.T.astype(jnp.float32), dys.astype(jnp.float32), preferred_element_type=jnp.float32) + errs.astype(jnp.float32)
            memory = lax.map(merged, (x_groups, dy_block, err_block))
            summed = jnp.einsum('gdk,kr->dr', memory, right_in, precision=lax.Precision.HIGHEST)
            left_hat = orthonormal(summed)
            mean_q = jnp.einsum('gdk,dr->kr', memory, left_hat, precision=lax.Precision.HIGHEST) / N_DP
            approx = jnp.dot(left_hat, mean_q.T, precision=lax.Precision.HIGHEST)
            err_cols.append((memory - approx[None]).astype(jnp.bfloat16))
            left_cols.append(left_hat)
            right_cols.append(mean_q)
        errors_out.append(jnp.concatenate(err_cols, axis=2))
        lefts_out.append(jnp.stack(left_cols, axis=0))
        rights_out.append(jnp.concatenate(right_cols, axis=0))
    return (jnp.stack(errors_out, axis=0), jnp.stack(lefts_out, axis=0), jnp.stack(rights_out, axis=0))
```

```python
import functools

import jax
import jax.numpy as jnp
from jax import lax
from jax.experimental import pallas as pl
from jax.experimental.pallas import tpu as pltpu
from jax.sharding import PartitionSpec as P

MESH = pl.DeviceIdType.MESH
BF = jnp.bfloat16
F32 = jnp.float32
NX = 4
RANK = 32
NT = (((1,), (1,)), ((), ()))
TN = (((0,), (0,)), ((), ()))


def split(value):
    high = value.astype(BF)
    return high, (value - high.astype(F32)).astype(BF)


def dot(a, b, dims=None):
    if dims is None:
        dims = (((1,), (0,)), ((), ()))
    return lax.dot_general(a, b, dims, preferred_element_type=F32)


def inverse_factor(gram):
    rows = lax.broadcasted_iota(jnp.int32, (RANK, 2 * RANK), 0)
    cols = lax.broadcasted_iota(jnp.int32, (RANK, 2 * RANK), 1)
    eye = jnp.where(cols == rows + RANK, 1.0, 0.0).astype(F32)
    wide = jnp.concatenate([gram, jnp.zeros((RANK, RANK), F32)], axis=1) + eye
    index = rows[:, :1]
    pivots = jnp.ones((RANK, 1), F32)
    for j in range(RANK):
        row = wide[j:j + 1, :]
        pivot = wide[j:j + 1, j:j + 1]
        column = wide[:, j:j + 1]
        factor = jnp.where(index > j, column * (1.0 / pivot), 0.0)
        pivots = jnp.where(index == j, pivot, pivots)
        wide = wide - factor * row
    return wide[:, RANK:] * (1.0 / jnp.sqrt(pivots))


def fused(NY, NZ, a_hbm, c_hbm, e_hbm, rt_hbm, mem_hbm, left_hbm, mean_ref,
          a, c, e, rt, v, vall, vl, rb, p, rc, ry, q, rz, sp, rx, s, sb, left, mem, t, tc, ty, t2, tz, tf,
          lsem, vs, vr, xs, xr, cs, cr, ys, yr, zs, zr, ws, wr, gzs, gzr, gys, gyr, gcs, gcr,
          tcs, tcr, tys, tyr, tzs, tzr, tgs, tgr, ths, thr):
    dp, x = lax.axis_index("dp"), lax.axis_index("tensor")
    core, yz = lax.rem(dp, 2), lax.div(dp, 2)
    z, y = lax.rem(yz, NZ), lax.div(yz, NZ)
    other = 1 - core
    tokens = a.shape[1]
    width = a.shape[2]
    kv = c.shape[2]
    span = NY * 128
    ndp = 2 * NY * NZ

    def at_x(k):
        return {"dp": dp, "tensor": lax.rem(x + k, NX)}

    def at_y(k):
        return {"dp": (lax.rem(y + k, NY) * NZ + z) * 2 + core, "tensor": x}

    def at_z(zz):
        return {"dp": (y * NZ + zz) * 2 + core, "tensor": x}

    partner = {"dp": yz * 2 + other, "tensor": x}

    def remote(src, dst, send, recv, device):
        return pltpu.make_async_remote_copy(src_ref=src, dst_ref=dst, send_sem=send, recv_sem=recv,
                                            device_id=device, device_id_type=MESH)

    load_a = pltpu.make_async_copy(a_hbm, a.at[x], lsem.at[0])
    load_c = pltpu.make_async_copy(c_hbm, c, lsem.at[1])
    load_e = pltpu.make_async_copy(e_hbm, e, lsem.at[2])
    load_r = pltpu.make_async_copy(rt_hbm, rt, lsem.at[3])
    load_r.start()
    load_c.start()
    load_a.start()
    load_e.start()

    barrier = pltpu.get_barrier_semaphore()
    for k in range(1, NX):
        pl.semaphore_signal(barrier, inc=1, device_id=at_x(k), device_id_type=MESH)
    for k in range(1, NY):
        pl.semaphore_signal(barrier, inc=1, device_id=at_y(k), device_id_type=MESH)
    for k in range(1, NZ):
        pl.semaphore_signal(barrier, inc=1, device_id=at_z(lax.rem(z + k, NZ)), device_id_type=MESH)
    pl.semaphore_signal(barrier, inc=1, device_id=partner, device_id_type=MESH)

    load_r.wait()
    load_c.wait()
    for m in range(2):
        high, low = split(rt[m])
        rb[m] = jnp.concatenate([high, low], axis=0)
        both = dot(rb[m], c[m], NT)
        vt = both[:RANK] + both[RANK:]
        for b in range(NX):
            v[b, m * RANK:(m + 1) * RANK, :] = vt[:, b * tokens:(b + 1) * tokens]

    pl.semaphore_wait(barrier, NX + NY + NZ - 2)

    v_copies = []
    for k in range(1, NX):
        copy = remote(v.at[lax.rem(x + k, NX)], vall.at[x], vs.at[k - 1], vr.at[k - 1], at_x(k))
        copy.start()
        v_copies.append(copy)

    half = tokens // 2
    left_x, right_x = lax.rem(x + NX - 1, NX), lax.rem(x + 1, NX)
    far_x = lax.rem(x + 2, NX)
    right_dev, left_dev = at_x(1), at_x(NX - 1)

    def rows(slot, h):
        return a.at[slot, pl.ds(h * half, half)]

    load_a.wait()
    send_r0 = remote(rows(x, 0), rows(x, 0), xs.at[0], xr.at[0], right_dev)
    send_l1 = remote(rows(x, 1), rows(x, 1), xs.at[3], xr.at[3], left_dev)
    send_r1 = remote(rows(x, 1), rows(x, 1), xs.at[1], xr.at[1], right_dev)
    send_l0 = remote(rows(x, 0), rows(x, 0), xs.at[2], xr.at[2], left_dev)
    for copy in (send_r0, send_l1, send_r1, send_l0):
        copy.start()
    forward_r = remote(rows(left_x, 0), rows(left_x, 0), xs.at[4], xr.at[4], right_dev)
    forward_l = remote(rows(right_x, 1), rows(right_x, 1), xs.at[5], xr.at[5], left_dev)

    def arrived(slot, h, sem):
        remote(rows(slot, h), rows(slot, h), xs.at[sem], xr.at[sem], right_dev).wait_recv()

    vall[x] = v[x]
    for k in range(1, NX):
        src = lax.rem(x + NX - k, NX)
        remote(v.at[0], vall.at[src], vs.at[k - 1], vr.at[k - 1], at_x(k)).wait_recv()
    stacked = jnp.concatenate(
        [vall[b, m * RANK:(m + 1) * RANK, :] for m in range(2) for b in range(NX)], axis=0)
    high, low = split(stacked)
    block = 2 * NX * RANK
    vl[:block] = high
    vl[block:] = low

    load_e.wait()

    def partials(j, carry):
        zj = lax.rem(z + 1 + j, NZ)
        at = pl.ds(pl.multiple_of(zj * span, span), span)
        both = dot(vl[...], a[x, :, at])
        both = both[:block] + both[block:]
        for m in range(2):
            for yb in range(NY):
                for b in range(NX):
                    r0 = (m * NX + b) * RANK
                    p[m, zj, yb, b] = both[r0:r0 + RANK, yb * 128:(yb + 1) * 128]
        for m in range(2):
            et = dot(rb[m], e[m, at, :], NT)
            et = et[:RANK] + et[RANK:]
            for yb in range(NY):
                p[m, zj, yb, x] = p[m, zj, yb, x] + et[:, yb * 128:(yb + 1) * 128]
        remote(p.at[other, zj], rc.at[zj], cs.at[zj], cr.at[zj], partner).start()
        return carry

    lax.fori_loop(0, NZ, partials, 0)

    def over_cores(j, carry):
        zj = lax.rem(z + 1 + j, NZ)
        remote(p.at[other, zj], rc.at[zj], cs.at[zj], cr.at[zj], partner).wait_recv()
        p[core, zj] = p[core, zj] + rc[zj]
        for k in range(1, NY):
            remote(p.at[core, zj, lax.rem(y + k, NY)], ry.at[k - 1, zj], ys.at[k - 1, zj], yr.at[k - 1, zj],
                   at_y(k)).start()
        return carry

    lax.fori_loop(0, NZ, over_cores, 0)

    step = min(512, width)

    def accumulate(slot, first):
        tok = pl.ds(pl.multiple_of(slot * tokens, tokens), tokens)
        cc = jnp.concatenate([c[0, tok, :], c[1, tok, :]], axis=1)

        def body(i, carry):
            at = pl.ds(pl.multiple_of(i * step, step), step)
            g = dot(a[slot, :, at], cc, TN)
            for m in range(2):
                base = e[m, at, :].astype(F32) if first else mem[m, at, :]
                mem[m, at, :] = base + g[:, m * kv:(m + 1) * kv]
            return carry

        lax.fori_loop(0, width // step, body, 0)

    accumulate(x, True)

    def over_y(zj):
        total = p[core, zj, y]
        for k in range(1, NY):
            remote(p.at[core, zj, y], ry.at[k - 1, zj], ys.at[k - 1, zj], yr.at[k - 1, zj], partner).wait_recv()
            total = total + ry[k - 1, zj]
        q[zj] = total

    def over_y_send(j, carry):
        zj = lax.rem(z + 1 + j, NZ)
        over_y(zj)
        remote(q.at[zj], rz.at[j], zs.at[j], zr.at[j], at_z(zj)).start()
        return carry

    lax.fori_loop(0, NZ - 1, over_y_send, 0)
    over_y(z)

    arrived(left_x, 0, 0)
    forward_r.start()
    arrived(right_x, 1, 3)
    forward_l.start()

    total = q[z]
    for j in range(NZ - 1):
        remote(q.at[z], rz.at[j], zs.at[j], zr.at[j], partner).wait_recv()
        total = total + rz[j]
    sp[...] = total

    for k in range(1, NX):
        remote(sp.at[lax.rem(x + k, NX)], rx.at[k - 1], ws.at[k - 1], wr.at[k - 1], at_x(k)).start()
    total = sp[x]
    for k in range(1, NX):
        remote(sp.at[0], rx.at[k - 1], ws.at[k - 1], wr.at[k - 1], at_x(k)).wait_recv()
        total = total + rx[k - 1]
    s[core, z, y] = total

    own = s.at[core, z, y]
    for k in range(1, NZ):
        remote(own, own, gzs.at[k - 1], gzr.at[k - 1], at_z(lax.rem(z + k, NZ))).start()
    for k in range(1, NZ):
        got = s.at[core, lax.rem(z + NZ - k, NZ), y]
        remote(got, got, gzs.at[k - 1], gzr.at[k - 1], partner).wait_recv()
    own_y = s.at[core, :, y]
    for k in range(1, NY):
        remote(own_y, own_y, gys.at[k - 1], gyr.at[k - 1], at_y(k)).start()
    for k in range(1, NY):
        got = s.at[core, :, lax.rem(y + NY - k, NY)]
        remote(got, got, gys.at[k - 1], gyr.at[k - 1], partner).wait_recv()
    remote(s.at[core], s.at[core], gcs.at[0], gcr.at[0], partner).start()
    remote(s.at[other], s.at[other], gcs.at[0], gcr.at[0], partner).wait_recv()

    for m in range(2):
        for zz in range(NZ):
            for yy in range(NY):
                d0 = (zz * NY + yy) * 128
                high, low = split(s[m, zz, yy])
                sb[m * 64:m * 64 + 32, d0:d0 + 128] = high
                sb[m * 64 + 32:m * 64 + 64, d0:d0 + 128] = low

    right = []
    for m in range(2):
        both = dot(sb[m * 64:m * 64 + 64, :], e[m])
        right.append(both[:RANK] + both[RANK:])

    def project(slot):
        tok = pl.ds(pl.multiple_of(slot * tokens, tokens), tokens)
        u = dot(sb[...], a[slot], NT)
        for m in range(2):
            high, low = split(u[m * 64:m * 64 + 32] + u[m * 64 + 32:m * 64 + 64])
            both = dot(jnp.concatenate([high, low], axis=0), c[m, tok, :])
            right[m] = right[m] + both[:RANK] + both[RANK:]

    project(x)

    inverse = []
    for m in range(2):
        both = dot(sb[m * 64:m * 64 + 64, :], sb[m * 64:m * 64 + 64, :], NT)
        inverse.append(inverse_factor(
            both[:RANK, :RANK] + both[:RANK, RANK:] + both[RANK:, :RANK] + both[RANK:, RANK:]))
    for m in range(2):
        high, low = split(inverse[m])
        pair = jnp.concatenate([high, low], axis=0)
        for i in range(width // step):
            at = pl.ds(i * step, step)
            both = dot(pair, sb[m * 64:m * 64 + 32, at])
            left[m, :, at] = both[:RANK] + both[RANK:] + dot(high, sb[m * 64 + 32:m * 64 + 64, at])
    store_left = pltpu.make_async_copy(left, left_hbm, lsem.at[4])
    store_left.start()

    arrived(left_x, 1, 1)
    project(left_x)
    accumulate(left_x, False)
    arrived(right_x, 0, 2)
    project(right_x)
    accumulate(right_x, False)
    arrived(far_x, 0, 4)
    arrived(far_x, 1, 5)
    project(far_x)

    group = t.shape[2]
    per_row = kv // 128

    def piece(i):
        return i // group, i % group

    for m in range(2):
        for i in range(NZ * group):
            rr, kk = i // per_row, i % per_row
            t[(m,) + piece(i)] = right[m][rr * 8:rr * 8 + 8, kk * 128:kk * 128 + 128]
    t_core = remote(t.at[other], tc, tcs.at[0], tcr.at[0], partner)
    t_core.start()
    t_core.wait_recv()
    t[core] = t[core] + tc[...]
    for k in range(1, NY):
        remote(t.at[core], ty.at[k - 1], tys.at[k - 1], tyr.at[k - 1], at_y(k)).start()
    accumulate(far_x, False)
    store_mem = pltpu.make_async_copy(mem, mem_hbm, lsem.at[5])
    store_mem.start()
    total = t[core]
    for k in range(1, NY):
        remote(t.at[core], ty.at[k - 1], tys.at[k - 1], tyr.at[k - 1], partner).wait_recv()
        total = total + ty[k - 1]
    t2[...] = total
    for k in range(1, NZ):
        zk = lax.rem(z + k, NZ)
        remote(t2.at[zk], tz.at[k - 1], tzs.at[k - 1], tzr.at[k - 1], at_z(zk)).start()
    total = t2[z]
    for k in range(1, NZ):
        remote(t2.at[z], tz.at[k - 1], tzs.at[k - 1], tzr.at[k - 1], partner).wait_recv()
        total = total + tz[k - 1]
    tf[core, z] = total
    own = tf.at[core, z]
    for k in range(1, NZ):
        remote(own, own, tgs.at[k - 1], tgr.at[k - 1], at_z(lax.rem(z + k, NZ))).start()
    for k in range(1, NZ):
        got = tf.at[core, lax.rem(z + NZ - k, NZ)]
        remote(got, got, tgs.at[k - 1], tgr.at[k - 1], partner).wait_recv()
    remote(tf.at[core], tf.at[core], ths.at[0], thr.at[0], partner).start()
    remote(tf.at[other], tf.at[other], ths.at[0], thr.at[0], partner).wait_recv()

    for m in range(2):
        tt = jnp.concatenate(
            [jnp.concatenate([tf[(m,) + piece(rr * per_row + kk)] for kk in range(per_row)], axis=1)
             for rr in range(RANK // 8)], axis=0)
        wh, wl = split(inverse[m])
        th, tl = split(tt)
        both = dot(jnp.concatenate([wh, wl], axis=0), th)
        mean_ref[m] = (both[:RANK] + both[RANK:] + dot(wh, tl)) * (1.0 / ndp)

    for copy in v_copies + [send_r0, send_l1, send_r1, send_l0, forward_r, forward_l]:
        copy.wait_send()

    def sent(j, carry):
        remote(p.at[other, j], rc.at[j], cs.at[j], cr.at[j], partner).wait_send()
        for k in range(1, NY):
            remote(p.at[core, j, y], ry.at[k - 1, j], ys.at[k - 1, j], yr.at[k - 1, j], partner).wait_send()
        return carry

    lax.fori_loop(0, NZ, sent, 0)
    for j in range(NZ - 1):
        remote(q.at[j], rz.at[j], zs.at[j], zr.at[j], partner).wait_send()
        got = s.at[core, z, y]
        remote(got, got, gzs.at[j], gzr.at[j], partner).wait_send()
        remote(t2.at[0], tz.at[j], tzs.at[j], tzr.at[j], partner).wait_send()
        remote(tf.at[core, z], tf.at[core, z], tgs.at[j], tgr.at[j], partner).wait_send()
    for k in range(NX - 1):
        remote(sp.at[0], rx.at[k], ws.at[k], wr.at[k], partner).wait_send()
    for k in range(NY - 1):
        remote(own_y, own_y, gys.at[k], gyr.at[k], partner).wait_send()
        remote(t.at[core], ty.at[k], tys.at[k], tyr.at[k], partner).wait_send()
    remote(s.at[core], s.at[core], gcs.at[0], gcr.at[0], partner).wait_send()
    remote(t.at[other], tc, tcs.at[0], tcr.at[0], partner).wait_send()
    remote(tf.at[core], tf.at[core], ths.at[0], thr.at[0], partner).wait_send()
    store_left.wait()
    store_mem.wait()


def residual(mem_ref, left_ref, mean_ref, out_ref, left_out, mean_out):
    lt = left_ref[0]
    left_out[0] = lt
    mean = mean_ref[0]
    mean_out[0] = mean
    lh, ll = split(lt)
    mh, ml = split(mean)
    approx = dot(jnp.concatenate([lh, ll, lh], axis=0), jnp.concatenate([mh, mh, ml], axis=0), TN)
    out_ref[0] = (mem_ref[0] - approx).astype(BF)


def shards(NY, NZ, activations, cotangent, error_memory, right_factor):
    tokens, width = activations.shape
    kv = cotangent.shape[2]
    error_memory = error_memory[:, 0]
    group = RANK * kv // (8 * 128 * NZ)
    dma = pltpu.SemaphoreType.DMA
    any_spec = pl.BlockSpec(memory_space=pl.ANY)
    mem, left, mean = pl.pallas_call(
        functools.partial(fused, NY, NZ),
        out_shape=(
            jax.ShapeDtypeStruct((2, width, kv), F32),
            jax.ShapeDtypeStruct((2, RANK, width), F32),
            jax.ShapeDtypeStruct((2, RANK, kv), F32),
        ),
        in_specs=[any_spec] * 4,
        out_specs=(any_spec, any_spec, pl.BlockSpec(memory_space=pltpu.VMEM)),
        scratch_shapes=[
            pltpu.VMEM((NX, tokens, width), BF),
            pltpu.VMEM((2, NX * tokens, kv), BF),
            pltpu.VMEM((2, width, kv), BF),
            pltpu.VMEM((2, RANK, kv), F32),
            pltpu.VMEM((NX, 2 * RANK, tokens), F32),
            pltpu.VMEM((NX, 2 * RANK, tokens), F32),
            pltpu.VMEM((4 * NX * RANK, tokens), BF),
            pltpu.VMEM((2, 2 * RANK, kv), BF),
            pltpu.VMEM((2, NZ, NY, NX, RANK, 128), F32),
            pltpu.VMEM((NZ, NY, NX, RANK, 128), F32),
            pltpu.VMEM((NY - 1, NZ, NX, RANK, 128), F32),
            pltpu.VMEM((NZ, NX, RANK, 128), F32),
            pltpu.VMEM((NZ - 1, NX, RANK, 128), F32),
            pltpu.VMEM((NX, RANK, 128), F32),
            pltpu.VMEM((NX - 1, RANK, 128), F32),
            pltpu.VMEM((2, NZ, NY, RANK, 128), F32),
            pltpu.VMEM((4 * RANK, width), BF),
            pltpu.VMEM((2, RANK, width), F32),
            pltpu.VMEM((2, width, kv), F32),
            pltpu.VMEM((2, NZ, group, 8, 128), F32),
            pltpu.VMEM((NZ, group, 8, 128), F32),
            pltpu.VMEM((NY - 1, NZ, group, 8, 128), F32),
            pltpu.VMEM((NZ, group, 8, 128), F32),
            pltpu.VMEM((NZ - 1, group, 8, 128), F32),
            pltpu.VMEM((2, NZ, group, 8, 128), F32),
            dma((6,)),
            dma((NX - 1,)), dma((NX - 1,)),
            dma((6,)), dma((6,)),
            dma((NZ,)), dma((NZ,)),
            dma((NY - 1, NZ)), dma((NY - 1, NZ)),
            dma((NZ - 1,)), dma((NZ - 1,)),
            dma((NX - 1,)), dma((NX - 1,)),
            dma((NZ - 1,)), dma((NZ - 1,)),
            dma((NY - 1,)), dma((NY - 1,)),
            dma((1,)), dma((1,)),
            dma((1,)), dma((1,)),
            dma((NY - 1,)), dma((NY - 1,)),
            dma((NZ - 1,)), dma((NZ - 1,)),
            dma((NZ - 1,)), dma((NZ - 1,)),
            dma((1,)), dma((1,)),
        ],
        compiler_params=pltpu.CompilerParams(
            collective_id=0, has_side_effects=True, vmem_limit_bytes=56 * 1024 * 1024),
    )(activations, cotangent, error_memory, jnp.swapaxes(right_factor, 1, 2))

    rows = min(1024, width)
    new_error, left, mean = pl.pallas_call(
        residual,
        grid=(2, width // rows),
        out_shape=(
            jax.ShapeDtypeStruct((2, width, kv), BF),
            jax.ShapeDtypeStruct((2, RANK, width), F32),
            jax.ShapeDtypeStruct((2, RANK, kv), F32),
        ),
        in_specs=[
            pl.BlockSpec((1, rows, kv), lambda m, i: (m, i, 0)),
            pl.BlockSpec((1, RANK, rows), lambda m, i: (m, 0, i)),
            pl.BlockSpec((1, RANK, kv), lambda m, i: (m, 0, 0)),
        ],
        out_specs=(
            pl.BlockSpec((1, rows, kv), lambda m, i: (m, i, 0)),
            pl.BlockSpec((1, RANK, rows), lambda m, i: (m, 0, i)),
            pl.BlockSpec((1, RANK, kv), lambda m, i: (m, 0, 0)),
        ),
        compiler_params=pltpu.CompilerParams(vmem_limit_bytes=32 * 1024 * 1024),
    )(mem, left, mean)
    return (new_error[:, None], jnp.swapaxes(left, 1, 2)[:, None], jnp.swapaxes(mean, 1, 2))


def build(mesh, NY, NZ):
    return jax.shard_map(
        functools.partial(shards, NY, NZ),
        mesh=mesh,
        in_specs=(
            P(("dp", "tensor"), None),
            P(None, "dp", "tensor"),
            P(None, "dp", None, "tensor"),
            P(None, "tensor", None),
        ),
        out_specs=(
            P(None, "dp", None, "tensor"),
            P(None, "tensor", None, None),
            P(None, "tensor", None),
        ),
        check_vma=False,
    )


def solution(mesh):
    return build(mesh, 4, mesh.shape["dp"] // 8)
```

```python
import functools

import jax
import jax.numpy as jnp
from jax import lax
from jax.experimental import pallas as pl
from jax.experimental.pallas import tpu as pltpu
from jax.sharding import PartitionSpec as P

MESH = pl.DeviceIdType.MESH
BF = jnp.bfloat16
F32 = jnp.float32
NX = 4
RANK = 32
NT = (((1,), (1,)), ((), ()))
TN = (((0,), (0,)), ((), ()))


def split(value):
    high = value.astype(BF)
    return high, (value - high.astype(F32)).astype(BF)


def dot(a, b, dims=None):
    if dims is None:
        dims = (((1,), (0,)), ((), ()))
    return lax.dot_general(a, b, dims, preferred_element_type=F32)


def inverse_factor(gram):
    rows = lax.broadcasted_iota(jnp.int32, (RANK, 2 * RANK), 0)
    cols = lax.broadcasted_iota(jnp.int32, (RANK, 2 * RANK), 1)
    eye = jnp.where(cols == rows + RANK, 1.0, 0.0).astype(F32)
    wide = jnp.concatenate([gram, jnp.zeros((RANK, RANK), F32)], axis=1) + eye
    index = rows[:, :1]
    pivots = jnp.ones((RANK, 1), F32)
    for j in range(RANK):
        row = wide[j:j + 1, :]
        pivot = wide[j:j + 1, j:j + 1]
        column = wide[:, j:j + 1]
        factor = jnp.where(index > j, column * (1.0 / pivot), 0.0)
        pivots = jnp.where(index == j, pivot, pivots)
        wide = wide - factor * row
    return wide[:, RANK:] * (1.0 / jnp.sqrt(pivots))


def fused(NY, NZ, a_hbm, c_hbm, e_hbm, rt_hbm, mem_hbm, left_hbm, mean_ref,
          a, c, e, rt, v, vall, vl, rb, p, rc, fy, ry, q, rz, sp, rx, s, sb, left, mem, t, ta, t2, ty, tf,
          lsem, vs, vr, xs, xr, cs, cr, fs, fr, ys, yr, zs, zr, ws, wr, gzs, gzr, gys, gyr, gcs, gcr,
          tas, tar, tys, tyr, tgs, tgr):
    dp, x = lax.axis_index("dp"), lax.axis_index("tensor")
    core, yz = lax.rem(dp, 2), lax.div(dp, 2)
    z, y = lax.rem(yz, NZ), lax.div(yz, NZ)
    other = 1 - core
    tokens = a.shape[1]
    width = a.shape[2]
    kv = c.shape[2]
    span = NY * 128
    ndp = 2 * NY * NZ

    def at_x(k):
        return {"dp": dp, "tensor": lax.rem(x + k, NX)}

    def at_y(k):
        return {"dp": (lax.rem(y + k, NY) * NZ + z) * 2 + core, "tensor": x}

    def at_zc(zz, cc):
        return {"dp": (y * NZ + zz) * 2 + cc, "tensor": x}

    def at_z(zz):
        return at_zc(zz, core)

    partner = at_zc(z, other)
    plane = [(d, k) for d in range(2) for k in range(NZ) if d + k]

    def remote(src, dst, send, recv, device):
        return pltpu.make_async_remote_copy(src_ref=src, dst_ref=dst, send_sem=send, recv_sem=recv,
                                            device_id=device, device_id_type=MESH)

    load_a = pltpu.make_async_copy(a_hbm, a.at[x], lsem.at[0])
    load_c = pltpu.make_async_copy(c_hbm, c, lsem.at[1])
    load_e = pltpu.make_async_copy(e_hbm, e, lsem.at[2])
    load_r = pltpu.make_async_copy(rt_hbm, rt, lsem.at[3])
    load_r.start()
    load_c.start()
    load_a.start()
    load_e.start()

    barrier = pltpu.get_barrier_semaphore()
    for k in range(1, NX):
        pl.semaphore_signal(barrier, inc=1, device_id=at_x(k), device_id_type=MESH)
    for k in range(1, NY):
        pl.semaphore_signal(barrier, inc=1, device_id=at_y(k), device_id_type=MESH)
    for d, k in plane:
        pl.semaphore_signal(barrier, inc=1, device_id=at_zc(lax.rem(z + k, NZ), (core, other)[d]), device_id_type=MESH)

    load_r.wait()
    load_c.wait()
    for m in range(2):
        high, low = split(rt[m])
        rb[m] = jnp.concatenate([high, low], axis=0)
        both = dot(rb[m], c[m], NT)
        vt = both[:RANK] + both[RANK:]
        for b in range(NX):
            v[b, m * RANK:(m + 1) * RANK, :] = vt[:, b * tokens:(b + 1) * tokens]

    pl.semaphore_wait(barrier, NX + NY + 2 * NZ - 3)

    v_copies = []
    for k in range(1, NX):
        copy = remote(v.at[lax.rem(x + k, NX)], vall.at[x], vs.at[k - 1], vr.at[k - 1], at_x(k))
        copy.start()
        v_copies.append(copy)

    half = tokens // 2
    left_x, right_x = lax.rem(x + NX - 1, NX), lax.rem(x + 1, NX)
    far_x = lax.rem(x + 2, NX)
    right_dev, left_dev = at_x(1), at_x(NX - 1)

    def rows(slot, h):
        return a.at[slot, pl.ds(h * half, half)]

    load_a.wait()
    send_r0 = remote(rows(x, 0), rows(x, 0), xs.at[0], xr.at[0], right_dev)
    send_l1 = remote(rows(x, 1), rows(x, 1), xs.at[3], xr.at[3], left_dev)
    send_r1 = remote(rows(x, 1), rows(x, 1), xs.at[1], xr.at[1], right_dev)
    send_l0 = remote(rows(x, 0), rows(x, 0), xs.at[2], xr.at[2], left_dev)
    send_r0.start()
    send_l1.start()
    forward_r = remote(rows(left_x, 0), rows(left_x, 0), xs.at[4], xr.at[4], right_dev)
    forward_l = remote(rows(right_x, 1), rows(right_x, 1), xs.at[5], xr.at[5], left_dev)

    def arrived(slot, h, sem):
        remote(rows(slot, h), rows(slot, h), xs.at[sem], xr.at[sem], right_dev).wait_recv()

    vall[x] = v[x]
    for k in range(1, NX):
        src = lax.rem(x + NX - k, NX)
        remote(v.at[0], vall.at[src], vs.at[k - 1], vr.at[k - 1], at_x(k)).wait_recv()
    stacked = jnp.concatenate(
        [vall[b, m * RANK:(m + 1) * RANK, :] for m in range(2) for b in range(NX)], axis=0)
    high, low = split(stacked)
    block = 2 * NX * RANK
    vl[:block] = high
    vl[block:] = low

    load_e.wait()

    def partials(j, carry):
        zj = lax.rem(z + 1 + j, NZ)
        at = pl.ds(pl.multiple_of(zj * span, span), span)
        both = dot(vl[...], a[x, :, at])
        both = both[:block] + both[block:]
        for m in range(2):
            for yb in range(NY):
                for b in range(NX):
                    r0 = (m * NX + b) * RANK
                    p[m, zj, yb, b] = both[r0:r0 + RANK, yb * 128:(yb + 1) * 128]
        for m in range(2):
            et = dot(rb[m], e[m, at, :], NT)
            et = et[:RANK] + et[RANK:]
            for yb in range(NY):
                p[m, zj, yb, x] = p[m, zj, yb, x] + et[:, yb * 128:(yb + 1) * 128]
        remote(p.at[other, zj], rc.at[zj], cs.at[zj], cr.at[zj], partner).start()
        return carry

    lax.fori_loop(0, NZ, partials, 0)

    hc = NX // 2
    up, down, far_y = lax.rem(y + 1, NY), lax.rem(y + NY - 1, NY), lax.rem(y + 2, NY)
    to_up, to_down = at_y(1), at_y(NY - 1)

    def over_cores(j, carry):
        zj = lax.rem(z + 1 + j, NZ)
        remote(p.at[other, zj], rc.at[zj], cs.at[zj], cr.at[zj], partner).wait_recv()
        p[core, zj] = p[core, zj] + rc[zj]
        remote(p.at[core, zj, far_y, pl.ds(0, hc)], fy.at[0, zj], fs.at[0, zj], fr.at[0, zj], to_up).start()
        remote(p.at[core, zj, far_y, pl.ds(hc, hc)], fy.at[1, zj], fs.at[1, zj], fr.at[1, zj], to_down).start()
        return carry

    lax.fori_loop(0, NZ, over_cores, 0)

    send_r1.start()
    send_l0.start()

    def to_neighbours(j, carry):
        zj = lax.rem(z + 1 + j, NZ)
        for i, target, device in ((0, up, to_up), (1, down, to_down)):
            part = pl.ds(i * hc, hc)
            remote(p.at[core, zj, far_y, part], fy.at[i, zj], fs.at[i, zj], fr.at[i, zj], device).wait_recv()
            p[core, zj, target, part] = p[core, zj, target, part] + fy[i, zj]
            remote(p.at[core, zj, target], ry.at[i, zj], ys.at[i, zj], yr.at[i, zj], device).start()
        return carry

    lax.fori_loop(0, NZ, to_neighbours, 0)

    step = min(512, width)

    def accumulate(slot, first):
        tok = pl.ds(pl.multiple_of(slot * tokens, tokens), tokens)
        cc = jnp.concatenate([c[0, tok, :], c[1, tok, :]], axis=1)

        def body(i, carry):
            at = pl.ds(pl.multiple_of(i * step, step), step)
            g = dot(a[slot, :, at], cc, TN)
            for m in range(2):
                base = e[m, at, :].astype(F32) if first else mem[m, at, :]
                mem[m, at, :] = base + g[:, m * kv:(m + 1) * kv]
            return carry

        lax.fori_loop(0, width // step, body, 0)

    accumulate(x, True)

    def over_y(zj):
        total = p[core, zj, y]
        for i in range(2):
            remote(p.at[core, zj, y], ry.at[i, zj], ys.at[i, zj], yr.at[i, zj], partner).wait_recv()
            total = total + ry[i, zj]
        q[zj] = total

    def over_y_send(j, carry):
        zj = lax.rem(z + 1 + j, NZ)
        over_y(zj)
        remote(q.at[zj], rz.at[j], zs.at[j], zr.at[j], at_z(zj)).start()
        return carry

    lax.fori_loop(0, NZ - 1, over_y_send, 0)
    over_y(z)

    arrived(left_x, 0, 0)
    forward_r.start()
    arrived(right_x, 1, 3)
    forward_l.start()

    total = q[z]
    for j in range(NZ - 1):
        remote(q.at[z], rz.at[j], zs.at[j], zr.at[j], partner).wait_recv()
        total = total + rz[j]
    sp[...] = total

    for k in range(1, NX):
        remote(sp.at[lax.rem(x + k, NX)], rx.at[k - 1], ws.at[k - 1], wr.at[k - 1], at_x(k)).start()
    total = sp[x]
    for k in range(1, NX):
        remote(sp.at[0], rx.at[k - 1], ws.at[k - 1], wr.at[k - 1], at_x(k)).wait_recv()
        total = total + rx[k - 1]
    s[core, z, y] = total

    own = s.at[core, z, y]
    for k in range(1, NZ):
        remote(own, own, gzs.at[k - 1], gzr.at[k - 1], at_z(lax.rem(z + k, NZ))).start()
    for k in range(1, NZ):
        got = s.at[core, lax.rem(z + NZ - k, NZ), y]
        remote(got, got, gzs.at[k - 1], gzr.at[k - 1], partner).wait_recv()
    own_y = s.at[core, :, y]
    hz = NZ // 2
    remote(own_y, own_y, gys.at[0], gyr.at[0], to_up).start()
    remote(own_y, own_y, gys.at[1], gyr.at[1], to_down).start()
    arrived(left_x, 1, 1)
    accumulate(left_x, False)
    pass_up, pass_down = s.at[core, pl.ds(0, hz), down], s.at[core, pl.ds(hz, hz), up]
    remote(s.at[core, :, down], s.at[core, :, down], gys.at[0], gyr.at[0], to_up).wait_recv()
    remote(pass_up, pass_up, gys.at[2], gyr.at[2], to_up).start()
    remote(s.at[core, :, up], s.at[core, :, up], gys.at[1], gyr.at[1], to_down).wait_recv()
    remote(pass_down, pass_down, gys.at[3], gyr.at[3], to_down).start()
    arrived(right_x, 0, 2)
    accumulate(right_x, False)
    for i in range(2):
        got = s.at[core, pl.ds(i * hz, hz), far_y]
        remote(got, got, gys.at[2 + i], gyr.at[2 + i], partner).wait_recv()
    remote(s.at[core], s.at[core], gcs.at[0], gcr.at[0], partner).start()
    remote(s.at[other], s.at[other], gcs.at[0], gcr.at[0], partner).wait_recv()

    for m in range(2):
        for zz in range(NZ):
            for yy in range(NY):
                d0 = (zz * NY + yy) * 128
                high, low = split(s[m, zz, yy])
                sb[m * 64:m * 64 + 32, d0:d0 + 128] = high
                sb[m * 64 + 32:m * 64 + 64, d0:d0 + 128] = low

    right = []
    for m in range(2):
        both = dot(sb[m * 64:m * 64 + 64, :], e[m])
        right.append(both[:RANK] + both[RANK:])

    def project(slot):
        tok = pl.ds(pl.multiple_of(slot * tokens, tokens), tokens)
        u = dot(sb[...], a[slot], NT)
        for m in range(2):
            high, low = split(u[m * 64:m * 64 + 32] + u[m * 64 + 32:m * 64 + 64])
            both = dot(jnp.concatenate([high, low], axis=0), c[m, tok, :])
            right[m] = right[m] + both[:RANK] + both[RANK:]

    project(x)
    project(left_x)
    project(right_x)

    inverse = []
    for m in range(2):
        both = dot(sb[m * 64:m * 64 + 64, :], sb[m * 64:m * 64 + 64, :], NT)
        inverse.append(inverse_factor(
            both[:RANK, :RANK] + both[:RANK, RANK:] + both[RANK:, :RANK] + both[RANK:, RANK:]))
    for m in range(2):
        high, low = split(inverse[m])
        pair = jnp.concatenate([high, low], axis=0)
        for i in range(width // step):
            at = pl.ds(i * step, step)
            both = dot(pair, sb[m * 64:m * 64 + 32, at])
            left[m, :, at] = both[:RANK] + both[RANK:] + dot(high, sb[m * 64 + 32:m * 64 + 64, at])
    store_left = pltpu.make_async_copy(left, left_hbm, lsem.at[4])
    store_left.start()

    arrived(far_x, 0, 4)
    arrived(far_x, 1, 5)
    project(far_x)

    group = t.shape[2]
    per_row = kv // 128

    def piece(i):
        return i // group, i % group

    for m in range(2):
        for i in range(NZ * group):
            rr, kk = i // per_row, i % per_row
            t[(m,) + piece(i)] = right[m][rr * 8:rr * 8 + 8, kk * 128:kk * 128 + 128]
    for i, (d, k) in enumerate(plane):
        zk, ck = lax.rem(z + k, NZ), (core, other)[d]
        remote(t.at[ck, zk], ta.at[i], tas.at[i], tar.at[i], at_zc(zk, ck)).start()
    accumulate(far_x, False)
    store_mem = pltpu.make_async_copy(mem, mem_hbm, lsem.at[5])
    store_mem.start()
    total = t[core, z]
    for i in range(len(plane)):
        remote(t.at[core, z], ta.at[i], tas.at[i], tar.at[i], partner).wait_recv()
        total = total + ta[i]
    t2[...] = total
    for k in range(1, NY):
        remote(t2, ty.at[k - 1], tys.at[k - 1], tyr.at[k - 1], at_y(k)).start()
    for k in range(1, NY):
        remote(t2, ty.at[k - 1], tys.at[k - 1], tyr.at[k - 1], partner).wait_recv()
        total = total + ty[k - 1]
    tf[core, z] = total
    own_t = tf.at[core, z]
    for i, (d, k) in enumerate(plane):
        remote(own_t, own_t, tgs.at[i], tgr.at[i], at_zc(lax.rem(z + k, NZ), (core, other)[d])).start()
    for i, (d, k) in enumerate(plane):
        got = tf.at[(core, other)[d], lax.rem(z + NZ - k, NZ)]
        remote(got, got, tgs.at[i], tgr.at[i], partner).wait_recv()

    for m in range(2):
        tt = jnp.concatenate(
            [jnp.concatenate([tf[(m,) + piece(rr * per_row + kk)] for kk in range(per_row)], axis=1)
             for rr in range(RANK // 8)], axis=0)
        wh, wl = split(inverse[m])
        th, tl = split(tt)
        both = dot(jnp.concatenate([wh, wl], axis=0), th)
        mean_ref[m] = (both[:RANK] + both[RANK:] + dot(wh, tl)) * (1.0 / ndp)

    for copy in v_copies + [send_r0, send_l1, send_r1, send_l0, forward_r, forward_l]:
        copy.wait_send()

    def sent(j, carry):
        remote(p.at[other, j], rc.at[j], cs.at[j], cr.at[j], partner).wait_send()
        for i in range(2):
            remote(fy.at[i, j], fy.at[i, j], fs.at[i, j], fr.at[i, j], partner).wait_send()
            remote(p.at[core, j, y], ry.at[i, j], ys.at[i, j], yr.at[i, j], partner).wait_send()
        return carry

    lax.fori_loop(0, NZ, sent, 0)
    own = s.at[core, z, y]
    for j in range(NZ - 1):
        remote(q.at[j], rz.at[j], zs.at[j], zr.at[j], partner).wait_send()
        remote(own, own, gzs.at[j], gzr.at[j], partner).wait_send()
    for k in range(NX - 1):
        remote(sp.at[0], rx.at[k], ws.at[k], wr.at[k], partner).wait_send()
    for i in range(2):
        remote(own_y, own_y, gys.at[i], gyr.at[i], partner).wait_send()
    remote(pass_up, pass_up, gys.at[2], gyr.at[2], partner).wait_send()
    remote(pass_down, pass_down, gys.at[3], gyr.at[3], partner).wait_send()
    remote(s.at[core], s.at[core], gcs.at[0], gcr.at[0], partner).wait_send()
    for i in range(len(plane)):
        remote(t2, ta.at[i], tas.at[i], tar.at[i], partner).wait_send()
        remote(own_t, own_t, tgs.at[i], tgr.at[i], partner).wait_send()
    for k in range(NY - 1):
        remote(t2, ty.at[k], tys.at[k], tyr.at[k], partner).wait_send()
    store_left.wait()
    store_mem.wait()


def residual(mem_ref, left_ref, mean_ref, out_ref, left_out, mean_out):
    lt = left_ref[0]
    left_out[0] = lt
    mean = mean_ref[0]
    mean_out[0] = mean
    lh, ll = split(lt)
    mh, ml = split(mean)
    approx = dot(jnp.concatenate([lh, ll, lh], axis=0), jnp.concatenate([mh, mh, ml], axis=0), TN)
    out_ref[0] = (mem_ref[0] - approx).astype(BF)


def shards(NY, NZ, activations, cotangent, error_memory, right_factor):
    tokens, width = activations.shape
    kv = cotangent.shape[2]
    error_memory = error_memory[:, 0]
    group = RANK * kv // (8 * 128 * NZ)
    dma = pltpu.SemaphoreType.DMA
    any_spec = pl.BlockSpec(memory_space=pl.ANY)
    mem, left, mean = pl.pallas_call(
        functools.partial(fused, NY, NZ),
        out_shape=(
            jax.ShapeDtypeStruct((2, width, kv), F32),
            jax.ShapeDtypeStruct((2, RANK, width), F32),
            jax.ShapeDtypeStruct((2, RANK, kv), F32),
        ),
        in_specs=[any_spec] * 4,
        out_specs=(any_spec, any_spec, pl.BlockSpec(memory_space=pltpu.VMEM)),
        scratch_shapes=[
            pltpu.VMEM((NX, tokens, width), BF),
            pltpu.VMEM((2, NX * tokens, kv), BF),
            pltpu.VMEM((2, width, kv), BF),
            pltpu.VMEM((2, RANK, kv), F32),
            pltpu.VMEM((NX, 2 * RANK, tokens), F32),
            pltpu.VMEM((NX, 2 * RANK, tokens), F32),
            pltpu.VMEM((4 * NX * RANK, tokens), BF),
            pltpu.VMEM((2, 2 * RANK, kv), BF),
            pltpu.VMEM((2, NZ, NY, NX, RANK, 128), F32),
            pltpu.VMEM((NZ, NY, NX, RANK, 128), F32),
            pltpu.VMEM((2, NZ, NX // 2, RANK, 128), F32),
            pltpu.VMEM((2, NZ, NX, RANK, 128), F32),
            pltpu.VMEM((NZ, NX, RANK, 128), F32),
            pltpu.VMEM((NZ - 1, NX, RANK, 128), F32),
            pltpu.VMEM((NX, RANK, 128), F32),
            pltpu.VMEM((NX - 1, RANK, 128), F32),
            pltpu.VMEM((2, NZ, NY, RANK, 128), F32),
            pltpu.VMEM((4 * RANK, width), BF),
            pltpu.VMEM((2, RANK, width), F32),
            pltpu.VMEM((2, width, kv), F32),
            pltpu.VMEM((2, NZ, group, 8, 128), F32),
            pltpu.VMEM((2 * NZ - 1, group, 8, 128), F32),
            pltpu.VMEM((group, 8, 128), F32),
            pltpu.VMEM((NY - 1, group, 8, 128), F32),
            pltpu.VMEM((2, NZ, group, 8, 128), F32),
            dma((6,)),
            dma((NX - 1,)), dma((NX - 1,)),
            dma((6,)), dma((6,)),
            dma((NZ,)), dma((NZ,)),
            dma((2, NZ)), dma((2, NZ)),
            dma((2, NZ)), dma((2, NZ)),
            dma((NZ - 1,)), dma((NZ - 1,)),
            dma((NX - 1,)), dma((NX - 1,)),
            dma((NZ - 1,)), dma((NZ - 1,)),
            dma((4,)), dma((4,)),
            dma((1,)), dma((1,)),
            dma((2 * NZ - 1,)), dma((2 * NZ - 1,)),
            dma((NY - 1,)), dma((NY - 1,)),
            dma((2 * NZ - 1,)), dma((2 * NZ - 1,)),
        ],
        compiler_params=pltpu.CompilerParams(
            collective_id=0, has_side_effects=True, vmem_limit_bytes=56 * 1024 * 1024),
    )(activations, cotangent, error_memory, jnp.swapaxes(right_factor, 1, 2))

    rows = min(1024, width)
    new_error, left, mean = pl.pallas_call(
        residual,
        grid=(2, width // rows),
        out_shape=(
            jax.ShapeDtypeStruct((2, width, kv), BF),
            jax.ShapeDtypeStruct((2, RANK, width), F32),
            jax.ShapeDtypeStruct((2, RANK, kv), F32),
        ),
        in_specs=[
            pl.BlockSpec((1, rows, kv), lambda m, i: (m, i, 0)),
            pl.BlockSpec((1, RANK, rows), lambda m, i: (m, 0, i)),
            pl.BlockSpec((1, RANK, kv), lambda m, i: (m, 0, 0)),
        ],
        out_specs=(
            pl.BlockSpec((1, rows, kv), lambda m, i: (m, i, 0)),
            pl.BlockSpec((1, RANK, rows), lambda m, i: (m, 0, i)),
            pl.BlockSpec((1, RANK, kv), lambda m, i: (m, 0, 0)),
        ),
        compiler_params=pltpu.CompilerParams(vmem_limit_bytes=56 * 1024 * 1024),
    )(mem, left, mean)
    return (new_error[:, None], jnp.swapaxes(left, 1, 2)[:, None], jnp.swapaxes(mean, 1, 2))


def build(mesh, NY, NZ):
    return jax.shard_map(
        functools.partial(shards, NY, NZ),
        mesh=mesh,
        in_specs=(
            P(("dp", "tensor"), None),
            P(None, "dp", "tensor"),
            P(None, "dp", None, "tensor"),
            P(None, "tensor", None),
        ),
        out_specs=(
            P(None, "dp", None, "tensor"),
            P(None, "tensor", None, None),
            P(None, "tensor", None),
        ),
        check_vma=False,
    )


def solution(mesh):
    return build(mesh, 4, mesh.shape["dp"] // 8)
```

```python
import functools

import jax
import jax.numpy as jnp
from jax import lax
from jax.experimental import pallas as pl
from jax.experimental.pallas import tpu as pltpu
from jax.sharding import PartitionSpec as P

MESH = pl.DeviceIdType.MESH
BF = jnp.bfloat16
F32 = jnp.float32
NX = 4
RANK = 32
NT = (((1,), (1,)), ((), ()))
TN = (((0,), (0,)), ((), ()))


def split(value):
    high = value.astype(BF)
    return high, (value - high.astype(F32)).astype(BF)


def dot(a, b, dims=None):
    if dims is None:
        dims = (((1,), (0,)), ((), ()))
    return lax.dot_general(a, b, dims, preferred_element_type=F32)


def inverse_factor(gram):
    rows = lax.broadcasted_iota(jnp.int32, (RANK, 2 * RANK), 0)
    cols = lax.broadcasted_iota(jnp.int32, (RANK, 2 * RANK), 1)
    eye = jnp.where(cols == rows + RANK, 1.0, 0.0).astype(F32)
    wide = jnp.concatenate([gram, jnp.zeros((RANK, RANK), F32)], axis=1) + eye
    index = rows[:, :1]
    pivots = jnp.ones((RANK, 1), F32)
    for j in range(RANK):
        row = wide[j:j + 1, :]
        pivot = wide[j:j + 1, j:j + 1]
        column = wide[:, j:j + 1]
        factor = jnp.where(index > j, column * (1.0 / pivot), 0.0)
        pivots = jnp.where(index == j, pivot, pivots)
        wide = wide - factor * row
    return wide[:, RANK:] * (1.0 / jnp.sqrt(pivots))


def fused(NY, NZ, a_hbm, c_hbm, e_hbm, rt_hbm, mem_hbm, left_hbm, mean_ref,
          a, c, e, rt, v, vall, vl, rb, p, rc, fy, ry, q, rz, sp, rx, s, sb, left, mem, t, ta, t2, ty, tf,
          lsem, vs, vr, xs, xr, cs, cr, fs, fr, ys, yr, zs, zr, ws, wr, gzs, gzr, gys, gyr, gcs, gcr,
          tas, tar, tys, tyr, tgs, tgr):
    dp, x = lax.axis_index("dp"), lax.axis_index("tensor")
    core, yz = lax.rem(dp, 2), lax.div(dp, 2)
    z, y = lax.rem(yz, NZ), lax.div(yz, NZ)
    other = 1 - core
    tokens = a.shape[1]
    width = a.shape[2]
    kv = c.shape[2]
    span = NY * 128
    ndp = 2 * NY * NZ

    def at_x(k):
        return {"dp": dp, "tensor": lax.rem(x + k, NX)}

    def at_y(k):
        return {"dp": (lax.rem(y + k, NY) * NZ + z) * 2 + core, "tensor": x}

    def at_zc(zz, cc):
        return {"dp": (y * NZ + zz) * 2 + cc, "tensor": x}

    def at_z(zz):
        return at_zc(zz, core)

    partner = at_zc(z, other)
    plane = [(d, k) for d in range(2) for k in range(NZ) if d + k]

    def remote(src, dst, send, recv, device):
        return pltpu.make_async_remote_copy(src_ref=src, dst_ref=dst, send_sem=send, recv_sem=recv,
                                            device_id=device, device_id_type=MESH)

    load_a = pltpu.make_async_copy(a_hbm, a.at[x], lsem.at[0])
    load_c = pltpu.make_async_copy(c_hbm, c, lsem.at[1])
    load_e = pltpu.make_async_copy(e_hbm, e, lsem.at[2])
    load_r = pltpu.make_async_copy(rt_hbm, rt, lsem.at[3])
    load_r.start()
    load_c.start()
    load_a.start()
    load_e.start()

    barrier = pltpu.get_barrier_semaphore()
    for k in range(1, NX):
        pl.semaphore_signal(barrier, inc=1, device_id=at_x(k), device_id_type=MESH)
    for k in range(1, NY):
        pl.semaphore_signal(barrier, inc=1, device_id=at_y(k), device_id_type=MESH)
    for d, k in plane:
        pl.semaphore_signal(barrier, inc=1, device_id=at_zc(lax.rem(z + k, NZ), (core, other)[d]), device_id_type=MESH)

    load_r.wait()
    load_c.wait()
    for m in range(2):
        high, low = split(rt[m])
        rb[m] = jnp.concatenate([high, low], axis=0)
        both = dot(rb[m], c[m], NT)
        vt = both[:RANK] + both[RANK:]
        for b in range(NX):
            v[b, m * RANK:(m + 1) * RANK, :] = vt[:, b * tokens:(b + 1) * tokens]

    pl.semaphore_wait(barrier, NX + NY + 2 * NZ - 3)

    v_copies = []
    for k in range(1, NX):
        copy = remote(v.at[lax.rem(x + k, NX)], vall.at[x], vs.at[k - 1], vr.at[k - 1], at_x(k))
        copy.start()
        v_copies.append(copy)

    quarter = tokens // 4
    left_x, right_x = lax.rem(x + NX - 1, NX), lax.rem(x + 1, NX)
    far_x = lax.rem(x + 2, NX)
    right_dev, left_dev = at_x(1), at_x(NX - 1)

    def quarter_copy(slot, i, sem, device):
        part = a.at[slot, pl.ds(i * quarter, quarter)]
        return remote(part, part, xs.at[sem], xr.at[sem], device)

    to_right = [quarter_copy(x, i, i, right_dev) for i in range(4)]
    to_left = [quarter_copy(x, i, 4 + i, left_dev) for i in (2, 3, 0, 1)]
    forward_right = [quarter_copy(left_x, i, 8 + i, right_dev) for i in range(2)]
    forward_left = [quarter_copy(right_x, 2 + i, 10 + i, left_dev) for i in range(2)]
    load_a.wait()
    for i in range(2):
        to_right[i].start()
        to_left[i].start()

    def left_arrived(parts):
        for i in parts:
            quarter_copy(left_x, i, i, right_dev).wait_recv()

    def right_arrived(parts):
        for i in parts:
            quarter_copy(right_x, i, 4 + i, right_dev).wait_recv()

    def far_arrived():
        for i in range(2):
            quarter_copy(far_x, i, 8 + i, right_dev).wait_recv()
            quarter_copy(far_x, 2 + i, 10 + i, right_dev).wait_recv()

    vall[x] = v[x]
    for k in range(1, NX):
        src = lax.rem(x + NX - k, NX)
        remote(v.at[0], vall.at[src], vs.at[k - 1], vr.at[k - 1], at_x(k)).wait_recv()
    stacked = jnp.concatenate(
        [vall[b, m * RANK:(m + 1) * RANK, :] for m in range(2) for b in range(NX)], axis=0)
    high, low = split(stacked)
    block = 2 * NX * RANK
    vl[:block] = high
    vl[block:] = low

    load_e.wait()

    def partials(j, carry):
        zj = lax.rem(z + 1 + j, NZ)
        at = pl.ds(pl.multiple_of(zj * span, span), span)
        both = dot(vl[...], a[x, :, at])
        both = both[:block] + both[block:]
        for m in range(2):
            for yb in range(NY):
                for b in range(NX):
                    r0 = (m * NX + b) * RANK
                    p[m, zj, yb, b] = both[r0:r0 + RANK, yb * 128:(yb + 1) * 128]
        for m in range(2):
            et = dot(rb[m], e[m, at, :], NT)
            et = et[:RANK] + et[RANK:]
            for yb in range(NY):
                p[m, zj, yb, x] = p[m, zj, yb, x] + et[:, yb * 128:(yb + 1) * 128]
        remote(p.at[other, zj], rc.at[zj], cs.at[zj], cr.at[zj], partner).start()
        return carry

    lax.fori_loop(0, NZ, partials, 0)

    hc = NX // 2
    up, down, far_y = lax.rem(y + 1, NY), lax.rem(y + NY - 1, NY), lax.rem(y + 2, NY)
    to_up, to_down = at_y(1), at_y(NY - 1)

    def over_cores(j, carry):
        zj = lax.rem(z + 1 + j, NZ)
        remote(p.at[other, zj], rc.at[zj], cs.at[zj], cr.at[zj], partner).wait_recv()
        p[core, zj] = p[core, zj] + rc[zj]
        remote(p.at[core, zj, far_y, pl.ds(0, hc)], fy.at[0, zj], fs.at[0, zj], fr.at[0, zj], to_up).start()
        remote(p.at[core, zj, far_y, pl.ds(hc, hc)], fy.at[1, zj], fs.at[1, zj], fr.at[1, zj], to_down).start()
        return carry

    lax.fori_loop(0, NZ, over_cores, 0)

    to_right[2].start()
    to_left[2].start()

    def to_neighbours(j, carry):
        zj = lax.rem(z + 1 + j, NZ)
        for i, target, device in ((0, up, to_up), (1, down, to_down)):
            part = pl.ds(i * hc, hc)
            remote(p.at[core, zj, far_y, part], fy.at[i, zj], fs.at[i, zj], fr.at[i, zj], device).wait_recv()
            p[core, zj, target, part] = p[core, zj, target, part] + fy[i, zj]
            remote(p.at[core, zj, target], ry.at[i, zj], ys.at[i, zj], yr.at[i, zj], device).start()
        return carry

    lax.fori_loop(0, NZ, to_neighbours, 0)

    step = min(512, width)

    def accumulate(slot, first):
        tok = pl.ds(pl.multiple_of(slot * tokens, tokens), tokens)
        cc = jnp.concatenate([c[0, tok, :], c[1, tok, :]], axis=1)

        def body(i, carry):
            at = pl.ds(pl.multiple_of(i * step, step), step)
            g = dot(a[slot, :, at], cc, TN)
            for m in range(2):
                base = e[m, at, :].astype(F32) if first else mem[m, at, :]
                mem[m, at, :] = base + g[:, m * kv:(m + 1) * kv]
            return carry

        lax.fori_loop(0, width // step, body, 0)

    accumulate(x, True)

    def over_y(zj):
        total = p[core, zj, y]
        for i in range(2):
            remote(p.at[core, zj, y], ry.at[i, zj], ys.at[i, zj], yr.at[i, zj], partner).wait_recv()
            total = total + ry[i, zj]
        q[zj] = total

    def over_y_send(j, carry):
        zj = lax.rem(z + 1 + j, NZ)
        over_y(zj)
        remote(q.at[zj], rz.at[j], zs.at[j], zr.at[j], at_z(zj)).start()
        return carry

    lax.fori_loop(0, NZ - 1, over_y_send, 0)
    over_y(z)

    total = q[z]
    for j in range(NZ - 1):
        remote(q.at[z], rz.at[j], zs.at[j], zr.at[j], partner).wait_recv()
        total = total + rz[j]
    sp[...] = total

    for k in range(1, NX):
        remote(sp.at[lax.rem(x + k, NX)], rx.at[k - 1], ws.at[k - 1], wr.at[k - 1], at_x(k)).start()
    to_right[3].start()
    to_left[3].start()
    for i in range(2):
        left_arrived([i])
        forward_right[i].start()
        right_arrived([2 + i])
        forward_left[i].start()
    total = sp[x]
    for k in range(1, NX):
        remote(sp.at[0], rx.at[k - 1], ws.at[k - 1], wr.at[k - 1], at_x(k)).wait_recv()
        total = total + rx[k - 1]
    s[core, z, y] = total

    own = s.at[core, z, y]
    for k in range(1, NZ):
        remote(own, own, gzs.at[k - 1], gzr.at[k - 1], at_z(lax.rem(z + k, NZ))).start()
    for k in range(1, NZ):
        got = s.at[core, lax.rem(z + NZ - k, NZ), y]
        remote(got, got, gzs.at[k - 1], gzr.at[k - 1], partner).wait_recv()
    own_y = s.at[core, :, y]
    hz = NZ // 2
    remote(own_y, own_y, gys.at[0], gyr.at[0], to_up).start()
    remote(own_y, own_y, gys.at[1], gyr.at[1], to_down).start()
    pass_up, pass_down = s.at[core, pl.ds(0, hz), down], s.at[core, pl.ds(hz, hz), up]
    remote(s.at[core, :, down], s.at[core, :, down], gys.at[0], gyr.at[0], to_up).wait_recv()
    remote(pass_up, pass_up, gys.at[2], gyr.at[2], to_up).start()
    remote(s.at[core, :, up], s.at[core, :, up], gys.at[1], gyr.at[1], to_down).wait_recv()
    remote(pass_down, pass_down, gys.at[3], gyr.at[3], to_down).start()
    for i in range(2):
        got = s.at[core, pl.ds(i * hz, hz), far_y]
        remote(got, got, gys.at[2 + i], gyr.at[2 + i], partner).wait_recv()
    remote(s.at[core], s.at[core], gcs.at[0], gcr.at[0], partner).start()
    remote(s.at[other], s.at[other], gcs.at[0], gcr.at[0], partner).wait_recv()

    for m in range(2):
        for zz in range(NZ):
            for yy in range(NY):
                d0 = (zz * NY + yy) * 128
                high, low = split(s[m, zz, yy])
                sb[m * 64:m * 64 + 32, d0:d0 + 128] = high
                sb[m * 64 + 32:m * 64 + 64, d0:d0 + 128] = low

    right = []
    for m in range(2):
        both = dot(sb[m * 64:m * 64 + 64, :], e[m])
        right.append(both[:RANK] + both[RANK:])

    def project(slot):
        tok = pl.ds(pl.multiple_of(slot * tokens, tokens), tokens)
        u = dot(sb[...], a[slot], NT)
        for m in range(2):
            high, low = split(u[m * 64:m * 64 + 32] + u[m * 64 + 32:m * 64 + 64])
            both = dot(jnp.concatenate([high, low], axis=0), c[m, tok, :])
            right[m] = right[m] + both[:RANK] + both[RANK:]

    project(x)

    inverse = []
    for m in range(2):
        both = dot(sb[m * 64:m * 64 + 64, :], sb[m * 64:m * 64 + 64, :], NT)
        inverse.append(inverse_factor(
            both[:RANK, :RANK] + both[:RANK, RANK:] + both[RANK:, :RANK] + both[RANK:, RANK:]))
    for m in range(2):
        high, low = split(inverse[m])
        pair = jnp.concatenate([high, low], axis=0)
        for i in range(width // step):
            at = pl.ds(i * step, step)
            both = dot(pair, sb[m * 64:m * 64 + 32, at])
            left[m, :, at] = both[:RANK] + both[RANK:] + dot(high, sb[m * 64 + 32:m * 64 + 64, at])
    store_left = pltpu.make_async_copy(left, left_hbm, lsem.at[4])
    store_left.start()

    left_arrived([2, 3])
    project(left_x)
    accumulate(left_x, False)
    right_arrived([0, 1])
    project(right_x)
    accumulate(right_x, False)
    far_arrived()
    project(far_x)

    group = t.shape[2]
    per_row = kv // 128

    def piece(i):
        return i // group, i % group

    for m in range(2):
        for i in range(NZ * group):
            rr, kk = i // per_row, i % per_row
            t[(m,) + piece(i)] = right[m][rr * 8:rr * 8 + 8, kk * 128:kk * 128 + 128]
    for i, (d, k) in enumerate(plane):
        zk, ck = lax.rem(z + k, NZ), (core, other)[d]
        remote(t.at[ck, zk], ta.at[i], tas.at[i], tar.at[i], at_zc(zk, ck)).start()
    accumulate(far_x, False)
    store_mem = pltpu.make_async_copy(mem, mem_hbm, lsem.at[5])
    store_mem.start()
    total = t[core, z]
    for i in range(len(plane)):
        remote(t.at[core, z], ta.at[i], tas.at[i], tar.at[i], partner).wait_recv()
        total = total + ta[i]
    t2[...] = total
    for k in range(1, NY):
        remote(t2, ty.at[k - 1], tys.at[k - 1], tyr.at[k - 1], at_y(k)).start()
    for k in range(1, NY):
        remote(t2, ty.at[k - 1], tys.at[k - 1], tyr.at[k - 1], partner).wait_recv()
        total = total + ty[k - 1]
    tf[core, z] = total
    own_t = tf.at[core, z]
    for i, (d, k) in enumerate(plane):
        remote(own_t, own_t, tgs.at[i], tgr.at[i], at_zc(lax.rem(z + k, NZ), (core, other)[d])).start()
    for i, (d, k) in enumerate(plane):
        got = tf.at[(core, other)[d], lax.rem(z + NZ - k, NZ)]
        remote(got, got, tgs.at[i], tgr.at[i], partner).wait_recv()

    for m in range(2):
        tt = jnp.concatenate(
            [jnp.concatenate([tf[(m,) + piece(rr * per_row + kk)] for kk in range(per_row)], axis=1)
             for rr in range(RANK // 8)], axis=0)
        wh, wl = split(inverse[m])
        th, tl = split(tt)
        both = dot(jnp.concatenate([wh, wl], axis=0), th)
        mean_ref[m] = (both[:RANK] + both[RANK:] + dot(wh, tl)) * (1.0 / ndp)

    for copy in v_copies + to_right + to_left + forward_right + forward_left:
        copy.wait_send()

    def sent(j, carry):
        remote(p.at[other, j], rc.at[j], cs.at[j], cr.at[j], partner).wait_send()
        for i in range(2):
            remote(fy.at[i, j], fy.at[i, j], fs.at[i, j], fr.at[i, j], partner).wait_send()
            remote(p.at[core, j, y], ry.at[i, j], ys.at[i, j], yr.at[i, j], partner).wait_send()
        return carry

    lax.fori_loop(0, NZ, sent, 0)
    own = s.at[core, z, y]
    for j in range(NZ - 1):
        remote(q.at[j], rz.at[j], zs.at[j], zr.at[j], partner).wait_send()
        remote(own, own, gzs.at[j], gzr.at[j], partner).wait_send()
    for k in range(NX - 1):
        remote(sp.at[0], rx.at[k], ws.at[k], wr.at[k], partner).wait_send()
    for i in range(2):
        remote(own_y, own_y, gys.at[i], gyr.at[i], partner).wait_send()
    remote(pass_up, pass_up, gys.at[2], gyr.at[2], partner).wait_send()
    remote(pass_down, pass_down, gys.at[3], gyr.at[3], partner).wait_send()
    remote(s.at[core], s.at[core], gcs.at[0], gcr.at[0], partner).wait_send()
    for i in range(len(plane)):
        remote(t2, ta.at[i], tas.at[i], tar.at[i], partner).wait_send()
        remote(own_t, own_t, tgs.at[i], tgr.at[i], partner).wait_send()
    for k in range(NY - 1):
        remote(t2, ty.at[k], tys.at[k], tyr.at[k], partner).wait_send()
    store_left.wait()
    store_mem.wait()


def residual(mem_ref, left_ref, mean_ref, out_ref, left_out, mean_out):
    lt = left_ref[0]
    left_out[0] = lt
    mean = mean_ref[0]
    mean_out[0] = mean
    lh, ll = split(lt)
    mh, ml = split(mean)
    approx = dot(jnp.concatenate([lh, ll, lh], axis=0), jnp.concatenate([mh, mh, ml], axis=0), TN)
    out_ref[0] = (mem_ref[0] - approx).astype(BF)


def shards(NY, NZ, activations, cotangent, error_memory, right_factor):
    tokens, width = activations.shape
    kv = cotangent.shape[2]
    error_memory = error_memory[:, 0]
    group = RANK * kv // (8 * 128 * NZ)
    dma = pltpu.SemaphoreType.DMA
    any_spec = pl.BlockSpec(memory_space=pl.ANY)
    mem, left, mean = pl.pallas_call(
        functools.partial(fused, NY, NZ),
        out_shape=(
            jax.ShapeDtypeStruct((2, width, kv), F32),
            jax.ShapeDtypeStruct((2, RANK, width), F32),
            jax.ShapeDtypeStruct((2, RANK, kv), F32),
        ),
        in_specs=[any_spec] * 4,
        out_specs=(any_spec, any_spec, pl.BlockSpec(memory_space=pltpu.VMEM)),
        scratch_shapes=[
            pltpu.VMEM((NX, tokens, width), BF),
            pltpu.VMEM((2, NX * tokens, kv), BF),
            pltpu.VMEM((2, width, kv), BF),
            pltpu.VMEM((2, RANK, kv), F32),
            pltpu.VMEM((NX, 2 * RANK, tokens), F32),
            pltpu.VMEM((NX, 2 * RANK, tokens), F32),
            pltpu.VMEM((4 * NX * RANK, tokens), BF),
            pltpu.VMEM((2, 2 * RANK, kv), BF),
            pltpu.VMEM((2, NZ, NY, NX, RANK, 128), F32),
            pltpu.VMEM((NZ, NY, NX, RANK, 128), F32),
            pltpu.VMEM((2, NZ, NX // 2, RANK, 128), F32),
            pltpu.VMEM((2, NZ, NX, RANK, 128), F32),
            pltpu.VMEM((NZ, NX, RANK, 128), F32),
            pltpu.VMEM((NZ - 1, NX, RANK, 128), F32),
            pltpu.VMEM((NX, RANK, 128), F32),
            pltpu.VMEM((NX - 1, RANK, 128), F32),
            pltpu.VMEM((2, NZ, NY, RANK, 128), F32),
            pltpu.VMEM((4 * RANK, width), BF),
            pltpu.VMEM((2, RANK, width), F32),
            pltpu.VMEM((2, width, kv), F32),
            pltpu.VMEM((2, NZ, group, 8, 128), F32),
            pltpu.VMEM((2 * NZ - 1, group, 8, 128), F32),
            pltpu.VMEM((group, 8, 128), F32),
            pltpu.VMEM((NY - 1, group, 8, 128), F32),
            pltpu.VMEM((2, NZ, group, 8, 128), F32),
            dma((6,)),
            dma((NX - 1,)), dma((NX - 1,)),
            dma((12,)), dma((12,)),
            dma((NZ,)), dma((NZ,)),
            dma((2, NZ)), dma((2, NZ)),
            dma((2, NZ)), dma((2, NZ)),
            dma((NZ - 1,)), dma((NZ - 1,)),
            dma((NX - 1,)), dma((NX - 1,)),
            dma((NZ - 1,)), dma((NZ - 1,)),
            dma((4,)), dma((4,)),
            dma((1,)), dma((1,)),
            dma((2 * NZ - 1,)), dma((2 * NZ - 1,)),
            dma((NY - 1,)), dma((NY - 1,)),
            dma((2 * NZ - 1,)), dma((2 * NZ - 1,)),
        ],
        compiler_params=pltpu.CompilerParams(
            collective_id=0, has_side_effects=True, vmem_limit_bytes=56 * 1024 * 1024),
    )(activations, cotangent, error_memory, jnp.swapaxes(right_factor, 1, 2))

    rows = min(512, width)
    new_error, left, mean = pl.pallas_call(
        residual,
        grid=(2, width // rows),
        out_shape=(
            jax.ShapeDtypeStruct((2, width, kv), BF),
            jax.ShapeDtypeStruct((2, RANK, width), F32),
            jax.ShapeDtypeStruct((2, RANK, kv), F32),
        ),
        in_specs=[
            pl.BlockSpec((1, rows, kv), lambda m, i: (m, i, 0)),
            pl.BlockSpec((1, RANK, rows), lambda m, i: (m, 0, i)),
            pl.BlockSpec((1, RANK, kv), lambda m, i: (m, 0, 0)),
        ],
        out_specs=(
            pl.BlockSpec((1, rows, kv), lambda m, i: (m, i, 0)),
            pl.BlockSpec((1, RANK, rows), lambda m, i: (m, 0, i)),
            pl.BlockSpec((1, RANK, kv), lambda m, i: (m, 0, 0)),
        ),
        compiler_params=pltpu.CompilerParams(vmem_limit_bytes=56 * 1024 * 1024),
    )(mem, left, mean)
    return (new_error[:, None], jnp.swapaxes(left, 1, 2)[:, None], jnp.swapaxes(mean, 1, 2))


def build(mesh, NY, NZ):
    return jax.shard_map(
        functools.partial(shards, NY, NZ),
        mesh=mesh,
        in_specs=(
            P(("dp", "tensor"), None),
            P(None, "dp", "tensor"),
            P(None, "dp", None, "tensor"),
            P(None, "tensor", None),
        ),
        out_specs=(
            P(None, "dp", None, "tensor"),
            P(None, "tensor", None, None),
            P(None, "tensor", None),
        ),
        check_vma=False,
    )


def solution(mesh):
    return build(mesh, 4, mesh.shape["dp"] // 8)
```

```python
import functools

import jax
import jax.numpy as jnp
from jax import lax
from jax.experimental import pallas as pl
from jax.experimental.pallas import tpu as pltpu
from jax.sharding import PartitionSpec as P

MESH = pl.DeviceIdType.MESH
BF = jnp.bfloat16
F32 = jnp.float32
NX = 4
RANK = 32
NT = (((1,), (1,)), ((), ()))
TN = (((0,), (0,)), ((), ()))


def split(value):
    high = value.astype(BF)
    return high, (value - high.astype(F32)).astype(BF)


def dot(a, b, dims=None):
    if dims is None:
        dims = (((1,), (0,)), ((), ()))
    return lax.dot_general(a, b, dims, preferred_element_type=F32)


def inverse_factor(gram):
    rows = lax.broadcasted_iota(jnp.int32, (RANK, 2 * RANK), 0)
    cols = lax.broadcasted_iota(jnp.int32, (RANK, 2 * RANK), 1)
    eye = jnp.where(cols == rows + RANK, 1.0, 0.0).astype(F32)
    wide = jnp.concatenate([gram, jnp.zeros((RANK, RANK), F32)], axis=1) + eye
    index = rows[:, :1]
    pivots = jnp.ones((RANK, 1), F32)
    for j in range(RANK):
        row = wide[j:j + 1, :]
        pivot = wide[j:j + 1, j:j + 1]
        column = wide[:, j:j + 1]
        factor = jnp.where(index > j, column * (1.0 / pivot), 0.0)
        pivots = jnp.where(index == j, pivot, pivots)
        wide = wide - factor * row
    return wide[:, RANK:] * (1.0 / jnp.sqrt(pivots))


def fused(NY, NZ, a_hbm, c_hbm, e_hbm, rt_hbm, mem_hbm, left_hbm, mean_ref,
          a, c, e, rt, v, vall, vl, rb, p, rc, fy, ry, q, rz, sp, rx, s, sb, left, mem, t, ta, t2, ty, tf,
          lsem, vs, vr, xs, xr, cs, cr, fs, fr, ys, yr, zs, zr, ws, wr, gzs, gzr, gys, gyr, gcs, gcr,
          tas, tar, tys, tyr, tgs, tgr):
    dp, x = lax.axis_index("dp"), lax.axis_index("tensor")
    core, yz = lax.rem(dp, 2), lax.div(dp, 2)
    z, y = lax.rem(yz, NZ), lax.div(yz, NZ)
    other = 1 - core
    tokens = a.shape[1]
    width = a.shape[2]
    kv = c.shape[2]
    span = NY * 128
    ndp = 2 * NY * NZ

    def at_x(k):
        return {"dp": dp, "tensor": lax.rem(x + k, NX)}

    def at_y(k):
        return {"dp": (lax.rem(y + k, NY) * NZ + z) * 2 + core, "tensor": x}

    def at_zc(zz, cc):
        return {"dp": (y * NZ + zz) * 2 + cc, "tensor": x}

    def at_z(zz):
        return at_zc(zz, core)

    partner = at_zc(z, other)
    plane = [(d, k) for d in range(2) for k in range(NZ) if d + k]

    def remote(src, dst, send, recv, device):
        return pltpu.make_async_remote_copy(src_ref=src, dst_ref=dst, send_sem=send, recv_sem=recv,
                                            device_id=device, device_id_type=MESH)

    load_a = pltpu.make_async_copy(a_hbm, a.at[x], lsem.at[0])
    load_c = pltpu.make_async_copy(c_hbm, c, lsem.at[1])
    load_e = pltpu.make_async_copy(e_hbm, e, lsem.at[2])
    load_r = pltpu.make_async_copy(rt_hbm, rt, lsem.at[3])
    load_r.start()
    load_c.start()
    load_a.start()
    load_e.start()

    barrier = pltpu.get_barrier_semaphore()
    for k in range(1, NX):
        pl.semaphore_signal(barrier, inc=1, device_id=at_x(k), device_id_type=MESH)
    for k in range(1, NY):
        pl.semaphore_signal(barrier, inc=1, device_id=at_y(k), device_id_type=MESH)
    for d, k in plane:
        pl.semaphore_signal(barrier, inc=1, device_id=at_zc(lax.rem(z + k, NZ), (core, other)[d]), device_id_type=MESH)

    load_r.wait()
    load_c.wait()
    for m in range(2):
        high, low = split(rt[m])
        rb[m] = jnp.concatenate([high, low], axis=0)
        both = dot(rb[m], c[m], NT)
        vt = both[:RANK] + both[RANK:]
        for b in range(NX):
            v[b, m * RANK:(m + 1) * RANK, :] = vt[:, b * tokens:(b + 1) * tokens]

    pl.semaphore_wait(barrier, NX + NY + 2 * NZ - 3)

    v_copies = []
    for k in range(1, NX):
        copy = remote(v.at[lax.rem(x + k, NX)], vall.at[x], vs.at[k - 1], vr.at[k - 1], at_x(k))
        copy.start()
        v_copies.append(copy)

    quarter = tokens // 4
    left_x, right_x = lax.rem(x + NX - 1, NX), lax.rem(x + 1, NX)
    far_x = lax.rem(x + 2, NX)
    right_dev, left_dev = at_x(1), at_x(NX - 1)

    def quarter_copy(slot, i, sem, device):
        part = a.at[slot, pl.ds(i * quarter, quarter)]
        return remote(part, part, xs.at[sem], xr.at[sem], device)

    to_right = [quarter_copy(x, i, i, right_dev) for i in range(4)]
    to_left = [quarter_copy(x, i, 4 + i, left_dev) for i in (2, 3, 0, 1)]
    forward_right = [quarter_copy(left_x, i, 8 + i, right_dev) for i in range(2)]
    forward_left = [quarter_copy(right_x, 2 + i, 10 + i, left_dev) for i in range(2)]
    load_a.wait()
    for i in range(2):
        to_right[i].start()
        to_left[i].start()

    def left_arrived(parts):
        for i in parts:
            quarter_copy(left_x, i, i, right_dev).wait_recv()

    def right_arrived(parts):
        for i in parts:
            quarter_copy(right_x, i, 4 + i, right_dev).wait_recv()

    def far_arrived():
        for i in range(2):
            quarter_copy(far_x, i, 8 + i, right_dev).wait_recv()
            quarter_copy(far_x, 2 + i, 10 + i, right_dev).wait_recv()

    vall[x] = v[x]
    for k in range(1, NX):
        src = lax.rem(x + NX - k, NX)
        remote(v.at[0], vall.at[src], vs.at[k - 1], vr.at[k - 1], at_x(k)).wait_recv()
    stacked = jnp.concatenate(
        [vall[b, m * RANK:(m + 1) * RANK, :] for m in range(2) for b in range(NX)], axis=0)
    high, low = split(stacked)
    block = 2 * NX * RANK
    vl[:block] = high
    vl[block:] = low

    load_e.wait()

    def partials(j, carry):
        zj = lax.rem(z + 1 + j, NZ)
        at = pl.ds(pl.multiple_of(zj * span, span), span)
        both = dot(vl[...], a[x, :, at])
        both = both[:block] + both[block:]
        for m in range(2):
            for yb in range(NY):
                for b in range(NX):
                    r0 = (m * NX + b) * RANK
                    p[m, zj, yb, b] = both[r0:r0 + RANK, yb * 128:(yb + 1) * 128]
        for m in range(2):
            et = dot(rb[m], e[m, at, :], NT)
            et = et[:RANK] + et[RANK:]
            for yb in range(NY):
                p[m, zj, yb, x] = p[m, zj, yb, x] + et[:, yb * 128:(yb + 1) * 128]
        remote(p.at[other, zj], rc.at[zj], cs.at[zj], cr.at[zj], partner).start()
        return carry

    lax.fori_loop(0, NZ, partials, 0)

    hc = NX // 2
    up, down, far_y = lax.rem(y + 1, NY), lax.rem(y + NY - 1, NY), lax.rem(y + 2, NY)
    to_up, to_down = at_y(1), at_y(NY - 1)

    def over_cores(j, carry):
        zj = lax.rem(z + 1 + j, NZ)
        remote(p.at[other, zj], rc.at[zj], cs.at[zj], cr.at[zj], partner).wait_recv()
        p[core, zj] = p[core, zj] + rc[zj]
        remote(p.at[core, zj, far_y, pl.ds(0, hc)], fy.at[0, zj], fs.at[0, zj], fr.at[0, zj], to_up).start()
        remote(p.at[core, zj, far_y, pl.ds(hc, hc)], fy.at[1, zj], fs.at[1, zj], fr.at[1, zj], to_down).start()
        return carry

    lax.fori_loop(0, NZ, over_cores, 0)

    to_right[2].start()
    to_left[2].start()

    def to_neighbours(j, carry):
        zj = lax.rem(z + 1 + j, NZ)
        for i, target, device in ((0, up, to_up), (1, down, to_down)):
            part = pl.ds(i * hc, hc)
            remote(p.at[core, zj, far_y, part], fy.at[i, zj], fs.at[i, zj], fr.at[i, zj], device).wait_recv()
            p[core, zj, target, part] = p[core, zj, target, part] + fy[i, zj]
            remote(p.at[core, zj, target], ry.at[i, zj], ys.at[i, zj], yr.at[i, zj], device).start()
        return carry

    lax.fori_loop(0, NZ, to_neighbours, 0)

    step = min(512, width)

    def accumulate(slot, first):
        tok = pl.ds(pl.multiple_of(slot * tokens, tokens), tokens)
        cc = jnp.concatenate([c[0, tok, :], c[1, tok, :]], axis=1)

        def body(i, carry):
            at = pl.ds(pl.multiple_of(i * step, step), step)
            g = dot(a[slot, :, at], cc, TN)
            for m in range(2):
                base = e[m, at, :].astype(F32) if first else mem[m, at, :]
                mem[m, at, :] = base + g[:, m * kv:(m + 1) * kv]
            return carry

        lax.fori_loop(0, width // step, body, 0)

    accumulate(x, True)

    def over_y(zj):
        total = p[core, zj, y]
        for i in range(2):
            remote(p.at[core, zj, y], ry.at[i, zj], ys.at[i, zj], yr.at[i, zj], partner).wait_recv()
            total = total + ry[i, zj]
        q[zj] = total

    def over_y_send(j, carry):
        zj = lax.rem(z + 1 + j, NZ)
        over_y(zj)
        remote(q.at[zj], rz.at[j], zs.at[j], zr.at[j], at_z(zj)).start()
        return carry

    lax.fori_loop(0, NZ - 1, over_y_send, 0)
    over_y(z)

    total = q[z]
    for j in range(NZ - 1):
        remote(q.at[z], rz.at[j], zs.at[j], zr.at[j], partner).wait_recv()
        total = total + rz[j]
    sp[...] = total

    for k in range(1, NX):
        remote(sp.at[lax.rem(x + k, NX)], rx.at[k - 1], ws.at[k - 1], wr.at[k - 1], at_x(k)).start()
    to_right[3].start()
    to_left[3].start()
    for i in range(2):
        left_arrived([i])
        forward_right[i].start()
        right_arrived([2 + i])
        forward_left[i].start()
    total = sp[x]
    for k in range(1, NX):
        remote(sp.at[0], rx.at[k - 1], ws.at[k - 1], wr.at[k - 1], at_x(k)).wait_recv()
        total = total + rx[k - 1]
    s[core, z, y] = total

    own = s.at[core, z, y]
    for k in range(1, NZ):
        remote(own, own, gzs.at[k - 1], gzr.at[k - 1], at_z(lax.rem(z + k, NZ))).start()
    for k in range(1, NZ):
        got = s.at[core, lax.rem(z + NZ - k, NZ), y]
        remote(got, got, gzs.at[k - 1], gzr.at[k - 1], partner).wait_recv()
    own_y = s.at[core, :, y]
    hz = NZ // 2
    remote(own_y, own_y, gys.at[0], gyr.at[0], to_up).start()
    remote(own_y, own_y, gys.at[1], gyr.at[1], to_down).start()
    pass_up, pass_down = s.at[core, pl.ds(0, hz), down], s.at[core, pl.ds(hz, hz), up]
    remote(s.at[core, :, down], s.at[core, :, down], gys.at[0], gyr.at[0], to_up).wait_recv()
    remote(pass_up, pass_up, gys.at[2], gyr.at[2], to_up).start()
    remote(s.at[core, :, up], s.at[core, :, up], gys.at[1], gyr.at[1], to_down).wait_recv()
    remote(pass_down, pass_down, gys.at[3], gyr.at[3], to_down).start()
    for i in range(2):
        got = s.at[core, pl.ds(i * hz, hz), far_y]
        remote(got, got, gys.at[2 + i], gyr.at[2 + i], partner).wait_recv()
    remote(s.at[core], s.at[core], gcs.at[0], gcr.at[0], partner).start()
    remote(s.at[other], s.at[other], gcs.at[0], gcr.at[0], partner).wait_recv()

    for m in range(2):
        for zz in range(NZ):
            for yy in range(NY):
                d0 = (zz * NY + yy) * 128
                high, low = split(s[m, zz, yy])
                sb[m * 64:m * 64 + 32, d0:d0 + 128] = high
                sb[m * 64 + 32:m * 64 + 64, d0:d0 + 128] = low

    right = []
    for m in range(2):
        both = dot(sb[m * 64:m * 64 + 64, :], e[m])
        right.append(both[:RANK] + both[RANK:])

    def project(slot):
        tok = pl.ds(pl.multiple_of(slot * tokens, tokens), tokens)
        u = dot(sb[...], a[slot], NT)
        for m in range(2):
            high, low = split(u[m * 64:m * 64 + 32] + u[m * 64 + 32:m * 64 + 64])
            both = dot(jnp.concatenate([high, low], axis=0), c[m, tok, :])
            right[m] = right[m] + both[:RANK] + both[RANK:]

    project(x)

    inverse = []
    for m in range(2):
        both = dot(sb[m * 64:m * 64 + 64, :], sb[m * 64:m * 64 + 64, :], NT)
        inverse.append(inverse_factor(
            both[:RANK, :RANK] + both[:RANK, RANK:] + both[RANK:, :RANK] + both[RANK:, RANK:]))
    for m in range(2):
        high, low = split(inverse[m])
        pair = jnp.concatenate([high, low], axis=0)
        for i in range(width // step):
            at = pl.ds(i * step, step)
            both = dot(pair, sb[m * 64:m * 64 + 32, at])
            left[m, :, at] = both[:RANK] + both[RANK:] + dot(high, sb[m * 64 + 32:m * 64 + 64, at])
    store_left = pltpu.make_async_copy(left, left_hbm, lsem.at[4])
    store_left.start()

    left_arrived([2, 3])
    project(left_x)
    accumulate(left_x, False)
    right_arrived([0, 1])
    project(right_x)
    accumulate(right_x, False)
    far_arrived()
    project(far_x)

    group = t.shape[2]
    per_row = kv // 128

    def piece(i):
        return i // group, i % group

    for m in range(2):
        for i in range(NZ * group):
            rr, kk = i // per_row, i % per_row
            t[(m,) + piece(i)] = right[m][rr * 8:rr * 8 + 8, kk * 128:kk * 128 + 128]
    for i, (d, k) in enumerate(plane):
        zk, ck = lax.rem(z + k, NZ), (core, other)[d]
        remote(t.at[ck, zk], ta.at[i], tas.at[i], tar.at[i], at_zc(zk, ck)).start()
    accumulate(far_x, False)
    store_mem = pltpu.make_async_copy(mem, mem_hbm, lsem.at[5])
    store_mem.start()
    total = t[core, z]
    for i in range(len(plane)):
        remote(t.at[core, z], ta.at[i], tas.at[i], tar.at[i], partner).wait_recv()
        total = total + ta[i]
    t2[...] = total
    for k in range(1, NY):
        remote(t2, ty.at[k - 1], tys.at[k - 1], tyr.at[k - 1], at_y(k)).start()
    for k in range(1, NY):
        remote(t2, ty.at[k - 1], tys.at[k - 1], tyr.at[k - 1], partner).wait_recv()
        total = total + ty[k - 1]
    tf[core, z] = total
    own_t = tf.at[core, z]
    for i, (d, k) in enumerate(plane):
        remote(own_t, own_t, tgs.at[i], tgr.at[i], at_zc(lax.rem(z + k, NZ), (core, other)[d])).start()
    for i, (d, k) in enumerate(plane):
        got = tf.at[(core, other)[d], lax.rem(z + NZ - k, NZ)]
        remote(got, got, tgs.at[i], tgr.at[i], partner).wait_recv()

    for m in range(2):
        tt = jnp.concatenate(
            [jnp.concatenate([tf[(m,) + piece(rr * per_row + kk)] for kk in range(per_row)], axis=1)
             for rr in range(RANK // 8)], axis=0)
        wh, wl = split(inverse[m])
        th, tl = split(tt)
        both = dot(jnp.concatenate([wh, wl], axis=0), th)
        mean_ref[m] = (both[:RANK] + both[RANK:] + dot(wh, tl)) * (1.0 / ndp)

    for copy in v_copies + to_right + to_left + forward_right + forward_left:
        copy.wait_send()

    def sent(j, carry):
        remote(p.at[other, j], rc.at[j], cs.at[j], cr.at[j], partner).wait_send()
        for i in range(2):
            remote(fy.at[i, j], fy.at[i, j], fs.at[i, j], fr.at[i, j], partner).wait_send()
            remote(p.at[core, j, y], ry.at[i, j], ys.at[i, j], yr.at[i, j], partner).wait_send()
        return carry

    lax.fori_loop(0, NZ, sent, 0)
    own = s.at[core, z, y]
    for j in range(NZ - 1):
        remote(q.at[j], rz.at[j], zs.at[j], zr.at[j], partner).wait_send()
        remote(own, own, gzs.at[j], gzr.at[j], partner).wait_send()
    for k in range(NX - 1):
        remote(sp.at[0], rx.at[k], ws.at[k], wr.at[k], partner).wait_send()
    for i in range(2):
        remote(own_y, own_y, gys.at[i], gyr.at[i], partner).wait_send()
    remote(pass_up, pass_up, gys.at[2], gyr.at[2], partner).wait_send()
    remote(pass_down, pass_down, gys.at[3], gyr.at[3], partner).wait_send()
    remote(s.at[core], s.at[core], gcs.at[0], gcr.at[0], partner).wait_send()
    for i in range(len(plane)):
        remote(t2, ta.at[i], tas.at[i], tar.at[i], partner).wait_send()
        remote(own_t, own_t, tgs.at[i], tgr.at[i], partner).wait_send()
    for k in range(NY - 1):
        remote(t2, ty.at[k], tys.at[k], tyr.at[k], partner).wait_send()
    store_left.wait()
    store_mem.wait()


def residual(parts, mem_hbm, left_hbm, mean_ref, out_hbm, left_out, mean_out,
             mem, left, out, load_sem, store_sem, left_sem):
    rows = mem.shape[1] // parts
    blocks = [(m, pl.ds(i * rows, rows), m * parts + i) for m in range(2) for i in range(parts)]
    load_left = pltpu.make_async_copy(left_hbm, left, left_sem.at[0])
    load_left.start()
    loads = [pltpu.make_async_copy(mem_hbm.at[m, at], mem.at[m, at], load_sem.at[i]) for m, at, i in blocks]
    stores = [pltpu.make_async_copy(out.at[m, at], out_hbm.at[m, at], store_sem.at[i]) for m, at, i in blocks]
    for load in loads:
        load.start()
    store_left = pltpu.make_async_copy(left, left_out, left_sem.at[1])
    load_left.wait()
    store_left.start()
    mean_out[...] = mean_ref[...]
    for m, at, i in blocks:
        lh, ll = split(left[m, :, at])
        mh, ml = split(mean_ref[m])
        approx = dot(jnp.concatenate([lh, ll, lh], axis=0), jnp.concatenate([mh, mh, ml], axis=0), TN)
        loads[i].wait()
        out[m, at, :] = (mem[m, at, :] - approx).astype(BF)
        stores[i].start()
    for store in stores:
        store.wait()
    store_left.wait()


def shards(NY, NZ, activations, cotangent, error_memory, right_factor):
    tokens, width = activations.shape
    kv = cotangent.shape[2]
    error_memory = error_memory[:, 0]
    group = RANK * kv // (8 * 128 * NZ)
    dma = pltpu.SemaphoreType.DMA
    any_spec = pl.BlockSpec(memory_space=pl.ANY)
    mem, left, mean = pl.pallas_call(
        functools.partial(fused, NY, NZ),
        out_shape=(
            jax.ShapeDtypeStruct((2, width, kv), F32),
            jax.ShapeDtypeStruct((2, RANK, width), F32),
            jax.ShapeDtypeStruct((2, RANK, kv), F32),
        ),
        in_specs=[any_spec] * 4,
        out_specs=(any_spec, any_spec, pl.BlockSpec(memory_space=pltpu.VMEM)),
        scratch_shapes=[
            pltpu.VMEM((NX, tokens, width), BF),
            pltpu.VMEM((2, NX * tokens, kv), BF),
            pltpu.VMEM((2, width, kv), BF),
            pltpu.VMEM((2, RANK, kv), F32),
            pltpu.VMEM((NX, 2 * RANK, tokens), F32),
            pltpu.VMEM((NX, 2 * RANK, tokens), F32),
            pltpu.VMEM((4 * NX * RANK, tokens), BF),
            pltpu.VMEM((2, 2 * RANK, kv), BF),
            pltpu.VMEM((2, NZ, NY, NX, RANK, 128), F32),
            pltpu.VMEM((NZ, NY, NX, RANK, 128), F32),
            pltpu.VMEM((2, NZ, NX // 2, RANK, 128), F32),
            pltpu.VMEM((2, NZ, NX, RANK, 128), F32),
            pltpu.VMEM((NZ, NX, RANK, 128), F32),
            pltpu.VMEM((NZ - 1, NX, RANK, 128), F32),
            pltpu.VMEM((NX, RANK, 128), F32),
            pltpu.VMEM((NX - 1, RANK, 128), F32),
            pltpu.VMEM((2, NZ, NY, RANK, 128), F32),
            pltpu.VMEM((4 * RANK, width), BF),
            pltpu.VMEM((2, RANK, width), F32),
            pltpu.VMEM((2, width, kv), F32),
            pltpu.VMEM((2, NZ, group, 8, 128), F32),
            pltpu.VMEM((2 * NZ - 1, group, 8, 128), F32),
            pltpu.VMEM((group, 8, 128), F32),
            pltpu.VMEM((NY - 1, group, 8, 128), F32),
            pltpu.VMEM((2, NZ, group, 8, 128), F32),
            dma((6,)),
            dma((NX - 1,)), dma((NX - 1,)),
            dma((12,)), dma((12,)),
            dma((NZ,)), dma((NZ,)),
            dma((2, NZ)), dma((2, NZ)),
            dma((2, NZ)), dma((2, NZ)),
            dma((NZ - 1,)), dma((NZ - 1,)),
            dma((NX - 1,)), dma((NX - 1,)),
            dma((NZ - 1,)), dma((NZ - 1,)),
            dma((4,)), dma((4,)),
            dma((1,)), dma((1,)),
            dma((2 * NZ - 1,)), dma((2 * NZ - 1,)),
            dma((NY - 1,)), dma((NY - 1,)),
            dma((2 * NZ - 1,)), dma((2 * NZ - 1,)),
        ],
        compiler_params=pltpu.CompilerParams(
            collective_id=0, has_side_effects=True, vmem_limit_bytes=56 * 1024 * 1024),
    )(activations, cotangent, error_memory, jnp.swapaxes(right_factor, 1, 2))

    parts = 4
    vmem_spec = pl.BlockSpec(memory_space=pltpu.VMEM)
    new_error, left, mean = pl.pallas_call(
        functools.partial(residual, parts),
        out_shape=(
            jax.ShapeDtypeStruct((2, width, kv), BF),
            jax.ShapeDtypeStruct((2, RANK, width), F32),
            jax.ShapeDtypeStruct((2, RANK, kv), F32),
        ),
        in_specs=[any_spec, any_spec, vmem_spec],
        out_specs=(any_spec, any_spec, vmem_spec),
        scratch_shapes=[
            pltpu.VMEM((2, width, kv), F32),
            pltpu.VMEM((2, RANK, width), F32),
            pltpu.VMEM((2, width, kv), BF),
            dma((2 * parts,)),
            dma((2 * parts,)),
            dma((2,)),
        ],
        compiler_params=pltpu.CompilerParams(vmem_limit_bytes=56 * 1024 * 1024),
    )(mem, left, mean)
    return (new_error[:, None], jnp.swapaxes(left, 1, 2)[:, None], jnp.swapaxes(mean, 1, 2))


def build(mesh, NY, NZ):
    return jax.shard_map(
        functools.partial(shards, NY, NZ),
        mesh=mesh,
        in_specs=(
            P(("dp", "tensor"), None),
            P(None, "dp", "tensor"),
            P(None, "dp", None, "tensor"),
            P(None, "tensor", None),
        ),
        out_specs=(
            P(None, "dp", None, "tensor"),
            P(None, "tensor", None, None),
            P(None, "tensor", None),
        ),
        check_vma=False,
    )


def solution(mesh):
    return build(mesh, 4, mesh.shape["dp"] // 8)
```

```python
import functools

import jax
import jax.numpy as jnp
from jax import lax
from jax.experimental import pallas as pl
from jax.experimental.pallas import tpu as pltpu
from jax.sharding import PartitionSpec as P

MESH = pl.DeviceIdType.MESH
BF = jnp.bfloat16
F32 = jnp.float32
NX = 4
RANK = 32
NT = (((1,), (1,)), ((), ()))
TN = (((0,), (0,)), ((), ()))


def split(value):
    high = value.astype(BF)
    return high, (value - high.astype(F32)).astype(BF)


def dot(a, b, dims=None):
    if dims is None:
        dims = (((1,), (0,)), ((), ()))
    return lax.dot_general(a, b, dims, preferred_element_type=F32)


def inverse_factor(gram):
    rows = lax.broadcasted_iota(jnp.int32, (RANK, 2 * RANK), 0)
    cols = lax.broadcasted_iota(jnp.int32, (RANK, 2 * RANK), 1)
    eye = jnp.where(cols == rows + RANK, 1.0, 0.0).astype(F32)
    wide = jnp.concatenate([gram, jnp.zeros((RANK, RANK), F32)], axis=1) + eye
    index = rows[:, :1]
    pivots = jnp.ones((RANK, 1), F32)
    for j in range(RANK):
        row = wide[j:j + 1, :]
        pivot = wide[j:j + 1, j:j + 1]
        column = wide[:, j:j + 1]
        factor = jnp.where(index > j, column * (1.0 / pivot), 0.0)
        pivots = jnp.where(index == j, pivot, pivots)
        wide = wide - factor * row
    return wide[:, RANK:] * (1.0 / jnp.sqrt(pivots))


def fused(NY, NZ, a_hbm, c_hbm, e_hbm, rt_hbm, mem_hbm, left_hbm, mean_ref,
          a, c, e, rt, v, vall, vl, rb, pe, p, rc, fy, ry, q, rz, sp, rx, s, sb, left, mem, t, ta, t2, ty, tf,
          lsem, vs, vr, xs, xr, cs, cr, fs, fr, ys, yr, zs, zr, ws, wr, gzs, gzr, gys, gyr, gcs, gcr,
          tas, tar, tys, tyr, tgs, tgr):
    dp, x = lax.axis_index("dp"), lax.axis_index("tensor")
    core, yz = lax.rem(dp, 2), lax.div(dp, 2)
    z, y = lax.rem(yz, NZ), lax.div(yz, NZ)
    other = 1 - core
    tokens = a.shape[1]
    width = a.shape[2]
    kv = c.shape[2]
    span = NY * 128
    ndp = 2 * NY * NZ

    def at_x(k):
        return {"dp": dp, "tensor": lax.rem(x + k, NX)}

    def at_y(k):
        return {"dp": (lax.rem(y + k, NY) * NZ + z) * 2 + core, "tensor": x}

    def at_zc(zz, cc):
        return {"dp": (y * NZ + zz) * 2 + cc, "tensor": x}

    def at_z(zz):
        return at_zc(zz, core)

    partner = at_zc(z, other)
    plane = [(d, k) for d in range(2) for k in range(NZ) if d + k]

    def remote(src, dst, send, recv, device):
        return pltpu.make_async_remote_copy(src_ref=src, dst_ref=dst, send_sem=send, recv_sem=recv,
                                            device_id=device, device_id_type=MESH)

    load_a = pltpu.make_async_copy(a_hbm, a.at[x], lsem.at[0])
    load_c = pltpu.make_async_copy(c_hbm, c, lsem.at[1])
    load_e = pltpu.make_async_copy(e_hbm, e, lsem.at[2])
    load_r = pltpu.make_async_copy(rt_hbm, rt, lsem.at[3])
    load_r.start()
    load_c.start()
    load_a.start()
    load_e.start()

    barrier = pltpu.get_barrier_semaphore()
    for k in range(1, NX):
        pl.semaphore_signal(barrier, inc=1, device_id=at_x(k), device_id_type=MESH)
    for k in range(1, NY):
        pl.semaphore_signal(barrier, inc=1, device_id=at_y(k), device_id_type=MESH)
    for d, k in plane:
        pl.semaphore_signal(barrier, inc=1, device_id=at_zc(lax.rem(z + k, NZ), (core, other)[d]), device_id_type=MESH)

    load_r.wait()
    load_c.wait()
    for m in range(2):
        high, low = split(rt[m])
        rb[m] = jnp.concatenate([high, low], axis=0)
        both = dot(rb[m], c[m], NT)
        vt = both[:RANK] + both[RANK:]
        for b in range(NX):
            v[b, m * RANK:(m + 1) * RANK, :] = vt[:, b * tokens:(b + 1) * tokens]

    pl.semaphore_wait(barrier, NX + NY + 2 * NZ - 3)

    v_copies = []
    for k in range(1, NX):
        copy = remote(v.at[lax.rem(x + k, NX)], vall.at[x], vs.at[k - 1], vr.at[k - 1], at_x(k))
        copy.start()
        v_copies.append(copy)

    quarter = tokens // 4
    left_x, right_x = lax.rem(x + NX - 1, NX), lax.rem(x + 1, NX)
    far_x = lax.rem(x + 2, NX)
    right_dev, left_dev = at_x(1), at_x(NX - 1)

    def quarter_copy(slot, i, sem, device):
        part = a.at[slot, pl.ds(i * quarter, quarter)]
        return remote(part, part, xs.at[sem], xr.at[sem], device)

    to_right = [quarter_copy(x, i, i, right_dev) for i in range(4)]
    to_left = [quarter_copy(x, i, 4 + i, left_dev) for i in (2, 3, 0, 1)]
    forward_right = [quarter_copy(left_x, i, 8 + i, right_dev) for i in range(2)]
    forward_left = [quarter_copy(right_x, 2 + i, 10 + i, left_dev) for i in range(2)]
    load_a.wait()
    for i in range(2):
        to_right[i].start()
        to_left[i].start()

    def left_arrived(parts):
        for i in parts:
            quarter_copy(left_x, i, i, right_dev).wait_recv()

    def right_arrived(parts):
        for i in parts:
            quarter_copy(right_x, i, 4 + i, right_dev).wait_recv()

    def far_arrived():
        for i in range(2):
            quarter_copy(far_x, i, 8 + i, right_dev).wait_recv()
            quarter_copy(far_x, 2 + i, 10 + i, right_dev).wait_recv()

    load_e.wait()

    def error_part(j, carry):
        at = pl.ds(pl.multiple_of(j * span, span), span)
        for m in range(2):
            et = dot(rb[m], e[m, at, :], NT)
            et = et[:RANK] + et[RANK:]
            for yb in range(NY):
                pe[m, j, yb] = et[:, yb * 128:(yb + 1) * 128]
        return carry

    lax.fori_loop(0, NZ, error_part, 0)

    vall[x] = v[x]
    for k in range(1, NX):
        src = lax.rem(x + NX - k, NX)
        remote(v.at[0], vall.at[src], vs.at[k - 1], vr.at[k - 1], at_x(k)).wait_recv()
    stacked = jnp.concatenate(
        [vall[b, m * RANK:(m + 1) * RANK, :] for m in range(2) for b in range(NX)], axis=0)
    high, low = split(stacked)
    block = 2 * NX * RANK
    vl[:block] = high
    vl[block:] = low

    def partials(j):
        zj = lax.rem(z + 1 + j, NZ)
        at = pl.ds(pl.multiple_of(zj * span, span), span)
        both = dot(vl[...], a[x, :, at])
        both = both[:block] + both[block:]
        for m in range(2):
            for yb in range(NY):
                for b in range(NX):
                    r0 = (m * NX + b) * RANK
                    p[m, zj, yb, b] = both[r0:r0 + RANK, yb * 128:(yb + 1) * 128]
        for m in range(2):
            for yb in range(NY):
                p[m, zj, yb, x] = p[m, zj, yb, x] + pe[m, zj, yb]
        remote(p.at[other, zj], rc.at[zj], cs.at[zj], cr.at[zj], partner).start()

    hc = NX // 2
    up, down, far_y = lax.rem(y + 1, NY), lax.rem(y + NY - 1, NY), lax.rem(y + 2, NY)
    to_up, to_down = at_y(1), at_y(NY - 1)

    def over_cores(j):
        zj = lax.rem(z + 1 + j, NZ)
        remote(p.at[other, zj], rc.at[zj], cs.at[zj], cr.at[zj], partner).wait_recv()
        p[core, zj] = p[core, zj] + rc[zj]
        remote(p.at[core, zj, far_y, pl.ds(0, hc)], fy.at[0, zj], fs.at[0, zj], fr.at[0, zj], to_up).start()
        remote(p.at[core, zj, far_y, pl.ds(hc, hc)], fy.at[1, zj], fs.at[1, zj], fr.at[1, zj], to_down).start()

    def staggered(j, carry):
        partials(j)
        over_cores(j - 1)
        return carry

    partials(0)
    lax.fori_loop(1, NZ, staggered, 0)
    over_cores(NZ - 1)

    to_right[2].start()
    to_left[2].start()

    def to_neighbours(j, carry):
        zj = lax.rem(z + 1 + j, NZ)
        for i, target, device in ((0, up, to_up), (1, down, to_down)):
            part = pl.ds(i * hc, hc)
            remote(p.at[core, zj, far_y, part], fy.at[i, zj], fs.at[i, zj], fr.at[i, zj], device).wait_recv()
            p[core, zj, target, part] = p[core, zj, target, part] + fy[i, zj]
            remote(p.at[core, zj, target], ry.at[i, zj], ys.at[i, zj], yr.at[i, zj], device).start()
        return carry

    lax.fori_loop(0, NZ, to_neighbours, 0)

    step = min(512, width)

    def accumulate(slot, first):
        tok = pl.ds(pl.multiple_of(slot * tokens, tokens), tokens)
        cc = jnp.concatenate([c[0, tok, :], c[1, tok, :]], axis=1)

        def body(i, carry):
            at = pl.ds(pl.multiple_of(i * step, step), step)
            g = dot(a[slot, :, at], cc, TN)
            for m in range(2):
                base = e[m, at, :].astype(F32) if first else mem[m, at, :]
                mem[m, at, :] = base + g[:, m * kv:(m + 1) * kv]
            return carry

        lax.fori_loop(0, width // step, body, 0)

    accumulate(x, True)

    def over_y(zj):
        total = p[core, zj, y]
        for i in range(2):
            remote(p.at[core, zj, y], ry.at[i, zj], ys.at[i, zj], yr.at[i, zj], partner).wait_recv()
            total = total + ry[i, zj]
        q[zj] = total

    def over_y_send(j, carry):
        zj = lax.rem(z + 1 + j, NZ)
        over_y(zj)
        remote(q.at[zj], rz.at[j], zs.at[j], zr.at[j], at_z(zj)).start()
        return carry

    lax.fori_loop(0, NZ - 1, over_y_send, 0)
    over_y(z)

    total = q[z]
    for j in range(NZ - 1):
        remote(q.at[z], rz.at[j], zs.at[j], zr.at[j], partner).wait_recv()
        total = total + rz[j]
    sp[...] = total

    for k in range(1, NX):
        remote(sp.at[lax.rem(x + k, NX)], rx.at[k - 1], ws.at[k - 1], wr.at[k - 1], at_x(k)).start()
    to_right[3].start()
    to_left[3].start()
    for i in range(2):
        left_arrived([i])
        forward_right[i].start()
        right_arrived([2 + i])
        forward_left[i].start()
    total = sp[x]
    for k in range(1, NX):
        remote(sp.at[0], rx.at[k - 1], ws.at[k - 1], wr.at[k - 1], at_x(k)).wait_recv()
        total = total + rx[k - 1]
    s[core, z, y] = total

    own = s.at[core, z, y]
    for k in range(1, NZ):
        remote(own, own, gzs.at[k - 1], gzr.at[k - 1], at_z(lax.rem(z + k, NZ))).start()
    for k in range(1, NZ):
        got = s.at[core, lax.rem(z + NZ - k, NZ), y]
        remote(got, got, gzs.at[k - 1], gzr.at[k - 1], partner).wait_recv()
    own_y = s.at[core, :, y]
    hz = NZ // 2
    remote(own_y, own_y, gys.at[0], gyr.at[0], to_up).start()
    remote(own_y, own_y, gys.at[1], gyr.at[1], to_down).start()
    pass_up, pass_down = s.at[core, pl.ds(0, hz), down], s.at[core, pl.ds(hz, hz), up]
    remote(s.at[core, :, down], s.at[core, :, down], gys.at[0], gyr.at[0], to_up).wait_recv()
    remote(pass_up, pass_up, gys.at[2], gyr.at[2], to_up).start()
    remote(s.at[core, :, up], s.at[core, :, up], gys.at[1], gyr.at[1], to_down).wait_recv()
    remote(pass_down, pass_down, gys.at[3], gyr.at[3], to_down).start()
    for i in range(2):
        got = s.at[core, pl.ds(i * hz, hz), far_y]
        remote(got, got, gys.at[2 + i], gyr.at[2 + i], partner).wait_recv()
    remote(s.at[core], s.at[core], gcs.at[0], gcr.at[0], partner).start()
    remote(s.at[other], s.at[other], gcs.at[0], gcr.at[0], partner).wait_recv()

    for m in range(2):
        for zz in range(NZ):
            for yy in range(NY):
                d0 = (zz * NY + yy) * 128
                high, low = split(s[m, zz, yy])
                sb[m * 64:m * 64 + 32, d0:d0 + 128] = high
                sb[m * 64 + 32:m * 64 + 64, d0:d0 + 128] = low

    right = []
    for m in range(2):
        both = dot(sb[m * 64:m * 64 + 64, :], e[m])
        right.append(both[:RANK] + both[RANK:])

    def project(slot):
        tok = pl.ds(pl.multiple_of(slot * tokens, tokens), tokens)
        u = dot(sb[...], a[slot], NT)
        for m in range(2):
            high, low = split(u[m * 64:m * 64 + 32] + u[m * 64 + 32:m * 64 + 64])
            both = dot(jnp.concatenate([high, low], axis=0), c[m, tok, :])
            right[m] = right[m] + both[:RANK] + both[RANK:]

    project(x)

    inverse = []
    for m in range(2):
        both = dot(sb[m * 64:m * 64 + 64, :], sb[m * 64:m * 64 + 64, :], NT)
        inverse.append(inverse_factor(
            both[:RANK, :RANK] + both[:RANK, RANK:] + both[RANK:, :RANK] + both[RANK:, RANK:]))
    for m in range(2):
        high, low = split(inverse[m])
        pair = jnp.concatenate([high, low], axis=0)
        for i in range(width // step):
            at = pl.ds(i * step, step)
            both = dot(pair, sb[m * 64:m * 64 + 32, at])
            left[m, :, at] = both[:RANK] + both[RANK:] + dot(high, sb[m * 64 + 32:m * 64 + 64, at])
    store_left = pltpu.make_async_copy(left, left_hbm, lsem.at[4])
    store_left.start()

    left_arrived([2, 3])
    project(left_x)
    accumulate(left_x, False)
    right_arrived([0, 1])
    project(right_x)
    accumulate(right_x, False)
    far_arrived()
    project(far_x)

    group = t.shape[2]
    per_row = kv // 128

    def piece(i):
        return i // group, i % group

    for m in range(2):
        for i in range(NZ * group):
            rr, kk = i // per_row, i % per_row
            t[(m,) + piece(i)] = right[m][rr * 8:rr * 8 + 8, kk * 128:kk * 128 + 128]
    for i, (d, k) in enumerate(plane):
        zk, ck = lax.rem(z + k, NZ), (core, other)[d]
        remote(t.at[ck, zk], ta.at[i], tas.at[i], tar.at[i], at_zc(zk, ck)).start()
    accumulate(far_x, False)
    store_mem = pltpu.make_async_copy(mem, mem_hbm, lsem.at[5])
    store_mem.start()
    total = t[core, z]
    for i in range(len(plane)):
        remote(t.at[core, z], ta.at[i], tas.at[i], tar.at[i], partner).wait_recv()
        total = total + ta[i]
    t2[...] = total
    for k in range(1, NY):
        remote(t2, ty.at[k - 1], tys.at[k - 1], tyr.at[k - 1], at_y(k)).start()
    for k in range(1, NY):
        remote(t2, ty.at[k - 1], tys.at[k - 1], tyr.at[k - 1], partner).wait_recv()
        total = total + ty[k - 1]
    tf[core, z] = total
    own_t = tf.at[core, z]
    for i, (d, k) in enumerate(plane):
        remote(own_t, own_t, tgs.at[i], tgr.at[i], at_zc(lax.rem(z + k, NZ), (core, other)[d])).start()
    for i, (d, k) in enumerate(plane):
        got = tf.at[(core, other)[d], lax.rem(z + NZ - k, NZ)]
        remote(got, got, tgs.at[i], tgr.at[i], partner).wait_recv()

    for m in range(2):
        tt = jnp.concatenate(
            [jnp.concatenate([tf[(m,) + piece(rr * per_row + kk)] for kk in range(per_row)], axis=1)
             for rr in range(RANK // 8)], axis=0)
        wh, wl = split(inverse[m])
        th, tl = split(tt)
        both = dot(jnp.concatenate([wh, wl], axis=0), th)
        mean_ref[m] = (both[:RANK] + both[RANK:] + dot(wh, tl)) * (1.0 / ndp)

    for copy in v_copies + to_right + to_left + forward_right + forward_left:
        copy.wait_send()

    def sent(j, carry):
        remote(p.at[other, j], rc.at[j], cs.at[j], cr.at[j], partner).wait_send()
        for i in range(2):
            remote(fy.at[i, j], fy.at[i, j], fs.at[i, j], fr.at[i, j], partner).wait_send()
            remote(p.at[core, j, y], ry.at[i, j], ys.at[i, j], yr.at[i, j], partner).wait_send()
        return carry

    lax.fori_loop(0, NZ, sent, 0)
    own = s.at[core, z, y]
    for j in range(NZ - 1):
        remote(q.at[j], rz.at[j], zs.at[j], zr.at[j], partner).wait_send()
        remote(own, own, gzs.at[j], gzr.at[j], partner).wait_send()
    for k in range(NX - 1):
        remote(sp.at[0], rx.at[k], ws.at[k], wr.at[k], partner).wait_send()
    for i in range(2):
        remote(own_y, own_y, gys.at[i], gyr.at[i], partner).wait_send()
    remote(pass_up, pass_up, gys.at[2], gyr.at[2], partner).wait_send()
    remote(pass_down, pass_down, gys.at[3], gyr.at[3], partner).wait_send()
    remote(s.at[core], s.at[core], gcs.at[0], gcr.at[0], partner).wait_send()
    for i in range(len(plane)):
        remote(t2, ta.at[i], tas.at[i], tar.at[i], partner).wait_send()
        remote(own_t, own_t, tgs.at[i], tgr.at[i], partner).wait_send()
    for k in range(NY - 1):
        remote(t2, ty.at[k], tys.at[k], tyr.at[k], partner).wait_send()
    store_left.wait()
    store_mem.wait()


def residual(parts, mem_hbm, left_hbm, mean_ref, out_hbm, left_out, mean_out,
             mem, left, out, load_sem, store_sem, left_sem, left_out_sem):
    rows = mem.shape[1] // parts
    blocks = [(m, pl.ds(i * rows, rows), m * parts + i) for m in range(2) for i in range(parts)]
    flight = 3
    loads = [(pltpu.make_async_copy(left_hbm.at[m, :, at], left.at[m, :, at], left_sem.at[i]),
              pltpu.make_async_copy(mem_hbm.at[m, at], mem.at[m, at], load_sem.at[i])) for m, at, i in blocks]
    stores = [pltpu.make_async_copy(out.at[m, at], out_hbm.at[m, at], store_sem.at[i]) for m, at, i in blocks]
    stores_left = [pltpu.make_async_copy(left.at[m, :, at], left_out.at[m, :, at], left_out_sem.at[i])
                   for m, at, i in blocks]
    for i in range(flight):
        for load in loads[i]:
            load.start()
    mean_out[...] = mean_ref[...]
    pairs = []
    for m in range(2):
        mh, ml = split(mean_ref[m])
        pairs.append(jnp.concatenate([mh, mh, ml], axis=0))
    for m, at, i in blocks:
        for load in loads[i]:
            load.wait()
        if i + flight < len(blocks):
            for load in loads[i + flight]:
                load.start()
        lh, ll = split(left[m, :, at])
        approx = dot(jnp.concatenate([lh, ll, lh], axis=0), pairs[m], TN)
        out[m, at, :] = (mem[m, at, :] - approx).astype(BF)
        stores[i].start()
        stores_left[i].start()
    for store in stores + stores_left:
        store.wait()


def shards(NY, NZ, activations, cotangent, error_memory, right_factor):
    tokens, width = activations.shape
    kv = cotangent.shape[2]
    error_memory = error_memory[:, 0]
    group = RANK * kv // (8 * 128 * NZ)
    dma = pltpu.SemaphoreType.DMA
    any_spec = pl.BlockSpec(memory_space=pl.ANY)
    mem, left, mean = pl.pallas_call(
        functools.partial(fused, NY, NZ),
        out_shape=(
            jax.ShapeDtypeStruct((2, width, kv), F32),
            jax.ShapeDtypeStruct((2, RANK, width), F32),
            jax.ShapeDtypeStruct((2, RANK, kv), F32),
        ),
        in_specs=[any_spec] * 4,
        out_specs=(any_spec, any_spec, pl.BlockSpec(memory_space=pltpu.VMEM)),
        scratch_shapes=[
            pltpu.VMEM((NX, tokens, width), BF),
            pltpu.VMEM((2, NX * tokens, kv), BF),
            pltpu.VMEM((2, width, kv), BF),
            pltpu.VMEM((2, RANK, kv), F32),
            pltpu.VMEM((NX, 2 * RANK, tokens), F32),
            pltpu.VMEM((NX, 2 * RANK, tokens), F32),
            pltpu.VMEM((4 * NX * RANK, tokens), BF),
            pltpu.VMEM((2, 2 * RANK, kv), BF),
            pltpu.VMEM((2, NZ, NY, RANK, 128), F32),
            pltpu.VMEM((2, NZ, NY, NX, RANK, 128), F32),
            pltpu.VMEM((NZ, NY, NX, RANK, 128), F32),
            pltpu.VMEM((2, NZ, NX // 2, RANK, 128), F32),
            pltpu.VMEM((2, NZ, NX, RANK, 128), F32),
            pltpu.VMEM((NZ, NX, RANK, 128), F32),
            pltpu.VMEM((NZ - 1, NX, RANK, 128), F32),
            pltpu.VMEM((NX, RANK, 128), F32),
            pltpu.VMEM((NX - 1, RANK, 128), F32),
            pltpu.VMEM((2, NZ, NY, RANK, 128), F32),
            pltpu.VMEM((4 * RANK, width), BF),
            pltpu.VMEM((2, RANK, width), F32),
            pltpu.VMEM((2, width, kv), F32),
            pltpu.VMEM((2, NZ, group, 8, 128), F32),
            pltpu.VMEM((2 * NZ - 1, group, 8, 128), F32),
            pltpu.VMEM((group, 8, 128), F32),
            pltpu.VMEM((NY - 1, group, 8, 128), F32),
            pltpu.VMEM((2, NZ, group, 8, 128), F32),
            dma((6,)),
            dma((NX - 1,)), dma((NX - 1,)),
            dma((12,)), dma((12,)),
            dma((NZ,)), dma((NZ,)),
            dma((2, NZ)), dma((2, NZ)),
            dma((2, NZ)), dma((2, NZ)),
            dma((NZ - 1,)), dma((NZ - 1,)),
            dma((NX - 1,)), dma((NX - 1,)),
            dma((NZ - 1,)), dma((NZ - 1,)),
            dma((4,)), dma((4,)),
            dma((1,)), dma((1,)),
            dma((2 * NZ - 1,)), dma((2 * NZ - 1,)),
            dma((NY - 1,)), dma((NY - 1,)),
            dma((2 * NZ - 1,)), dma((2 * NZ - 1,)),
        ],
        compiler_params=pltpu.CompilerParams(
            collective_id=0, has_side_effects=True, vmem_limit_bytes=56 * 1024 * 1024),
    )(activations, cotangent, error_memory, jnp.swapaxes(right_factor, 1, 2))

    parts = 4
    vmem_spec = pl.BlockSpec(memory_space=pltpu.VMEM)
    new_error, left, mean = pl.pallas_call(
        functools.partial(residual, parts),
        out_shape=(
            jax.ShapeDtypeStruct((2, width, kv), BF),
            jax.ShapeDtypeStruct((2, RANK, width), F32),
            jax.ShapeDtypeStruct((2, RANK, kv), F32),
        ),
        in_specs=[any_spec, any_spec, vmem_spec],
        out_specs=(any_spec, any_spec, vmem_spec),
        scratch_shapes=[
            pltpu.VMEM((2, width, kv), F32),
            pltpu.VMEM((2, RANK, width), F32),
            pltpu.VMEM((2, width, kv), BF),
            dma((2 * parts,)),
            dma((2 * parts,)),
            dma((2 * parts,)),
            dma((2 * parts,)),
        ],
        compiler_params=pltpu.CompilerParams(vmem_limit_bytes=56 * 1024 * 1024),
    )(mem, left, mean)
    return (new_error[:, None], jnp.swapaxes(left, 1, 2)[:, None], jnp.swapaxes(mean, 1, 2))


def build(mesh, NY, NZ):
    return jax.shard_map(
        functools.partial(shards, NY, NZ),
        mesh=mesh,
        in_specs=(
            P(("dp", "tensor"), None),
            P(None, "dp", "tensor"),
            P(None, "dp", None, "tensor"),
            P(None, "tensor", None),
        ),
        out_specs=(
            P(None, "dp", None, "tensor"),
            P(None, "tensor", None, None),
            P(None, "tensor", None),
        ),
        check_vma=False,
    )


def solution(mesh):
    return build(mesh, 4, mesh.shape["dp"] // 8)
```

```python
import functools

import jax
import jax.numpy as jnp
from jax import lax
from jax.experimental import pallas as pl
from jax.experimental.pallas import tpu as pltpu
from jax.sharding import PartitionSpec as P

MESH = pl.DeviceIdType.MESH
BF = jnp.bfloat16
F32 = jnp.float32
NX = 4
RANK = 32
NT = (((1,), (1,)), ((), ()))
TN = (((0,), (0,)), ((), ()))


def split(value):
    high = value.astype(BF)
    return high, (value - high.astype(F32)).astype(BF)


def dot(a, b, dims=None):
    if dims is None:
        dims = (((1,), (0,)), ((), ()))
    return lax.dot_general(a, b, dims, preferred_element_type=F32)


def inverse_factor(gram):
    rows = lax.broadcasted_iota(jnp.int32, (RANK, 2 * RANK), 0)
    cols = lax.broadcasted_iota(jnp.int32, (RANK, 2 * RANK), 1)
    eye = jnp.where(cols == rows + RANK, 1.0, 0.0).astype(F32)
    wide = jnp.concatenate([gram, jnp.zeros((RANK, RANK), F32)], axis=1) + eye
    index = rows[:, :1]
    pivots = jnp.ones((RANK, 1), F32)
    for j in range(RANK):
        row = wide[j:j + 1, :]
        pivot = wide[j:j + 1, j:j + 1]
        column = wide[:, j:j + 1]
        factor = jnp.where(index > j, column * (1.0 / pivot), 0.0)
        pivots = jnp.where(index == j, pivot, pivots)
        wide = wide - factor * row
    return wide[:, RANK:] * (1.0 / jnp.sqrt(pivots))


def fused(NY, NZ, a_hbm, c_hbm, e_hbm, rt_hbm, new_hbm, left_hbm, mean_ref,
          a, c, e, rt, v, vall, vl, rb, pe, p, rc, fy, ry, q, rz, sp, rx, s, sb, sf, us, uf, left, stack, mem, new,
          t, ta, t2, ty, tf,
          lsem, vs, vr, xs, xr, cs, cr, fs, fr, ys, yr, zs, zr, ws, wr, gzs, gzr, gys, gyr, ghs, ghr, gcs, gcr,
          us_sem, ur_sem, tas, tar, tys, tyr, tgs, tgr, out_sem):
    dp, x = lax.axis_index("dp"), lax.axis_index("tensor")
    core, yz = lax.rem(dp, 2), lax.div(dp, 2)
    z, y = lax.rem(yz, NZ), lax.div(yz, NZ)
    other = 1 - core
    tokens = a.shape[1]
    width = a.shape[2]
    kv = c.shape[2]
    span = NY * 128
    ndp = 2 * NY * NZ

    def at_x(k):
        return {"dp": dp, "tensor": lax.rem(x + k, NX)}

    def at_y(k):
        return {"dp": (lax.rem(y + k, NY) * NZ + z) * 2 + core, "tensor": x}

    def at_zc(zz, cc):
        return {"dp": (y * NZ + zz) * 2 + cc, "tensor": x}

    def at_z(zz):
        return at_zc(zz, core)

    partner = at_zc(z, other)
    plane = [(d, k) for d in range(2) for k in range(NZ) if d + k]

    def remote(src, dst, send, recv, device):
        return pltpu.make_async_remote_copy(src_ref=src, dst_ref=dst, send_sem=send, recv_sem=recv,
                                            device_id=device, device_id_type=MESH)

    load_a = pltpu.make_async_copy(a_hbm, a.at[x], lsem.at[0])
    load_c = pltpu.make_async_copy(c_hbm, c, lsem.at[1])
    load_e = pltpu.make_async_copy(e_hbm, e, lsem.at[2])
    load_r = pltpu.make_async_copy(rt_hbm, rt, lsem.at[3])
    load_r.start()
    load_c.start()
    load_a.start()
    load_e.start()

    barrier = pltpu.get_barrier_semaphore()
    for k in range(1, NX):
        pl.semaphore_signal(barrier, inc=1, device_id=at_x(k), device_id_type=MESH)
    for k in range(1, NY):
        pl.semaphore_signal(barrier, inc=1, device_id=at_y(k), device_id_type=MESH)
    for d, k in plane:
        pl.semaphore_signal(barrier, inc=1, device_id=at_zc(lax.rem(z + k, NZ), (core, other)[d]), device_id_type=MESH)

    load_r.wait()
    load_c.wait()
    for m in range(2):
        high, low = split(rt[m])
        rb[m] = jnp.concatenate([high, low], axis=0)
        both = dot(rb[m], c[m], NT)
        vt = both[:RANK] + both[RANK:]
        for b in range(NX):
            v[b, m * RANK:(m + 1) * RANK, :] = vt[:, b * tokens:(b + 1) * tokens]

    pl.semaphore_wait(barrier, NX + NY + 2 * NZ - 3)

    v_copies = []
    for k in range(1, NX):
        copy = remote(v.at[lax.rem(x + k, NX)], vall.at[x], vs.at[k - 1], vr.at[k - 1], at_x(k))
        copy.start()
        v_copies.append(copy)

    quarter = tokens // 4
    left_x, right_x = lax.rem(x + NX - 1, NX), lax.rem(x + 1, NX)
    far_x = lax.rem(x + 2, NX)
    right_dev, left_dev = at_x(1), at_x(NX - 1)

    def quarter_copy(slot, i, sem, device):
        part = a.at[slot, pl.ds(i * quarter, quarter)]
        return remote(part, part, xs.at[sem], xr.at[sem], device)

    to_right = [quarter_copy(x, i, i, right_dev) for i in range(4)]
    to_left = [quarter_copy(x, i, 4 + i, left_dev) for i in (2, 3, 0, 1)]
    forward_right = [quarter_copy(left_x, i, 8 + i, right_dev) for i in range(2)]
    forward_left = [quarter_copy(right_x, 2 + i, 10 + i, left_dev) for i in range(2)]
    load_a.wait()
    for i in range(2):
        to_right[i].start()
        to_left[i].start()

    def left_arrived(parts):
        for i in parts:
            quarter_copy(left_x, i, i, right_dev).wait_recv()

    def right_arrived(parts):
        for i in parts:
            quarter_copy(right_x, i, 4 + i, right_dev).wait_recv()

    def far_arrived():
        for i in range(2):
            quarter_copy(far_x, i, 8 + i, right_dev).wait_recv()
            quarter_copy(far_x, 2 + i, 10 + i, right_dev).wait_recv()

    load_e.wait()

    def error_part(j, carry):
        at = pl.ds(pl.multiple_of(j * span, span), span)
        for m in range(2):
            et = dot(rb[m], e[m, at, :], NT)
            et = et[:RANK] + et[RANK:]
            for yb in range(NY):
                pe[m, j, yb] = et[:, yb * 128:(yb + 1) * 128]
        return carry

    lax.fori_loop(0, NZ, error_part, 0)

    vall[x] = v[x]
    for k in range(1, NX):
        src = lax.rem(x + NX - k, NX)
        remote(v.at[0], vall.at[src], vs.at[k - 1], vr.at[k - 1], at_x(k)).wait_recv()
    stacked = jnp.concatenate(
        [vall[b, m * RANK:(m + 1) * RANK, :] for m in range(2) for b in range(NX)], axis=0)
    high, low = split(stacked)
    block = 2 * NX * RANK
    vl[:block] = high
    vl[block:] = low

    def partials(j):
        zj = lax.rem(z + 1 + j, NZ)
        at = pl.ds(pl.multiple_of(zj * span, span), span)
        both = dot(vl[...], a[x, :, at])
        both = both[:block] + both[block:]
        for m in range(2):
            for yb in range(NY):
                for b in range(NX):
                    r0 = (m * NX + b) * RANK
                    p[m, zj, yb, b] = both[r0:r0 + RANK, yb * 128:(yb + 1) * 128]
        for m in range(2):
            for yb in range(NY):
                p[m, zj, yb, x] = p[m, zj, yb, x] + pe[m, zj, yb]
        remote(p.at[other, zj], rc.at[zj], cs.at[zj], cr.at[zj], partner).start()

    hc = NX // 2
    up, down, far_y = lax.rem(y + 1, NY), lax.rem(y + NY - 1, NY), lax.rem(y + 2, NY)
    to_up, to_down = at_y(1), at_y(NY - 1)

    def over_cores(j):
        zj = lax.rem(z + 1 + j, NZ)
        remote(p.at[other, zj], rc.at[zj], cs.at[zj], cr.at[zj], partner).wait_recv()
        p[core, zj] = p[core, zj] + rc[zj]
        remote(p.at[core, zj, far_y, pl.ds(0, hc)], fy.at[0, zj], fs.at[0, zj], fr.at[0, zj], to_up).start()
        remote(p.at[core, zj, far_y, pl.ds(hc, hc)], fy.at[1, zj], fs.at[1, zj], fr.at[1, zj], to_down).start()

    def staggered(j, carry):
        partials(j)
        over_cores(j - 1)
        return carry

    partials(0)
    lax.fori_loop(1, NZ, staggered, 0)
    over_cores(NZ - 1)

    to_right[2].start()
    to_left[2].start()

    def to_neighbours(j, carry):
        zj = lax.rem(z + 1 + j, NZ)
        for i, target, device in ((0, up, to_up), (1, down, to_down)):
            part = pl.ds(i * hc, hc)
            remote(p.at[core, zj, far_y, part], fy.at[i, zj], fs.at[i, zj], fr.at[i, zj], device).wait_recv()
            p[core, zj, target, part] = p[core, zj, target, part] + fy[i, zj]
            remote(p.at[core, zj, target], ry.at[i, zj], ys.at[i, zj], yr.at[i, zj], device).start()
        return carry

    lax.fori_loop(0, NZ, to_neighbours, 0)

    step = min(512, width)

    def cotangents(parts):
        rows = [pl.ds(pl.multiple_of(slot * tokens + r0, n), n) for slot, r0, n in parts]
        return jnp.concatenate([jnp.concatenate([c[0, r, :], c[1, r, :]], axis=1) for r in rows], axis=0)

    def product(parts, cc, at):
        return dot(jnp.concatenate([a[slot, r0:r0 + n, at] for slot, r0, n in parts], axis=0), cc, TN)

    def accumulate(parts, first=False):
        cc = cotangents(parts)

        def body(i, carry):
            at = pl.ds(pl.multiple_of(i * step, step), step)
            g = product(parts, cc, at)
            for m in range(2):
                base = e[m, at, :].astype(F32) if first else mem[m, at, :]
                mem[m, at, :] = base + g[:, m * kv:(m + 1) * kv]
            return carry

        lax.fori_loop(0, width // step, body, 0)

    half = tokens // 2
    accumulate([(x, 0, tokens)], True)

    def over_y(zj):
        total = p[core, zj, y]
        for i in range(2):
            remote(p.at[core, zj, y], ry.at[i, zj], ys.at[i, zj], yr.at[i, zj], partner).wait_recv()
            total = total + ry[i, zj]
        q[zj] = total

    def over_y_send(j, carry):
        zj = lax.rem(z + 1 + j, NZ)
        over_y(zj)
        remote(q.at[zj], rz.at[j], zs.at[j], zr.at[j], at_z(zj)).start()
        return carry

    lax.fori_loop(0, NZ - 1, over_y_send, 0)
    over_y(z)

    total = q[z]
    for j in range(NZ - 1):
        remote(q.at[z], rz.at[j], zs.at[j], zr.at[j], partner).wait_recv()
        total = total + rz[j]
    sp[...] = total

    def over_x(k, slot):
        return remote(sp.at[lax.rem(x + k + 2 * slot, NX)], rx.at[k - 1, slot], ws.at[k - 1, slot], wr.at[k - 1, slot],
                      at_x(k))

    for k in range(1, NX):
        for slot in range(2):
            over_x(k, slot).start()
    to_right[3].start()
    to_left[3].start()
    for i in range(2):
        left_arrived([i])
        right_arrived([2 + i])
    forward_right[0].start()
    forward_left[0].start()
    accumulate([(left_x, 0, half), (right_x, half, half)])
    for slot in range(2):
        total = sp[lax.rem(x + 2 * slot, NX)]
        for k in range(1, NX):
            over_x(k, slot).wait_recv()
            total = total + rx[k - 1, slot]
        s[core, z, y, slot] = total

    own = s.at[core, z, y]

    def along_z(k):
        return lax.rem(z + NZ - k, NZ)

    def same(piece, send, recv, device):
        return remote(piece, piece, send, recv, device)

    def spread(k):
        piece = s.at[core, along_z(k), y]
        same(piece, gys.at[0, k], gyr.at[0, k], to_up).start()
        same(piece, gys.at[1, k], gyr.at[1, k], to_down).start()

    for k in range(1, NZ):
        same(own, gzs.at[k - 1], gzr.at[k - 1], at_z(lax.rem(z + k, NZ))).start()
    spread(0)

    def from_z(k, carry):
        same(s.at[core, along_z(k), y], gzs.at[k - 1], gzr.at[k - 1], partner).wait_recv()
        spread(k)
        return carry

    lax.fori_loop(1, NZ, from_z, 0)

    def to_partner(r):
        return same(s.at[core, :, lax.rem(y + r, NY)], gcs.at[r], gcr.at[r], partner)

    to_partner(0).start()

    def from_y(first):
        def body(k, carry):
            zz = along_z(k)
            lower, upper = s.at[core, zz, down], s.at[core, zz, up]
            same(lower, gys.at[0, k], gyr.at[0, k], partner).wait_recv()
            same(upper, gys.at[1, k], gyr.at[1, k], partner).wait_recv()
            if first:
                same(lower, ghs.at[k], ghr.at[k], to_up).start()
            else:
                same(upper, ghs.at[k], ghr.at[k], to_down).start()
            return carry
        return body

    lax.fori_loop(0, NZ // 2, from_y(True), 0)
    lax.fori_loop(NZ // 2, NZ, from_y(False), 0)
    to_partner(NY - 1).start()
    to_partner(1).start()

    def from_far(k, carry):
        same(s.at[core, along_z(k), far_y], ghs.at[k], ghr.at[k], partner).wait_recv()
        return carry

    lax.fori_loop(0, NZ, from_far, 0)
    to_partner(2).start()
    left_arrived([2, 3])
    right_arrived([0, 1])
    accumulate([(left_x, half, half), (right_x, 0, half)])
    for r in range(NY):
        same(s.at[other, :, lax.rem(y + r, NY)], gcs.at[r], gcr.at[r], partner).wait_recv()

    def two_terms(dst, slot):
        for m in range(2):
            for zz in range(NZ):
                for yy in range(NY):
                    d0 = (zz * NY + yy) * 128
                    high, low = split(s[m, zz, yy, slot])
                    dst[m * 64:m * 64 + 32, d0:d0 + 128] = high
                    dst[m * 64 + 32:m * 64 + 64, d0:d0 + 128] = low

    two_terms(sf, 1)
    u = dot(sf[...], a[x], NT)
    for m in range(2):
        us[m * RANK:(m + 1) * RANK, :] = u[m * 64:m * 64 + 32] + u[m * 64 + 32:m * 64 + 64]
    to_far = remote(us, uf, us_sem.at[0], ur_sem.at[0], at_x(2))
    to_far.start()
    forward_right[1].start()
    forward_left[1].start()
    two_terms(sb, 0)

    right = []
    for m in range(2):
        both = dot(sb[m * 64:m * 64 + 64, :], e[m])
        right.append(both[:RANK] + both[RANK:])

    def add_right(slot, m, um):
        tok = pl.ds(pl.multiple_of(slot * tokens, tokens), tokens)
        both = dot(jnp.concatenate(split(um), axis=0), c[m, tok, :])
        right[m] = right[m] + both[:RANK] + both[RANK:]

    for slot in (x, left_x, right_x):
        u = dot(sb[...], a[slot], NT)
        for m in range(2):
            add_right(slot, m, u[m * 64:m * 64 + 32] + u[m * 64 + 32:m * 64 + 64])
    to_far.wait_recv()
    for m in range(2):
        add_right(far_x, m, uf[m * RANK:(m + 1) * RANK, :])

    group = t.shape[2]
    per_row = kv // 128

    def piece(i):
        return i // group, i % group

    for m in range(2):
        for i in range(NZ * group):
            rr, kk = i // per_row, i % per_row
            t[(m,) + piece(i)] = right[m][rr * 8:rr * 8 + 8, kk * 128:kk * 128 + 128]
    for i, (d, k) in enumerate(plane):
        zk, ck = lax.rem(z + k, NZ), (core, other)[d]
        remote(t.at[ck, zk], ta.at[i], tas.at[i], tar.at[i], at_zc(zk, ck)).start()
    inverse = []
    for m in range(2):
        both = dot(sb[m * 64:m * 64 + 64, :], sb[m * 64:m * 64 + 64, :], NT)
        inverse.append(inverse_factor(
            both[:RANK, :RANK] + both[:RANK, RANK:] + both[RANK:, :RANK] + both[RANK:, RANK:]))
    total = t[core, z]
    for i in range(len(plane)):
        remote(t.at[core, z], ta.at[i], tas.at[i], tar.at[i], partner).wait_recv()
        total = total + ta[i]
    t2[...] = total
    for k in range(1, NY):
        remote(t2, ty.at[k - 1], tys.at[k - 1], tyr.at[k - 1], at_y(k)).start()
    for k in range(1, NY):
        remote(t2, ty.at[k - 1], tys.at[k - 1], tyr.at[k - 1], partner).wait_recv()
        total = total + ty[k - 1]
    tf[core, z] = total
    own_t = tf.at[core, z]
    for i, (d, k) in enumerate(plane):
        remote(own_t, own_t, tgs.at[i], tgr.at[i], at_zc(lax.rem(z + k, NZ), (core, other)[d])).start()
    for m in range(2):
        high, low = split(inverse[m])
        pair = jnp.concatenate([high, low], axis=0)
        for i in range(width // step):
            at = pl.ds(i * step, step)
            both = dot(pair, sb[m * 64:m * 64 + 32, at])
            lt = both[:RANK] + both[RANK:] + dot(high, sb[m * 64 + 32:m * 64 + 64, at])
            left[m, :, at] = lt
            lh, ll = split(lt)
            stack[m * 96:m * 96 + 96, at] = jnp.concatenate([lh, ll, lh], axis=0)
    store_left = pltpu.make_async_copy(left, left_hbm, lsem.at[4])
    store_left.start()
    for i, (d, k) in enumerate(plane):
        got = tf.at[(core, other)[d], lax.rem(z + NZ - k, NZ)]
        remote(got, got, tgs.at[i], tgr.at[i], partner).wait_recv()

    means = []
    for m in range(2):
        tt = jnp.concatenate(
            [jnp.concatenate([tf[(m,) + piece(rr * per_row + kk)] for kk in range(per_row)], axis=1)
             for rr in range(RANK // 8)], axis=0)
        wh, wl = split(inverse[m])
        th, tl = split(tt)
        both = dot(jnp.concatenate([wh, wl], axis=0), th)
        mean = (both[:RANK] + both[RANK:] + dot(wh, tl)) * (1.0 / ndp)
        mean_ref[m] = mean
        mh, ml = split(mean)
        means.append(jnp.concatenate([mh, mh, ml], axis=0))

    def subtract(i, carry):
        at = pl.ds(pl.multiple_of(i * step, step), step)
        for m in range(2):
            mem[m, at, :] = mem[m, at, :] - dot(stack[m * 96:m * 96 + 96, at], means[m], TN)
        return carry

    lax.fori_loop(0, width // step, subtract, 0)

    far_arrived()
    far_parts = [(far_x, 0, tokens)]
    cc_far = cotangents(far_parts)

    def store_new(i):
        at = pl.ds(pl.multiple_of(i * step, step), step)
        return pltpu.make_async_copy(new.at[:, at], new_hbm.at[:, at], out_sem.at[i])

    def finish(i, carry):
        at = pl.ds(pl.multiple_of(i * step, step), step)
        g = product(far_parts, cc_far, at)
        for m in range(2):
            new[m, at, :] = (mem[m, at, :] + g[:, m * kv:(m + 1) * kv]).astype(BF)
        store_new(i).start()
        return carry

    lax.fori_loop(0, width // step, finish, 0)

    for copy in v_copies + to_right + to_left + forward_right + forward_left:
        copy.wait_send()

    def sent(j, carry):
        remote(p.at[other, j], rc.at[j], cs.at[j], cr.at[j], partner).wait_send()
        for i in range(2):
            remote(fy.at[i, j], fy.at[i, j], fs.at[i, j], fr.at[i, j], partner).wait_send()
            remote(p.at[core, j, y], ry.at[i, j], ys.at[i, j], yr.at[i, j], partner).wait_send()
        return carry

    lax.fori_loop(0, NZ, sent, 0)
    for j in range(NZ - 1):
        remote(q.at[j], rz.at[j], zs.at[j], zr.at[j], partner).wait_send()
        same(own, gzs.at[j], gzr.at[j], partner).wait_send()
    for k in range(1, NX):
        for slot in range(2):
            over_x(k, slot).wait_send()

    def sent_s(k, carry):
        same(own, gys.at[0, k], gyr.at[0, k], partner).wait_send()
        same(own, gys.at[1, k], gyr.at[1, k], partner).wait_send()
        same(own, ghs.at[k], ghr.at[k], partner).wait_send()
        return carry

    lax.fori_loop(0, NZ, sent_s, 0)
    for r in range(NY):
        to_partner(r).wait_send()
    to_far.wait_send()
    for i in range(len(plane)):
        remote(t2, ta.at[i], tas.at[i], tar.at[i], partner).wait_send()
        remote(own_t, own_t, tgs.at[i], tgr.at[i], partner).wait_send()
    for k in range(NY - 1):
        remote(t2, ty.at[k], tys.at[k], tyr.at[k], partner).wait_send()
    store_left.wait()

    def stored(i, carry):
        store_new(i).wait()
        return carry

    lax.fori_loop(0, width // step, stored, 0)


def hand_over(parts, new_hbm, left_hbm, mean_ref, new_out, left_out, mean_out, sems):
    rows = new_hbm.shape[1] // parts
    copies = [pltpu.make_async_copy(new_hbm.at[m, pl.ds(i * rows, rows)], new_out.at[m, pl.ds(i * rows, rows)],
                                    sems.at[m * parts + i]) for m in range(2) for i in range(parts)]
    copies.append(pltpu.make_async_copy(left_hbm, left_out, sems.at[2 * parts]))
    for copy in copies:
        copy.start()
    mean_out[...] = mean_ref[...]
    for copy in copies:
        copy.wait()


def shards(NY, NZ, activations, cotangent, error_memory, right_factor):
    tokens, width = activations.shape
    kv = cotangent.shape[2]
    error_memory = error_memory[:, 0]
    group = RANK * kv // (8 * 128 * NZ)
    dma = pltpu.SemaphoreType.DMA
    any_spec = pl.BlockSpec(memory_space=pl.ANY)
    new_error, left, mean = pl.pallas_call(
        functools.partial(fused, NY, NZ),
        out_shape=(
            jax.ShapeDtypeStruct((2, width, kv), BF),
            jax.ShapeDtypeStruct((2, RANK, width), F32),
            jax.ShapeDtypeStruct((2, RANK, kv), F32),
        ),
        in_specs=[any_spec] * 4,
        out_specs=(any_spec, any_spec, pl.BlockSpec(memory_space=pltpu.VMEM)),
        scratch_shapes=[
            pltpu.VMEM((NX, tokens, width), BF),
            pltpu.VMEM((2, NX * tokens, kv), BF),
            pltpu.VMEM((2, width, kv), BF),
            pltpu.VMEM((2, RANK, kv), F32),
            pltpu.VMEM((NX, 2 * RANK, tokens), F32),
            pltpu.VMEM((NX, 2 * RANK, tokens), F32),
            pltpu.VMEM((4 * NX * RANK, tokens), BF),
            pltpu.VMEM((2, 2 * RANK, kv), BF),
            pltpu.VMEM((2, NZ, NY, RANK, 128), F32),
            pltpu.VMEM((2, NZ, NY, NX, RANK, 128), F32),
            pltpu.VMEM((NZ, NY, NX, RANK, 128), F32),
            pltpu.VMEM((2, NZ, NX // 2, RANK, 128), F32),
            pltpu.VMEM((2, NZ, NX, RANK, 128), F32),
            pltpu.VMEM((NZ, NX, RANK, 128), F32),
            pltpu.VMEM((NZ - 1, NX, RANK, 128), F32),
            pltpu.VMEM((NX, RANK, 128), F32),
            pltpu.VMEM((NX - 1, 2, RANK, 128), F32),
            pltpu.VMEM((2, NZ, NY, 2, RANK, 128), F32),
            pltpu.VMEM((4 * RANK, width), BF),
            pltpu.VMEM((4 * RANK, width), BF),
            pltpu.VMEM((2 * RANK, tokens), F32),
            pltpu.VMEM((2 * RANK, tokens), F32),
            pltpu.VMEM((2, RANK, width), F32),
            pltpu.VMEM((6 * RANK, width), BF),
            pltpu.VMEM((2, width, kv), F32),
            pltpu.VMEM((2, width, kv), BF),
            pltpu.VMEM((2, NZ, group, 8, 128), F32),
            pltpu.VMEM((2 * NZ - 1, group, 8, 128), F32),
            pltpu.VMEM((group, 8, 128), F32),
            pltpu.VMEM((NY - 1, group, 8, 128), F32),
            pltpu.VMEM((2, NZ, group, 8, 128), F32),
            dma((6,)),
            dma((NX - 1,)), dma((NX - 1,)),
            dma((12,)), dma((12,)),
            dma((NZ,)), dma((NZ,)),
            dma((2, NZ)), dma((2, NZ)),
            dma((2, NZ)), dma((2, NZ)),
            dma((NZ - 1,)), dma((NZ - 1,)),
            dma((NX - 1, 2)), dma((NX - 1, 2)),
            dma((NZ - 1,)), dma((NZ - 1,)),
            dma((2, NZ)), dma((2, NZ)),
            dma((NZ,)), dma((NZ,)),
            dma((NY,)), dma((NY,)),
            dma((1,)), dma((1,)),
            dma((2 * NZ - 1,)), dma((2 * NZ - 1,)),
            dma((NY - 1,)), dma((NY - 1,)),
            dma((2 * NZ - 1,)), dma((2 * NZ - 1,)),
            dma((max(1, width // 512),)),
        ],
        compiler_params=pltpu.CompilerParams(
            collective_id=0, has_side_effects=True, vmem_limit_bytes=56 * 1024 * 1024),
    )(activations, cotangent, error_memory, jnp.swapaxes(right_factor, 1, 2))

    parts = 4
    vmem_spec = pl.BlockSpec(memory_space=pltpu.VMEM)
    new_error, left, mean = pl.pallas_call(
        functools.partial(hand_over, parts),
        out_shape=(
            jax.ShapeDtypeStruct((2, width, kv), BF),
            jax.ShapeDtypeStruct((2, RANK, width), F32),
            jax.ShapeDtypeStruct((2, RANK, kv), F32),
        ),
        in_specs=[any_spec, any_spec, vmem_spec],
        out_specs=(any_spec, any_spec, vmem_spec),
        scratch_shapes=[dma((2 * parts + 1,))],
        compiler_params=pltpu.CompilerParams(vmem_limit_bytes=56 * 1024 * 1024),
    )(new_error, left, mean)
    return (new_error[:, None], jnp.swapaxes(left, 1, 2)[:, None], jnp.swapaxes(mean, 1, 2))


def build(mesh, NY, NZ):
    return jax.shard_map(
        functools.partial(shards, NY, NZ),
        mesh=mesh,
        in_specs=(
            P(("dp", "tensor"), None),
            P(None, "dp", "tensor"),
            P(None, "dp", None, "tensor"),
            P(None, "tensor", None),
        ),
        out_specs=(
            P(None, "dp", None, "tensor"),
            P(None, "tensor", None, None),
            P(None, "tensor", None),
        ),
        check_vma=False,
    )


def solution(mesh):
    return build(mesh, 4, mesh.shape["dp"] // 8)
```

```python
import functools

import jax
import jax.numpy as jnp
from jax import lax
from jax.experimental import pallas as pl
from jax.experimental.pallas import tpu as pltpu
from jax.sharding import PartitionSpec as P

MESH = pl.DeviceIdType.MESH
BF = jnp.bfloat16
F32 = jnp.float32
NX = 4
RANK = 32
NT = (((1,), (1,)), ((), ()))
TN = (((0,), (0,)), ((), ()))


def split(value):
    high = value.astype(BF)
    return high, (value - high.astype(F32)).astype(BF)


def dot(a, b, dims=None):
    if dims is None:
        dims = (((1,), (0,)), ((), ()))
    return lax.dot_general(a, b, dims, preferred_element_type=F32)


def inverse_factor(gram):
    rows = lax.broadcasted_iota(jnp.int32, (RANK, 2 * RANK), 0)
    cols = lax.broadcasted_iota(jnp.int32, (RANK, 2 * RANK), 1)
    eye = jnp.where(cols == rows + RANK, 1.0, 0.0).astype(F32)
    wide = jnp.concatenate([gram, jnp.zeros((RANK, RANK), F32)], axis=1) + eye
    index = rows[:, :1]
    pivots = jnp.ones((RANK, 1), F32)
    for j in range(RANK):
        row = wide[j:j + 1, :]
        pivot = wide[j:j + 1, j:j + 1]
        column = wide[:, j:j + 1]
        factor = jnp.where(index > j, column * (1.0 / pivot), 0.0)
        pivots = jnp.where(index == j, pivot, pivots)
        wide = wide - factor * row
    return wide[:, RANK:] * (1.0 / jnp.sqrt(pivots))


def fused(NY, NZ, a_hbm, c_hbm, e_hbm, rt_hbm, new_hbm, left_hbm, mean_ref,
          a, c, e, rt, v, vall, vl, rb, pe, p, rc, fy, ry, q, rz, sp, rx, s, sb, sf, us, uf, left, stack, mem, new,
          t, ta, t2, ty, tf,
          lsem, vs, vr, xs, xr, cs, cr, fs, fr, ys, yr, zs, zr, ws, wr, gzs, gzr, gys, gyr, ghs, ghr, gcs, gcr,
          us_sem, ur_sem, tas, tar, tys, tyr, tgs, tgr, out_sem):
    dp, x = lax.axis_index("dp"), lax.axis_index("tensor")
    core, yz = lax.rem(dp, 2), lax.div(dp, 2)
    z, y = lax.rem(yz, NZ), lax.div(yz, NZ)
    other = 1 - core
    tokens = a.shape[1]
    width = a.shape[2]
    kv = c.shape[2]
    span = NY * 128
    ndp = 2 * NY * NZ

    def at_x(k):
        return {"dp": dp, "tensor": lax.rem(x + k, NX)}

    def at_y(k):
        return {"dp": (lax.rem(y + k, NY) * NZ + z) * 2 + core, "tensor": x}

    def at_zc(zz, cc):
        return {"dp": (y * NZ + zz) * 2 + cc, "tensor": x}

    def at_z(zz):
        return at_zc(zz, core)

    partner = at_zc(z, other)
    plane = [(d, k) for d in range(2) for k in range(NZ) if d + k]

    def remote(src, dst, send, recv, device):
        return pltpu.make_async_remote_copy(src_ref=src, dst_ref=dst, send_sem=send, recv_sem=recv,
                                            device_id=device, device_id_type=MESH)

    load_a = pltpu.make_async_copy(a_hbm, a.at[x], lsem.at[0])
    load_c = pltpu.make_async_copy(c_hbm, c, lsem.at[1])
    load_e = pltpu.make_async_copy(e_hbm, e, lsem.at[2])
    load_r = pltpu.make_async_copy(rt_hbm, rt, lsem.at[3])
    load_r.start()
    load_c.start()

    barrier = pltpu.get_barrier_semaphore()
    for k in range(1, NX):
        pl.semaphore_signal(barrier, inc=1, device_id=at_x(k), device_id_type=MESH)
    for k in range(1, NY):
        pl.semaphore_signal(barrier, inc=1, device_id=at_y(k), device_id_type=MESH)
    for d, k in plane:
        pl.semaphore_signal(barrier, inc=1, device_id=at_zc(lax.rem(z + k, NZ), (core, other)[d]), device_id_type=MESH)

    load_r.wait()
    load_c.wait()
    load_a.start()
    load_e.start()
    for m in range(2):
        high, low = split(rt[m])
        rb[m] = jnp.concatenate([high, low], axis=0)
        both = dot(rb[m], c[m], NT)
        vt = both[:RANK] + both[RANK:]
        for b in range(NX):
            v[b, m * RANK:(m + 1) * RANK, :] = vt[:, b * tokens:(b + 1) * tokens]

    pl.semaphore_wait(barrier, NX + NY + 2 * NZ - 3)

    v_copies = []
    for k in range(1, NX):
        copy = remote(v.at[lax.rem(x + k, NX)], vall.at[x], vs.at[k - 1], vr.at[k - 1], at_x(k))
        copy.start()
        v_copies.append(copy)

    quarter = tokens // 4
    left_x, right_x = lax.rem(x + NX - 1, NX), lax.rem(x + 1, NX)
    far_x = lax.rem(x + 2, NX)
    right_dev, left_dev = at_x(1), at_x(NX - 1)

    def quarter_copy(slot, i, sem, device):
        part = a.at[slot, pl.ds(i * quarter, quarter)]
        return remote(part, part, xs.at[sem], xr.at[sem], device)

    def own_quarter(i, sem, device):
        part = pl.ds(i * quarter, quarter)
        return remote(a_hbm.at[part], a.at[x, part], xs.at[sem], xr.at[sem], device)

    to_right = [own_quarter(i, i, right_dev) for i in range(4)]
    to_left = [own_quarter(i, 4 + i, left_dev) for i in (2, 3, 0, 1)]
    forward_right = [quarter_copy(left_x, i, 8 + i, right_dev) for i in range(2)]
    forward_left = [quarter_copy(right_x, 2 + i, 10 + i, left_dev) for i in range(2)]
    for i in range(2):
        to_right[i].start()
        to_left[i].start()

    def left_arrived(parts):
        for i in parts:
            quarter_copy(left_x, i, i, right_dev).wait_recv()

    def right_arrived(parts):
        for i in parts:
            quarter_copy(right_x, i, 4 + i, right_dev).wait_recv()

    def far_arrived():
        for i in range(2):
            quarter_copy(far_x, i, 8 + i, right_dev).wait_recv()
            quarter_copy(far_x, 2 + i, 10 + i, right_dev).wait_recv()

    load_e.wait()
    load_a.wait()

    def error_part(j, carry):
        at = pl.ds(pl.multiple_of(j * span, span), span)
        for m in range(2):
            et = dot(rb[m], e[m, at, :], NT)
            et = et[:RANK] + et[RANK:]
            for yb in range(NY):
                pe[m, j, yb] = et[:, yb * 128:(yb + 1) * 128]
        return carry

    lax.fori_loop(0, NZ, error_part, 0)

    vall[x] = v[x]
    for k in range(1, NX):
        src = lax.rem(x + NX - k, NX)
        remote(v.at[0], vall.at[src], vs.at[k - 1], vr.at[k - 1], at_x(k)).wait_recv()
    stacked = jnp.concatenate(
        [vall[b, m * RANK:(m + 1) * RANK, :] for m in range(2) for b in range(NX)], axis=0)
    high, low = split(stacked)
    block = 2 * NX * RANK
    vl[:block] = high
    vl[block:] = low

    def partials(j):
        zj = lax.rem(z + 1 + j, NZ)
        at = pl.ds(pl.multiple_of(zj * span, span), span)
        both = dot(vl[...], a[x, :, at])
        both = both[:block] + both[block:]
        for m in range(2):
            for yb in range(NY):
                for b in range(NX):
                    r0 = (m * NX + b) * RANK
                    p[m, zj, yb, b] = both[r0:r0 + RANK, yb * 128:(yb + 1) * 128]
        for m in range(2):
            for yb in range(NY):
                p[m, zj, yb, x] = p[m, zj, yb, x] + pe[m, zj, yb]
        remote(p.at[other, zj], rc.at[zj], cs.at[zj], cr.at[zj], partner).start()

    hc = NX // 2
    up, down, far_y = lax.rem(y + 1, NY), lax.rem(y + NY - 1, NY), lax.rem(y + 2, NY)
    to_up, to_down = at_y(1), at_y(NY - 1)

    def over_cores(j):
        zj = lax.rem(z + 1 + j, NZ)
        remote(p.at[other, zj], rc.at[zj], cs.at[zj], cr.at[zj], partner).wait_recv()
        p[core, zj] = p[core, zj] + rc[zj]
        remote(p.at[core, zj, far_y, pl.ds(0, hc)], fy.at[0, zj], fs.at[0, zj], fr.at[0, zj], to_up).start()
        remote(p.at[core, zj, far_y, pl.ds(hc, hc)], fy.at[1, zj], fs.at[1, zj], fr.at[1, zj], to_down).start()

    def staggered(j, carry):
        partials(j)
        over_cores(j - 1)
        return carry

    partials(0)
    lax.fori_loop(1, NZ, staggered, 0)
    over_cores(NZ - 1)

    to_right[2].start()
    to_left[2].start()

    def to_neighbours(j, carry):
        zj = lax.rem(z + 1 + j, NZ)
        for i, target, device in ((0, up, to_up), (1, down, to_down)):
            part = pl.ds(i * hc, hc)
            remote(p.at[core, zj, far_y, part], fy.at[i, zj], fs.at[i, zj], fr.at[i, zj], device).wait_recv()
            p[core, zj, target, part] = p[core, zj, target, part] + fy[i, zj]
            remote(p.at[core, zj, target], ry.at[i, zj], ys.at[i, zj], yr.at[i, zj], device).start()
        return carry

    lax.fori_loop(0, NZ, to_neighbours, 0)

    step = min(512, width)

    def cotangents(parts):
        rows = [pl.ds(pl.multiple_of(slot * tokens + r0, n), n) for slot, r0, n in parts]
        return jnp.concatenate([jnp.concatenate([c[0, r, :], c[1, r, :]], axis=1) for r in rows], axis=0)

    def product(parts, cc, at):
        return dot(jnp.concatenate([a[slot, r0:r0 + n, at] for slot, r0, n in parts], axis=0), cc, TN)

    def accumulate(parts, first=False):
        cc = cotangents(parts)

        def body(i, carry):
            at = pl.ds(pl.multiple_of(i * step, step), step)
            g = product(parts, cc, at)
            for m in range(2):
                base = e[m, at, :].astype(F32) if first else mem[m, at, :]
                mem[m, at, :] = base + g[:, m * kv:(m + 1) * kv]
            return carry

        lax.fori_loop(0, width // step, body, 0)

    half = tokens // 2
    accumulate([(x, 0, tokens)], True)

    def over_y(zj):
        total = p[core, zj, y]
        for i in range(2):
            remote(p.at[core, zj, y], ry.at[i, zj], ys.at[i, zj], yr.at[i, zj], partner).wait_recv()
            total = total + ry[i, zj]
        q[zj] = total

    def over_y_send(j, carry):
        zj = lax.rem(z + 1 + j, NZ)
        over_y(zj)
        remote(q.at[zj], rz.at[j], zs.at[j], zr.at[j], at_z(zj)).start()
        return carry

    lax.fori_loop(0, NZ - 1, over_y_send, 0)
    over_y(z)

    total = q[z]
    for j in range(NZ - 1):
        remote(q.at[z], rz.at[j], zs.at[j], zr.at[j], partner).wait_recv()
        total = total + rz[j]
    sp[...] = total

    def over_x(k, slot):
        return remote(sp.at[lax.rem(x + k + 2 * slot, NX)], rx.at[k - 1, slot], ws.at[k - 1, slot], wr.at[k - 1, slot],
                      at_x(k))

    for k in range(1, NX):
        for slot in range(2):
            over_x(k, slot).start()
    to_right[3].start()
    to_left[3].start()
    for i in range(2):
        left_arrived([i])
        right_arrived([2 + i])
    forward_right[0].start()
    forward_left[0].start()
    accumulate([(left_x, 0, half), (right_x, half, half)])
    for slot in range(2):
        total = sp[lax.rem(x + 2 * slot, NX)]
        for k in range(1, NX):
            over_x(k, slot).wait_recv()
            total = total + rx[k - 1, slot]
        s[core, z, y, slot] = total

    own = s.at[core, z, y]

    def along_z(k):
        return lax.rem(z + NZ - k, NZ)

    def same(piece, send, recv, device):
        return remote(piece, piece, send, recv, device)

    def spread(k):
        piece = s.at[core, along_z(k), y]
        same(piece, gys.at[0, k], gyr.at[0, k], to_up).start()
        same(piece, gys.at[1, k], gyr.at[1, k], to_down).start()

    for k in range(1, NZ):
        same(own, gzs.at[k - 1], gzr.at[k - 1], at_z(lax.rem(z + k, NZ))).start()
    spread(0)

    def from_z(k, carry):
        same(s.at[core, along_z(k), y], gzs.at[k - 1], gzr.at[k - 1], partner).wait_recv()
        spread(k)
        return carry

    lax.fori_loop(1, NZ, from_z, 0)

    def to_partner(r):
        return same(s.at[core, :, lax.rem(y + r, NY)], gcs.at[r], gcr.at[r], partner)

    to_partner(0).start()

    def from_y(first):
        def body(k, carry):
            zz = along_z(k)
            lower, upper = s.at[core, zz, down], s.at[core, zz, up]
            same(lower, gys.at[0, k], gyr.at[0, k], partner).wait_recv()
            same(upper, gys.at[1, k], gyr.at[1, k], partner).wait_recv()
            if first:
                same(lower, ghs.at[k], ghr.at[k], to_up).start()
            else:
                same(upper, ghs.at[k], ghr.at[k], to_down).start()
            return carry
        return body

    lax.fori_loop(0, NZ // 2, from_y(True), 0)
    lax.fori_loop(NZ // 2, NZ, from_y(False), 0)
    to_partner(NY - 1).start()
    to_partner(1).start()

    def from_far(k, carry):
        same(s.at[core, along_z(k), far_y], ghs.at[k], ghr.at[k], partner).wait_recv()
        return carry

    lax.fori_loop(0, NZ, from_far, 0)
    to_partner(2).start()
    left_arrived([2, 3])
    right_arrived([0, 1])
    accumulate([(left_x, half, half), (right_x, 0, half)])
    for r in range(NY):
        same(s.at[other, :, lax.rem(y + r, NY)], gcs.at[r], gcr.at[r], partner).wait_recv()

    def two_terms(dst, slot):
        for m in range(2):
            for zz in range(NZ):
                for yy in range(NY):
                    d0 = (zz * NY + yy) * 128
                    high, low = split(s[m, zz, yy, slot])
                    dst[m * 64:m * 64 + 32, d0:d0 + 128] = high
                    dst[m * 64 + 32:m * 64 + 64, d0:d0 + 128] = low

    two_terms(sf, 1)
    u = dot(sf[...], a[x], NT)
    for m in range(2):
        us[m * RANK:(m + 1) * RANK, :] = u[m * 64:m * 64 + 32] + u[m * 64 + 32:m * 64 + 64]
    to_far = remote(us, uf, us_sem.at[0], ur_sem.at[0], at_x(2))
    to_far.start()
    forward_right[1].start()
    forward_left[1].start()
    two_terms(sb, 0)

    right = []
    for m in range(2):
        both = dot(sb[m * 64:m * 64 + 64, :], e[m])
        right.append(both[:RANK] + both[RANK:])

    def add_right(slot, m, um):
        tok = pl.ds(pl.multiple_of(slot * tokens, tokens), tokens)
        both = dot(jnp.concatenate(split(um), axis=0), c[m, tok, :])
        right[m] = right[m] + both[:RANK] + both[RANK:]

    for slot in (x, left_x, right_x):
        u = dot(sb[...], a[slot], NT)
        for m in range(2):
            add_right(slot, m, u[m * 64:m * 64 + 32] + u[m * 64 + 32:m * 64 + 64])
    to_far.wait_recv()
    for m in range(2):
        add_right(far_x, m, uf[m * RANK:(m + 1) * RANK, :])

    group = t.shape[2]
    per_row = kv // 128

    def piece(i):
        return i // group, i % group

    for m in range(2):
        for i in range(NZ * group):
            rr, kk = i // per_row, i % per_row
            t[(m,) + piece(i)] = right[m][rr * 8:rr * 8 + 8, kk * 128:kk * 128 + 128]
    for i, (d, k) in enumerate(plane):
        zk, ck = lax.rem(z + k, NZ), (core, other)[d]
        remote(t.at[ck, zk], ta.at[i], tas.at[i], tar.at[i], at_zc(zk, ck)).start()
    inverse = []
    for m in range(2):
        both = dot(sb[m * 64:m * 64 + 64, :], sb[m * 64:m * 64 + 64, :], NT)
        inverse.append(inverse_factor(
            both[:RANK, :RANK] + both[:RANK, RANK:] + both[RANK:, :RANK] + both[RANK:, RANK:]))
    total = t[core, z]
    for i in range(len(plane)):
        remote(t.at[core, z], ta.at[i], tas.at[i], tar.at[i], partner).wait_recv()
        total = total + ta[i]
    t2[...] = total
    for k in range(1, NY):
        remote(t2, ty.at[k - 1], tys.at[k - 1], tyr.at[k - 1], at_y(k)).start()
    for k in range(1, NY):
        remote(t2, ty.at[k - 1], tys.at[k - 1], tyr.at[k - 1], partner).wait_recv()
        total = total + ty[k - 1]
    tf[core, z] = total
    own_t = tf.at[core, z]
    for i, (d, k) in enumerate(plane):
        remote(own_t, own_t, tgs.at[i], tgr.at[i], at_zc(lax.rem(z + k, NZ), (core, other)[d])).start()
    for m in range(2):
        high, low = split(inverse[m])
        pair = jnp.concatenate([high, low], axis=0)
        for i in range(width // step):
            at = pl.ds(i * step, step)
            both = dot(pair, sb[m * 64:m * 64 + 32, at])
            lt = both[:RANK] + both[RANK:] + dot(high, sb[m * 64 + 32:m * 64 + 64, at])
            left[m, :, at] = lt
            lh, ll = split(lt)
            stack[m * 96:m * 96 + 96, at] = jnp.concatenate([lh, ll, lh], axis=0)
    store_left = pltpu.make_async_copy(left, left_hbm, lsem.at[4])
    store_left.start()
    for i, (d, k) in enumerate(plane):
        got = tf.at[(core, other)[d], lax.rem(z + NZ - k, NZ)]
        remote(got, got, tgs.at[i], tgr.at[i], partner).wait_recv()

    means = []
    for m in range(2):
        tt = jnp.concatenate(
            [jnp.concatenate([tf[(m,) + piece(rr * per_row + kk)] for kk in range(per_row)], axis=1)
             for rr in range(RANK // 8)], axis=0)
        wh, wl = split(inverse[m])
        th, tl = split(tt)
        both = dot(jnp.concatenate([wh, wl], axis=0), th)
        mean = (both[:RANK] + both[RANK:] + dot(wh, tl)) * (1.0 / ndp)
        mean_ref[m] = mean
        mh, ml = split(mean)
        means.append(jnp.concatenate([mh, mh, ml], axis=0))

    def subtract(i, carry):
        at = pl.ds(pl.multiple_of(i * step, step), step)
        for m in range(2):
            mem[m, at, :] = mem[m, at, :] - dot(stack[m * 96:m * 96 + 96, at], means[m], TN)
        return carry

    lax.fori_loop(0, width // step, subtract, 0)

    far_arrived()
    far_parts = [(far_x, 0, tokens)]
    cc_far = cotangents(far_parts)

    def store_new(i):
        at = pl.ds(pl.multiple_of(i * step, step), step)
        return pltpu.make_async_copy(new.at[:, at], new_hbm.at[:, at], out_sem.at[i])

    def finish(i, carry):
        at = pl.ds(pl.multiple_of(i * step, step), step)
        g = product(far_parts, cc_far, at)
        for m in range(2):
            new[m, at, :] = (mem[m, at, :] + g[:, m * kv:(m + 1) * kv]).astype(BF)
        store_new(i).start()
        return carry

    lax.fori_loop(0, width // step, finish, 0)

    for copy in v_copies + to_right + to_left + forward_right + forward_left:
        copy.wait_send()

    def sent(j, carry):
        remote(p.at[other, j], rc.at[j], cs.at[j], cr.at[j], partner).wait_send()
        for i in range(2):
            remote(fy.at[i, j], fy.at[i, j], fs.at[i, j], fr.at[i, j], partner).wait_send()
            remote(p.at[core, j, y], ry.at[i, j], ys.at[i, j], yr.at[i, j], partner).wait_send()
        return carry

    lax.fori_loop(0, NZ, sent, 0)
    for j in range(NZ - 1):
        remote(q.at[j], rz.at[j], zs.at[j], zr.at[j], partner).wait_send()
        same(own, gzs.at[j], gzr.at[j], partner).wait_send()
    for k in range(1, NX):
        for slot in range(2):
            over_x(k, slot).wait_send()

    def sent_s(k, carry):
        same(own, gys.at[0, k], gyr.at[0, k], partner).wait_send()
        same(own, gys.at[1, k], gyr.at[1, k], partner).wait_send()
        same(own, ghs.at[k], ghr.at[k], partner).wait_send()
        return carry

    lax.fori_loop(0, NZ, sent_s, 0)
    for r in range(NY):
        to_partner(r).wait_send()
    to_far.wait_send()
    for i in range(len(plane)):
        remote(t2, ta.at[i], tas.at[i], tar.at[i], partner).wait_send()
        remote(own_t, own_t, tgs.at[i], tgr.at[i], partner).wait_send()
    for k in range(NY - 1):
        remote(t2, ty.at[k], tys.at[k], tyr.at[k], partner).wait_send()
    store_left.wait()

    def stored(i, carry):
        store_new(i).wait()
        return carry

    lax.fori_loop(0, width // step, stored, 0)


def hand_over(parts, new_hbm, left_hbm, mean_ref, new_out, left_out, mean_out, new, left, load_sem, store_sem):
    rows = new_hbm.shape[1] // parts
    at = [(m, pl.ds(i * rows, rows)) for m in range(2) for i in range(parts)]
    moves = [(new_hbm.at[w], new.at[w], new_out.at[w]) for w in at]
    moves += [(left_hbm.at[m], left.at[m], left_out.at[m]) for m in range(2)]
    loads = [pltpu.make_async_copy(src, mid, load_sem.at[i]) for i, (src, mid, dst) in enumerate(moves)]
    stores = [pltpu.make_async_copy(mid, dst, store_sem.at[i]) for i, (src, mid, dst) in enumerate(moves)]
    flight = 4
    for load in loads[:flight]:
        load.start()
    mean_out[...] = mean_ref[...]
    for i in range(len(moves)):
        loads[i].wait()
        if i + flight < len(moves):
            loads[i + flight].start()
        stores[i].start()
    for store in stores:
        store.wait()


def shards(NY, NZ, activations, cotangent, error_memory, right_factor):
    tokens, width = activations.shape
    kv = cotangent.shape[2]
    error_memory = error_memory[:, 0]
    group = RANK * kv // (8 * 128 * NZ)
    dma = pltpu.SemaphoreType.DMA
    any_spec = pl.BlockSpec(memory_space=pl.ANY)
    new_error, left, mean = pl.pallas_call(
        functools.partial(fused, NY, NZ),
        out_shape=(
            jax.ShapeDtypeStruct((2, width, kv), BF),
            jax.ShapeDtypeStruct((2, RANK, width), F32),
            jax.ShapeDtypeStruct((2, RANK, kv), F32),
        ),
        in_specs=[any_spec] * 4,
        out_specs=(any_spec, any_spec, pl.BlockSpec(memory_space=pltpu.VMEM)),
        scratch_shapes=[
            pltpu.VMEM((NX, tokens, width), BF),
            pltpu.VMEM((2, NX * tokens, kv), BF),
            pltpu.VMEM((2, width, kv), BF),
            pltpu.VMEM((2, RANK, kv), F32),
            pltpu.VMEM((NX, 2 * RANK, tokens), F32),
            pltpu.VMEM((NX, 2 * RANK, tokens), F32),
            pltpu.VMEM((4 * NX * RANK, tokens), BF),
            pltpu.VMEM((2, 2 * RANK, kv), BF),
            pltpu.VMEM((2, NZ, NY, RANK, 128), F32),
            pltpu.VMEM((2, NZ, NY, NX, RANK, 128), F32),
            pltpu.VMEM((NZ, NY, NX, RANK, 128), F32),
            pltpu.VMEM((2, NZ, NX // 2, RANK, 128), F32),
            pltpu.VMEM((2, NZ, NX, RANK, 128), F32),
            pltpu.VMEM((NZ, NX, RANK, 128), F32),
            pltpu.VMEM((NZ - 1, NX, RANK, 128), F32),
            pltpu.VMEM((NX, RANK, 128), F32),
            pltpu.VMEM((NX - 1, 2, RANK, 128), F32),
            pltpu.VMEM((2, NZ, NY, 2, RANK, 128), F32),
            pltpu.VMEM((4 * RANK, width), BF),
            pltpu.VMEM((4 * RANK, width), BF),
            pltpu.VMEM((2 * RANK, tokens), F32),
            pltpu.VMEM((2 * RANK, tokens), F32),
            pltpu.VMEM((2, RANK, width), F32),
            pltpu.VMEM((6 * RANK, width), BF),
            pltpu.VMEM((2, width, kv), F32),
            pltpu.VMEM((2, width, kv), BF),
            pltpu.VMEM((2, NZ, group, 8, 128), F32),
            pltpu.VMEM((2 * NZ - 1, group, 8, 128), F32),
            pltpu.VMEM((group, 8, 128), F32),
            pltpu.VMEM((NY - 1, group, 8, 128), F32),
            pltpu.VMEM((2, NZ, group, 8, 128), F32),
            dma((6,)),
            dma((NX - 1,)), dma((NX - 1,)),
            dma((12,)), dma((12,)),
            dma((NZ,)), dma((NZ,)),
            dma((2, NZ)), dma((2, NZ)),
            dma((2, NZ)), dma((2, NZ)),
            dma((NZ - 1,)), dma((NZ - 1,)),
            dma((NX - 1, 2)), dma((NX - 1, 2)),
            dma((NZ - 1,)), dma((NZ - 1,)),
            dma((2, NZ)), dma((2, NZ)),
            dma((NZ,)), dma((NZ,)),
            dma((NY,)), dma((NY,)),
            dma((1,)), dma((1,)),
            dma((2 * NZ - 1,)), dma((2 * NZ - 1,)),
            dma((NY - 1,)), dma((NY - 1,)),
            dma((2 * NZ - 1,)), dma((2 * NZ - 1,)),
            dma((max(1, width // 512),)),
        ],
        compiler_params=pltpu.CompilerParams(
            collective_id=0, has_side_effects=True, vmem_limit_bytes=56 * 1024 * 1024),
    )(activations, cotangent, error_memory, jnp.swapaxes(right_factor, 1, 2))

    parts = 4
    vmem_spec = pl.BlockSpec(memory_space=pltpu.VMEM)
    new_error, left, mean = pl.pallas_call(
        functools.partial(hand_over, parts),
        out_shape=(
            jax.ShapeDtypeStruct((2, width, kv), BF),
            jax.ShapeDtypeStruct((2, RANK, width), F32),
            jax.ShapeDtypeStruct((2, RANK, kv), F32),
        ),
        in_specs=[any_spec, any_spec, vmem_spec],
        out_specs=(any_spec, any_spec, vmem_spec),
        scratch_shapes=[
            pltpu.VMEM((2, width, kv), BF),
            pltpu.VMEM((2, RANK, width), F32),
            dma((2 * parts + 2,)),
            dma((2 * parts + 2,)),
        ],
        compiler_params=pltpu.CompilerParams(vmem_limit_bytes=56 * 1024 * 1024),
    )(new_error, left, mean)
    return (new_error[:, None], jnp.swapaxes(left, 1, 2)[:, None], jnp.swapaxes(mean, 1, 2))


def build(mesh, NY, NZ):
    return jax.shard_map(
        functools.partial(shards, NY, NZ),
        mesh=mesh,
        in_specs=(
            P(("dp", "tensor"), None),
            P(None, "dp", "tensor"),
            P(None, "dp", None, "tensor"),
            P(None, "tensor", None),
        ),
        out_specs=(
            P(None, "dp", None, "tensor"),
            P(None, "tensor", None, None),
            P(None, "tensor", None),
        ),
        check_vma=False,
    )


def solution(mesh):
    return build(mesh, 4, mesh.shape["dp"] // 8)
```

```python
import functools

import jax
import jax.numpy as jnp
from jax import lax
from jax.experimental import pallas as pl
from jax.experimental.pallas import tpu as pltpu
from jax.sharding import PartitionSpec as P

MESH = pl.DeviceIdType.MESH
BF = jnp.bfloat16
F32 = jnp.float32
NX = 4
RANK = 32
NT = (((1,), (1,)), ((), ()))
TN = (((0,), (0,)), ((), ()))


def split(value):
    high = value.astype(BF)
    return high, (value - high.astype(F32)).astype(BF)


def dot(a, b, dims=None):
    if dims is None:
        dims = (((1,), (0,)), ((), ()))
    return lax.dot_general(a, b, dims, preferred_element_type=F32)


def eliminate(state, first, last):
    wide, pivots = state
    index = lax.broadcasted_iota(jnp.int32, (RANK, 1), 0)
    for j in range(first, last):
        row = wide[j:j + 1, :]
        pivot = wide[j:j + 1, j:j + 1]
        column = wide[:, j:j + 1]
        factor = jnp.where(index > j, column * (1.0 / pivot), 0.0)
        pivots = jnp.where(index == j, pivot, pivots)
        wide = wide - factor * row
    return wide, pivots


def elimination(gram):
    rows = lax.broadcasted_iota(jnp.int32, (RANK, 2 * RANK), 0)
    cols = lax.broadcasted_iota(jnp.int32, (RANK, 2 * RANK), 1)
    eye = jnp.where(cols == rows + RANK, 1.0, 0.0).astype(F32)
    wide = jnp.concatenate([gram, jnp.zeros((RANK, RANK), F32)], axis=1) + eye
    return wide, jnp.ones((RANK, 1), F32)


def inverse_factor(state):
    wide, pivots = state
    return wide[:, RANK:] * (1.0 / jnp.sqrt(pivots))


def fused(NY, NZ, a_hbm, c_hbm, e_hbm, rt_hbm, new_hbm, left_hbm, mean_hbm,
          a, c, e, rt, v, vall, vl, rb, pe, p, rc, fy, ry, q, rz, sp, rx, s, sb, sf, us, uf, left, stack, mem, new, means_f32,
          t, ta, t2, ty, tf,
          lsem, vs, vr, xs, xr, cs, cr, fs, fr, ys, yr, zs, zr, ws, wr, gzs, gzr, gys, gyr, ghs, ghr, gcs, gcr,
          us_sem, ur_sem, tas, tar, tys, tyr, tgs, tgr, out_sem):
    dp, x = lax.axis_index("dp"), lax.axis_index("tensor")
    core, yz = lax.rem(dp, 2), lax.div(dp, 2)
    z, y = lax.rem(yz, NZ), lax.div(yz, NZ)
    other = 1 - core
    tokens = a.shape[1]
    width = a.shape[2]
    kv = c.shape[2]
    span = NY * 128
    ndp = 2 * NY * NZ

    def at_x(k):
        return {"dp": dp, "tensor": lax.rem(x + k, NX)}

    def at_y(k):
        return {"dp": (lax.rem(y + k, NY) * NZ + z) * 2 + core, "tensor": x}

    def at_zc(zz, cc):
        return {"dp": (y * NZ + zz) * 2 + cc, "tensor": x}

    def at_z(zz):
        return at_zc(zz, core)

    partner = at_zc(z, other)
    plane = [(d, k) for d in range(2) for k in range(NZ) if d + k]

    def remote(src, dst, send, recv, device):
        return pltpu.make_async_remote_copy(src_ref=src, dst_ref=dst, send_sem=send, recv_sem=recv,
                                            device_id=device, device_id_type=MESH)

    load_a = pltpu.make_async_copy(a_hbm, a.at[x], lsem.at[0])
    load_c = pltpu.make_async_copy(c_hbm, c, lsem.at[1])
    load_e = pltpu.make_async_copy(e_hbm, e, lsem.at[2])
    load_r = pltpu.make_async_copy(rt_hbm, rt, lsem.at[3])
    load_r.start()
    load_c.start()

    barrier = pltpu.get_barrier_semaphore()
    for k in range(1, NX):
        pl.semaphore_signal(barrier, inc=1, device_id=at_x(k), device_id_type=MESH)
    for k in range(1, NY):
        pl.semaphore_signal(barrier, inc=1, device_id=at_y(k), device_id_type=MESH)
    for d, k in plane:
        pl.semaphore_signal(barrier, inc=1, device_id=at_zc(lax.rem(z + k, NZ), (core, other)[d]), device_id_type=MESH)

    load_r.wait()
    load_c.wait()
    load_a.start()
    load_e.start()
    for m in range(2):
        high, low = split(rt[m])
        rb[m] = jnp.concatenate([high, low], axis=0)
        both = dot(rb[m], c[m], NT)
        vt = both[:RANK] + both[RANK:]
        for b in range(NX):
            v[b, m * RANK:(m + 1) * RANK, :] = vt[:, b * tokens:(b + 1) * tokens]

    pl.semaphore_wait(barrier, NX + NY + 2 * NZ - 3)

    v_copies = []
    for k in range(1, NX):
        copy = remote(v.at[lax.rem(x + k, NX)], vall.at[x], vs.at[k - 1], vr.at[k - 1], at_x(k))
        copy.start()
        v_copies.append(copy)

    quarter = tokens // 4
    left_x, right_x = lax.rem(x + NX - 1, NX), lax.rem(x + 1, NX)
    far_x = lax.rem(x + 2, NX)
    right_dev, left_dev = at_x(1), at_x(NX - 1)

    def quarter_copy(slot, i, sem, device):
        part = a.at[slot, pl.ds(i * quarter, quarter)]
        return remote(part, part, xs.at[sem], xr.at[sem], device)

    def own_quarter(i, sem, device):
        part = pl.ds(i * quarter, quarter)
        return remote(a_hbm.at[part], a.at[x, part], xs.at[sem], xr.at[sem], device)

    to_right = [own_quarter(i, i, right_dev) for i in range(4)]
    to_left = [own_quarter(i, 4 + i, left_dev) for i in (2, 3, 0, 1)]
    forward_right = [quarter_copy(left_x, i, 8 + i, right_dev) for i in range(2)]
    forward_left = [quarter_copy(right_x, 2 + i, 10 + i, left_dev) for i in range(2)]
    for i in range(2):
        to_right[i].start()
        to_left[i].start()

    def left_arrived(parts):
        for i in parts:
            quarter_copy(left_x, i, i, right_dev).wait_recv()

    def right_arrived(parts):
        for i in parts:
            quarter_copy(right_x, i, 4 + i, right_dev).wait_recv()

    def far_arrived():
        for i in range(2):
            quarter_copy(far_x, i, 8 + i, right_dev).wait_recv()
            quarter_copy(far_x, 2 + i, 10 + i, right_dev).wait_recv()

    load_e.wait()
    load_a.wait()

    def error_part(j, carry):
        at = pl.ds(pl.multiple_of(j * span, span), span)
        for m in range(2):
            et = dot(rb[m], e[m, at, :], NT)
            et = et[:RANK] + et[RANK:]
            for yb in range(NY):
                pe[m, j, yb] = et[:, yb * 128:(yb + 1) * 128]
        return carry

    lax.fori_loop(0, NZ, error_part, 0)

    vall[x] = v[x]
    for k in range(1, NX):
        src = lax.rem(x + NX - k, NX)
        remote(v.at[0], vall.at[src], vs.at[k - 1], vr.at[k - 1], at_x(k)).wait_recv()
    stacked = jnp.concatenate(
        [vall[b, m * RANK:(m + 1) * RANK, :] for m in range(2) for b in range(NX)], axis=0)
    high, low = split(stacked)
    block = 2 * NX * RANK
    vl[:block] = high
    vl[block:] = low

    def partials(j):
        zj = lax.rem(z + 1 + j, NZ)
        at = pl.ds(pl.multiple_of(zj * span, span), span)
        both = dot(vl[...], a[x, :, at])
        both = both[:block] + both[block:]
        for m in range(2):
            for yb in range(NY):
                for b in range(NX):
                    r0 = (m * NX + b) * RANK
                    p[m, zj, yb, b] = both[r0:r0 + RANK, yb * 128:(yb + 1) * 128]
        for m in range(2):
            for yb in range(NY):
                p[m, zj, yb, x] = p[m, zj, yb, x] + pe[m, zj, yb]
        remote(p.at[other, zj], rc.at[zj], cs.at[zj], cr.at[zj], partner).start()

    hc = NX // 2
    up, down, far_y = lax.rem(y + 1, NY), lax.rem(y + NY - 1, NY), lax.rem(y + 2, NY)
    to_up, to_down = at_y(1), at_y(NY - 1)

    def over_cores(j):
        zj = lax.rem(z + 1 + j, NZ)
        remote(p.at[other, zj], rc.at[zj], cs.at[zj], cr.at[zj], partner).wait_recv()
        p[core, zj] = p[core, zj] + rc[zj]
        remote(p.at[core, zj, far_y, pl.ds(0, hc)], fy.at[0, zj], fs.at[0, zj], fr.at[0, zj], to_up).start()
        remote(p.at[core, zj, far_y, pl.ds(hc, hc)], fy.at[1, zj], fs.at[1, zj], fr.at[1, zj], to_down).start()

    def staggered(j, carry):
        partials(j)
        over_cores(j - 1)
        return carry

    partials(0)
    lax.fori_loop(1, NZ, staggered, 0)
    over_cores(NZ - 1)

    to_right[2].start()
    to_left[2].start()

    def to_neighbours(j, carry):
        zj = lax.rem(z + 1 + j, NZ)
        for i, target, device in ((0, up, to_up), (1, down, to_down)):
            part = pl.ds(i * hc, hc)
            remote(p.at[core, zj, far_y, part], fy.at[i, zj], fs.at[i, zj], fr.at[i, zj], device).wait_recv()
            p[core, zj, target, part] = p[core, zj, target, part] + fy[i, zj]
            remote(p.at[core, zj, target], ry.at[i, zj], ys.at[i, zj], yr.at[i, zj], device).start()
        return carry

    lax.fori_loop(0, NZ, to_neighbours, 0)

    step = min(512, width)

    def cotangents(parts):
        rows = [pl.ds(pl.multiple_of(slot * tokens + r0, n), n) for slot, r0, n in parts]
        return jnp.concatenate([jnp.concatenate([c[0, r, :], c[1, r, :]], axis=1) for r in rows], axis=0)

    def product(parts, cc, at):
        return dot(jnp.concatenate([a[slot, r0:r0 + n, at] for slot, r0, n in parts], axis=0), cc, TN)

    def accumulate(parts, first=False):
        cc = cotangents(parts)

        def body(i, carry):
            at = pl.ds(pl.multiple_of(i * step, step), step)
            g = product(parts, cc, at)
            for m in range(2):
                base = e[m, at, :].astype(F32) if first else mem[m, at, :]
                mem[m, at, :] = base + g[:, m * kv:(m + 1) * kv]
            return carry

        lax.fori_loop(0, width // step, body, 0)

    half = tokens // 2
    accumulate([(x, 0, tokens)], True)

    def over_y(zj):
        total = p[core, zj, y]
        for i in range(2):
            remote(p.at[core, zj, y], ry.at[i, zj], ys.at[i, zj], yr.at[i, zj], partner).wait_recv()
            total = total + ry[i, zj]
        q[zj] = total

    def over_y_send(j, carry):
        zj = lax.rem(z + 1 + j, NZ)
        over_y(zj)
        remote(q.at[zj], rz.at[j], zs.at[j], zr.at[j], at_z(zj)).start()
        return carry

    lax.fori_loop(0, NZ - 1, over_y_send, 0)
    over_y(z)

    total = q[z]
    for j in range(NZ - 1):
        remote(q.at[z], rz.at[j], zs.at[j], zr.at[j], partner).wait_recv()
        total = total + rz[j]
    sp[...] = total

    def over_x(k, slot):
        return remote(sp.at[lax.rem(x + k + 2 * slot, NX)], rx.at[k - 1, slot], ws.at[k - 1, slot], wr.at[k - 1, slot],
                      at_x(k))

    for k in range(1, NX):
        for slot in range(2):
            over_x(k, slot).start()
    to_right[3].start()
    to_left[3].start()
    for i in range(2):
        left_arrived([i])
        right_arrived([2 + i])
    forward_right[0].start()
    forward_left[0].start()
    accumulate([(left_x, 0, half), (right_x, half, half)])
    for slot in range(2):
        total = sp[lax.rem(x + 2 * slot, NX)]
        for k in range(1, NX):
            over_x(k, slot).wait_recv()
            total = total + rx[k - 1, slot]
        s[core, z, y, slot] = total

    own = s.at[core, z, y]

    def along_z(k):
        return lax.rem(z + NZ - k, NZ)

    def same(piece, send, recv, device):
        return remote(piece, piece, send, recv, device)

    def spread(k):
        piece = s.at[core, along_z(k), y]
        same(piece, gys.at[0, k], gyr.at[0, k], to_up).start()
        same(piece, gys.at[1, k], gyr.at[1, k], to_down).start()

    for k in range(1, NZ):
        same(own, gzs.at[k - 1], gzr.at[k - 1], at_z(lax.rem(z + k, NZ))).start()
    spread(0)

    def from_z(k, carry):
        same(s.at[core, along_z(k), y], gzs.at[k - 1], gzr.at[k - 1], partner).wait_recv()
        spread(k)
        return carry

    lax.fori_loop(1, NZ, from_z, 0)

    def to_partner(r):
        return same(s.at[core, :, lax.rem(y + r, NY)], gcs.at[r], gcr.at[r], partner)

    to_partner(0).start()

    def from_y(first):
        def body(k, carry):
            zz = along_z(k)
            lower, upper = s.at[core, zz, down], s.at[core, zz, up]
            same(lower, gys.at[0, k], gyr.at[0, k], partner).wait_recv()
            same(upper, gys.at[1, k], gyr.at[1, k], partner).wait_recv()
            if first:
                same(lower, ghs.at[k], ghr.at[k], to_up).start()
            else:
                same(upper, ghs.at[k], ghr.at[k], to_down).start()
            return carry
        return body

    lax.fori_loop(0, NZ // 2, from_y(True), 0)
    lax.fori_loop(NZ // 2, NZ, from_y(False), 0)
    to_partner(NY - 1).start()
    to_partner(1).start()

    def from_far(k, carry):
        same(s.at[core, along_z(k), far_y], ghs.at[k], ghr.at[k], partner).wait_recv()
        return carry

    lax.fori_loop(0, NZ, from_far, 0)
    to_partner(2).start()
    left_arrived([2, 3])
    right_arrived([0, 1])
    accumulate([(left_x, half, half), (right_x, 0, half)])
    for r in range(NY):
        same(s.at[other, :, lax.rem(y + r, NY)], gcs.at[r], gcr.at[r], partner).wait_recv()

    def two_terms(dst, slot):
        for m in range(2):
            for zz in range(NZ):
                for yy in range(NY):
                    d0 = (zz * NY + yy) * 128
                    high, low = split(s[m, zz, yy, slot])
                    dst[m * 64:m * 64 + 32, d0:d0 + 128] = high
                    dst[m * 64 + 32:m * 64 + 64, d0:d0 + 128] = low

    two_terms(sf, 1)
    u = dot(sf[...], a[x], NT)
    for m in range(2):
        us[m * RANK:(m + 1) * RANK, :] = u[m * 64:m * 64 + 32] + u[m * 64 + 32:m * 64 + 64]
    to_far = remote(us, uf, us_sem.at[0], ur_sem.at[0], at_x(2))
    to_far.start()
    forward_right[1].start()
    forward_left[1].start()
    two_terms(sb, 0)

    right = []
    for m in range(2):
        both = dot(sb[m * 64:m * 64 + 64, :], e[m])
        right.append(both[:RANK] + both[RANK:])

    def add_right(slot, m, um):
        tok = pl.ds(pl.multiple_of(slot * tokens, tokens), tokens)
        both = dot(jnp.concatenate(split(um), axis=0), c[m, tok, :])
        right[m] = right[m] + both[:RANK] + both[RANK:]

    for slot in (x, left_x, right_x):
        u = dot(sb[...], a[slot], NT)
        for m in range(2):
            add_right(slot, m, u[m * 64:m * 64 + 32] + u[m * 64 + 32:m * 64 + 64])
    states = []
    for m in range(2):
        both = dot(sb[m * 64:m * 64 + 64, :], sb[m * 64:m * 64 + 64, :], NT)
        states.append(elimination(
            both[:RANK, :RANK] + both[:RANK, RANK:] + both[RANK:, :RANK] + both[RANK:, RANK:]))
    to_far.wait_recv()
    for m in range(2):
        add_right(far_x, m, uf[m * RANK:(m + 1) * RANK, :])

    group = t.shape[2]
    per_row = kv // 128

    def piece(i):
        return i // group, i % group

    for m in range(2):
        for i in range(NZ * group):
            rr, kk = i // per_row, i % per_row
            t[(m,) + piece(i)] = right[m][rr * 8:rr * 8 + 8, kk * 128:kk * 128 + 128]
    for i, (d, k) in enumerate(plane):
        zk, ck = lax.rem(z + k, NZ), (core, other)[d]
        remote(t.at[ck, zk], ta.at[i], tas.at[i], tar.at[i], at_zc(zk, ck)).start()
    states = [eliminate(state, 0, 11) for state in states]
    total = t[core, z]
    for i in range(len(plane)):
        remote(t.at[core, z], ta.at[i], tas.at[i], tar.at[i], partner).wait_recv()
        total = total + ta[i]
    t2[...] = total
    for k in range(1, NY):
        remote(t2, ty.at[k - 1], tys.at[k - 1], tyr.at[k - 1], at_y(k)).start()
    states = [eliminate(state, 11, 22) for state in states]
    for k in range(1, NY):
        remote(t2, ty.at[k - 1], tys.at[k - 1], tyr.at[k - 1], partner).wait_recv()
        total = total + ty[k - 1]
    tf[core, z] = total
    own_t = tf.at[core, z]
    for i, (d, k) in enumerate(plane):
        remote(own_t, own_t, tgs.at[i], tgr.at[i], at_zc(lax.rem(z + k, NZ), (core, other)[d])).start()
    inverse = [inverse_factor(eliminate(state, 22, RANK)) for state in states]
    for m in range(2):
        high, low = split(inverse[m])
        pair = jnp.concatenate([high, low], axis=0)
        for i in range(width // step):
            at = pl.ds(i * step, step)
            both = dot(pair, sb[m * 64:m * 64 + 32, at])
            lt = both[:RANK] + both[RANK:] + dot(high, sb[m * 64 + 32:m * 64 + 64, at])
            left[m, :, at] = lt
            lh, ll = split(lt)
            stack[m * 96:m * 96 + 96, at] = jnp.concatenate([lh, ll, lh], axis=0)
    store_left = pltpu.make_async_copy(left, left_hbm, lsem.at[4])
    store_left.start()
    for i, (d, k) in enumerate(plane):
        got = tf.at[(core, other)[d], lax.rem(z + NZ - k, NZ)]
        remote(got, got, tgs.at[i], tgr.at[i], partner).wait_recv()

    means = []
    for m in range(2):
        tt = jnp.concatenate(
            [jnp.concatenate([tf[(m,) + piece(rr * per_row + kk)] for kk in range(per_row)], axis=1)
             for rr in range(RANK // 8)], axis=0)
        wh, wl = split(inverse[m])
        th, tl = split(tt)
        both = dot(jnp.concatenate([wh, wl], axis=0), th)
        mean = (both[:RANK] + both[RANK:] + dot(wh, tl)) * (1.0 / ndp)
        means_f32[m] = mean
        mh, ml = split(mean)
        means.append(jnp.concatenate([mh, mh, ml], axis=0))
    store_mean = pltpu.make_async_copy(means_f32, mean_hbm, lsem.at[5])
    store_mean.start()

    def subtract(i, carry):
        at = pl.ds(pl.multiple_of(i * step, step), step)
        for m in range(2):
            mem[m, at, :] = mem[m, at, :] - dot(stack[m * 96:m * 96 + 96, at], means[m], TN)
        return carry

    lax.fori_loop(0, width // step, subtract, 0)

    far_arrived()
    far_parts = [(far_x, 0, tokens)]
    cc_far = cotangents(far_parts)

    def store_new(i):
        at = pl.ds(pl.multiple_of(i * step, step), step)
        return pltpu.make_async_copy(new.at[:, at], new_hbm.at[:, at], out_sem.at[i])

    def finish(i, carry):
        at = pl.ds(pl.multiple_of(i * step, step), step)
        g = product(far_parts, cc_far, at)
        for m in range(2):
            new[m, at, :] = (mem[m, at, :] + g[:, m * kv:(m + 1) * kv]).astype(BF)
        store_new(i).start()
        return carry

    lax.fori_loop(0, width // step, finish, 0)

    for copy in v_copies + to_right + to_left + forward_right + forward_left:
        copy.wait_send()

    def sent(j, carry):
        remote(p.at[other, j], rc.at[j], cs.at[j], cr.at[j], partner).wait_send()
        for i in range(2):
            remote(fy.at[i, j], fy.at[i, j], fs.at[i, j], fr.at[i, j], partner).wait_send()
            remote(p.at[core, j, y], ry.at[i, j], ys.at[i, j], yr.at[i, j], partner).wait_send()
        return carry

    lax.fori_loop(0, NZ, sent, 0)
    for j in range(NZ - 1):
        remote(q.at[j], rz.at[j], zs.at[j], zr.at[j], partner).wait_send()
        same(own, gzs.at[j], gzr.at[j], partner).wait_send()
    for k in range(1, NX):
        for slot in range(2):
            over_x(k, slot).wait_send()

    def sent_s(k, carry):
        same(own, gys.at[0, k], gyr.at[0, k], partner).wait_send()
        same(own, gys.at[1, k], gyr.at[1, k], partner).wait_send()
        same(own, ghs.at[k], ghr.at[k], partner).wait_send()
        return carry

    lax.fori_loop(0, NZ, sent_s, 0)
    for r in range(NY):
        to_partner(r).wait_send()
    to_far.wait_send()
    for i in range(len(plane)):
        remote(t2, ta.at[i], tas.at[i], tar.at[i], partner).wait_send()
        remote(own_t, own_t, tgs.at[i], tgr.at[i], partner).wait_send()
    for k in range(NY - 1):
        remote(t2, ty.at[k], tys.at[k], tyr.at[k], partner).wait_send()
    store_left.wait()
    store_mean.wait()

    def stored(i, carry):
        store_new(i).wait()
        return carry

    lax.fori_loop(0, width // step, stored, 0)


def hand_over(parts, new_hbm, left_hbm, mean_hbm, new_out, left_out, mean_out, new, left, mean, load_sem, store_sem):
    rows = new_hbm.shape[1] // parts
    at = [(m, pl.ds(i * rows, rows)) for m in range(2) for i in range(parts)]
    moves = [(new_hbm.at[w], new.at[w], new_out.at[w]) for w in at]
    moves += [(left_hbm.at[m], left.at[m], left_out.at[m]) for m in range(2)]
    moves += [(mean_hbm, mean, mean_out)]
    loads = [pltpu.make_async_copy(src, mid, load_sem.at[i]) for i, (src, mid, dst) in enumerate(moves)]
    stores = [pltpu.make_async_copy(mid, dst, store_sem.at[i]) for i, (src, mid, dst) in enumerate(moves)]
    for load in loads:
        load.start()
    for load, store in zip(loads, stores):
        load.wait()
        store.start()
    for store in stores:
        store.wait()


def shards(NY, NZ, activations, cotangent, error_memory, right_factor):
    tokens, width = activations.shape
    kv = cotangent.shape[2]
    error_memory = error_memory[:, 0]
    group = RANK * kv // (8 * 128 * NZ)
    dma = pltpu.SemaphoreType.DMA
    any_spec = pl.BlockSpec(memory_space=pl.ANY)
    new_error, left, mean = pl.pallas_call(
        functools.partial(fused, NY, NZ),
        out_shape=(
            jax.ShapeDtypeStruct((2, width, kv), BF),
            jax.ShapeDtypeStruct((2, RANK, width), F32),
            jax.ShapeDtypeStruct((2, RANK, kv), F32),
        ),
        in_specs=[any_spec] * 4,
        out_specs=(any_spec,) * 3,
        scratch_shapes=[
            pltpu.VMEM((NX, tokens, width), BF),
            pltpu.VMEM((2, NX * tokens, kv), BF),
            pltpu.VMEM((2, width, kv), BF),
            pltpu.VMEM((2, RANK, kv), F32),
            pltpu.VMEM((NX, 2 * RANK, tokens), F32),
            pltpu.VMEM((NX, 2 * RANK, tokens), F32),
            pltpu.VMEM((4 * NX * RANK, tokens), BF),
            pltpu.VMEM((2, 2 * RANK, kv), BF),
            pltpu.VMEM((2, NZ, NY, RANK, 128), F32),
            pltpu.VMEM((2, NZ, NY, NX, RANK, 128), F32),
            pltpu.VMEM((NZ, NY, NX, RANK, 128), F32),
            pltpu.VMEM((2, NZ, NX // 2, RANK, 128), F32),
            pltpu.VMEM((2, NZ, NX, RANK, 128), F32),
            pltpu.VMEM((NZ, NX, RANK, 128), F32),
            pltpu.VMEM((NZ - 1, NX, RANK, 128), F32),
            pltpu.VMEM((NX, RANK, 128), F32),
            pltpu.VMEM((NX - 1, 2, RANK, 128), F32),
            pltpu.VMEM((2, NZ, NY, 2, RANK, 128), F32),
            pltpu.VMEM((4 * RANK, width), BF),
            pltpu.VMEM((4 * RANK, width), BF),
            pltpu.VMEM((2 * RANK, tokens), F32),
            pltpu.VMEM((2 * RANK, tokens), F32),
            pltpu.VMEM((2, RANK, width), F32),
            pltpu.VMEM((6 * RANK, width), BF),
            pltpu.VMEM((2, width, kv), F32),
            pltpu.VMEM((2, width, kv), BF),
            pltpu.VMEM((2, RANK, kv), F32),
            pltpu.VMEM((2, NZ, group, 8, 128), F32),
            pltpu.VMEM((2 * NZ - 1, group, 8, 128), F32),
            pltpu.VMEM((group, 8, 128), F32),
            pltpu.VMEM((NY - 1, group, 8, 128), F32),
            pltpu.VMEM((2, NZ, group, 8, 128), F32),
            dma((6,)),
            dma((NX - 1,)), dma((NX - 1,)),
            dma((12,)), dma((12,)),
            dma((NZ,)), dma((NZ,)),
            dma((2, NZ)), dma((2, NZ)),
            dma((2, NZ)), dma((2, NZ)),
            dma((NZ - 1,)), dma((NZ - 1,)),
            dma((NX - 1, 2)), dma((NX - 1, 2)),
            dma((NZ - 1,)), dma((NZ - 1,)),
            dma((2, NZ)), dma((2, NZ)),
            dma((NZ,)), dma((NZ,)),
            dma((NY,)), dma((NY,)),
            dma((1,)), dma((1,)),
            dma((2 * NZ - 1,)), dma((2 * NZ - 1,)),
            dma((NY - 1,)), dma((NY - 1,)),
            dma((2 * NZ - 1,)), dma((2 * NZ - 1,)),
            dma((max(1, width // 512),)),
        ],
        compiler_params=pltpu.CompilerParams(
            collective_id=0, has_side_effects=True, vmem_limit_bytes=56 * 1024 * 1024),
    )(activations, cotangent, error_memory, jnp.swapaxes(right_factor, 1, 2))

    parts = 4
    new_error, left, mean = pl.pallas_call(
        functools.partial(hand_over, parts),
        out_shape=(
            jax.ShapeDtypeStruct((2, width, kv), BF),
            jax.ShapeDtypeStruct((2, RANK, width), F32),
            jax.ShapeDtypeStruct((2, RANK, kv), F32),
        ),
        in_specs=[any_spec] * 3,
        out_specs=(any_spec,) * 3,
        scratch_shapes=[
            pltpu.VMEM((2, width, kv), BF),
            pltpu.VMEM((2, RANK, width), F32),
            pltpu.VMEM((2, RANK, kv), F32),
            dma((2 * parts + 3,)),
            dma((2 * parts + 3,)),
        ],
        compiler_params=pltpu.CompilerParams(vmem_limit_bytes=56 * 1024 * 1024),
    )(new_error, left, mean)
    return (new_error[:, None], jnp.swapaxes(left, 1, 2)[:, None], jnp.swapaxes(mean, 1, 2))


def build(mesh, NY, NZ):
    return jax.shard_map(
        functools.partial(shards, NY, NZ),
        mesh=mesh,
        in_specs=(
            P(("dp", "tensor"), None),
            P(None, "dp", "tensor"),
            P(None, "dp", None, "tensor"),
            P(None, "tensor", None),
        ),
        out_specs=(
            P(None, "dp", None, "tensor"),
            P(None, "tensor", None, None),
            P(None, "tensor", None),
        ),
        check_vma=False,
    )


def solution(mesh):
    return build(mesh, 4, mesh.shape["dp"] // 8)
```

```python
import functools

import jax
import jax.numpy as jnp
from jax import lax
from jax.experimental import pallas as pl
from jax.experimental.pallas import tpu as pltpu
from jax.sharding import PartitionSpec as P

MESH = pl.DeviceIdType.MESH
BF = jnp.bfloat16
F32 = jnp.float32
NX = 4
RANK = 32
NT = (((1,), (1,)), ((), ()))
TN = (((0,), (0,)), ((), ()))


def split(value):
    high = value.astype(BF)
    return high, (value - high.astype(F32)).astype(BF)


def dot(a, b, dims=None):
    if dims is None:
        dims = (((1,), (0,)), ((), ()))
    return lax.dot_general(a, b, dims, preferred_element_type=F32)


def eliminate(state, first, last):
    wide, pivots = state
    index = lax.broadcasted_iota(jnp.int32, (RANK, 1), 0)
    for j in range(first, last):
        row = wide[j:j + 1, :]
        pivot = wide[j:j + 1, j:j + 1]
        column = wide[:, j:j + 1]
        factor = jnp.where(index > j, column * (1.0 / pivot), 0.0)
        pivots = jnp.where(index == j, pivot, pivots)
        wide = wide - factor * row
    return wide, pivots


def elimination(gram):
    rows = lax.broadcasted_iota(jnp.int32, (RANK, 2 * RANK), 0)
    cols = lax.broadcasted_iota(jnp.int32, (RANK, 2 * RANK), 1)
    eye = jnp.where(cols == rows + RANK, 1.0, 0.0).astype(F32)
    wide = jnp.concatenate([gram, jnp.zeros((RANK, RANK), F32)], axis=1) + eye
    return wide, jnp.ones((RANK, 1), F32)


def inverse_factor(state):
    wide, pivots = state
    return wide[:, RANK:] * (1.0 / jnp.sqrt(pivots))


def fused(NY, NZ, a_hbm, c_hbm, e_hbm, rt_hbm, new_hbm, left_hbm, mean_hbm,
          a, c, e, rt, v, vall, vl, rb, pe, p, rc, fy, ry, q, rz, sp, rx, s, sb, sf, us, uf, left, stack, mem, new, means_f32,
          t, ta, t2, ty, tf,
          lsem, vs, vr, xs, xr, cs, cr, fs, fr, ys, yr, zs, zr, ws, wr, gzs, gzr, gys, gyr, ghs, ghr, gcs, gcr,
          us_sem, ur_sem, tas, tar, tys, tyr, tgs, tgr, out_sem):
    dp, x = lax.axis_index("dp"), lax.axis_index("tensor")
    core, yz = lax.rem(dp, 2), lax.div(dp, 2)
    z, y = lax.rem(yz, NZ), lax.div(yz, NZ)
    other = 1 - core
    tokens = a.shape[1]
    width = a.shape[2]
    kv = c.shape[2]
    span = NY * 128
    ndp = 2 * NY * NZ

    def at_x(k):
        return {"dp": dp, "tensor": lax.rem(x + k, NX)}

    def at_y(k):
        return {"dp": (lax.rem(y + k, NY) * NZ + z) * 2 + core, "tensor": x}

    def at_zc(zz, cc):
        return {"dp": (y * NZ + zz) * 2 + cc, "tensor": x}

    def at_z(zz):
        return at_zc(zz, core)

    partner = at_zc(z, other)
    plane = [(d, k) for d in range(2) for k in range(NZ) if d + k]

    def remote(src, dst, send, recv, device):
        return pltpu.make_async_remote_copy(src_ref=src, dst_ref=dst, send_sem=send, recv_sem=recv,
                                            device_id=device, device_id_type=MESH)

    load_a = pltpu.make_async_copy(a_hbm, a.at[x], lsem.at[0])
    load_c = pltpu.make_async_copy(c_hbm, c, lsem.at[1])
    load_e = pltpu.make_async_copy(e_hbm, e, lsem.at[2])
    load_r = pltpu.make_async_copy(rt_hbm, rt, lsem.at[3])
    load_r.start()
    load_c.start()

    barrier = pltpu.get_barrier_semaphore()
    for k in range(1, NX):
        pl.semaphore_signal(barrier, inc=1, device_id=at_x(k), device_id_type=MESH)
    for k in range(1, NY):
        pl.semaphore_signal(barrier, inc=1, device_id=at_y(k), device_id_type=MESH)
    for d, k in plane:
        pl.semaphore_signal(barrier, inc=1, device_id=at_zc(lax.rem(z + k, NZ), (core, other)[d]), device_id_type=MESH)

    load_r.wait()
    load_c.wait()
    load_a.start()
    load_e.start()
    for m in range(2):
        high, low = split(rt[m])
        rb[m] = jnp.concatenate([high, low], axis=0)
        both = dot(rb[m], c[m], NT)
        vt = both[:RANK] + both[RANK:]
        for b in range(NX):
            v[b, m * RANK:(m + 1) * RANK, :] = vt[:, b * tokens:(b + 1) * tokens]

    pl.semaphore_wait(barrier, NX + NY + 2 * NZ - 3)

    v_copies = []
    for k in range(1, NX):
        copy = remote(v.at[lax.rem(x + k, NX)], vall.at[x], vs.at[k - 1], vr.at[k - 1], at_x(k))
        copy.start()
        v_copies.append(copy)

    quarter = tokens // 4
    left_x, right_x = lax.rem(x + NX - 1, NX), lax.rem(x + 1, NX)
    far_x = lax.rem(x + 2, NX)
    right_dev, left_dev = at_x(1), at_x(NX - 1)

    def quarter_copy(slot, i, sem, device):
        part = a.at[slot, pl.ds(i * quarter, quarter)]
        return remote(part, part, xs.at[sem], xr.at[sem], device)

    def own_quarter(i, sem, device):
        part = pl.ds(i * quarter, quarter)
        return remote(a_hbm.at[part], a.at[x, part], xs.at[sem], xr.at[sem], device)

    to_right = [own_quarter(i, i, right_dev) for i in range(4)]
    to_left = [own_quarter(i, 4 + i, left_dev) for i in (2, 3, 0, 1)]
    forward_right = [quarter_copy(left_x, i, 8 + i, right_dev) for i in range(2)]
    forward_left = [quarter_copy(right_x, 2 + i, 10 + i, left_dev) for i in range(2)]
    for i in range(2):
        to_right[i].start()
        to_left[i].start()

    def left_arrived(parts):
        for i in parts:
            quarter_copy(left_x, i, i, right_dev).wait_recv()

    def right_arrived(parts):
        for i in parts:
            quarter_copy(right_x, i, 4 + i, right_dev).wait_recv()

    def far_arrived():
        for i in range(2):
            quarter_copy(far_x, i, 8 + i, right_dev).wait_recv()
            quarter_copy(far_x, 2 + i, 10 + i, right_dev).wait_recv()

    load_e.wait()
    load_a.wait()

    def error_part(j, carry):
        at = pl.ds(pl.multiple_of(j * span, span), span)
        for m in range(2):
            et = dot(rb[m], e[m, at, :], NT)
            et = et[:RANK] + et[RANK:]
            for yb in range(NY):
                pe[m, j, yb] = et[:, yb * 128:(yb + 1) * 128]
        return carry

    lax.fori_loop(0, NZ, error_part, 0)

    vall[x] = v[x]
    for k in range(1, NX):
        src = lax.rem(x + NX - k, NX)
        remote(v.at[0], vall.at[src], vs.at[k - 1], vr.at[k - 1], at_x(k)).wait_recv()
    stacked = jnp.concatenate(
        [vall[b, m * RANK:(m + 1) * RANK, :] for m in range(2) for b in range(NX)], axis=0)
    high, low = split(stacked)
    block = 2 * NX * RANK
    vl[:block] = high
    vl[block:] = low

    def partials(j):
        zj = lax.rem(z + 1 + j, NZ)
        at = pl.ds(pl.multiple_of(zj * span, span), span)
        both = dot(vl[...], a[x, :, at])
        both = both[:block] + both[block:]
        for m in range(2):
            for yb in range(NY):
                for b in range(NX):
                    r0 = (m * NX + b) * RANK
                    p[m, zj, yb, b] = both[r0:r0 + RANK, yb * 128:(yb + 1) * 128]
        for m in range(2):
            for yb in range(NY):
                p[m, zj, yb, x] = p[m, zj, yb, x] + pe[m, zj, yb]
        remote(p.at[other, zj], rc.at[zj], cs.at[zj], cr.at[zj], partner).start()

    hc = NX // 2
    up, down, far_y = lax.rem(y + 1, NY), lax.rem(y + NY - 1, NY), lax.rem(y + 2, NY)
    to_up, to_down = at_y(1), at_y(NY - 1)

    def over_cores(j):
        zj = lax.rem(z + 1 + j, NZ)
        remote(p.at[other, zj], rc.at[zj], cs.at[zj], cr.at[zj], partner).wait_recv()
        p[core, zj] = p[core, zj] + rc[zj]
        remote(p.at[core, zj, far_y, pl.ds(0, hc)], fy.at[0, zj], fs.at[0, zj], fr.at[0, zj], to_up).start()
        remote(p.at[core, zj, far_y, pl.ds(hc, hc)], fy.at[1, zj], fs.at[1, zj], fr.at[1, zj], to_down).start()

    def staggered(j, carry):
        partials(j)
        over_cores(j - 1)
        return carry

    partials(0)
    lax.fori_loop(1, NZ, staggered, 0)
    over_cores(NZ - 1)

    to_right[2].start()
    to_left[2].start()

    def to_neighbours(j, carry):
        zj = lax.rem(z + 1 + j, NZ)
        for i, target, device in ((0, up, to_up), (1, down, to_down)):
            part = pl.ds(i * hc, hc)
            remote(p.at[core, zj, far_y, part], fy.at[i, zj], fs.at[i, zj], fr.at[i, zj], device).wait_recv()
            p[core, zj, target, part] = p[core, zj, target, part] + fy[i, zj]
            remote(p.at[core, zj, target], ry.at[i, zj], ys.at[i, zj], yr.at[i, zj], device).start()
        return carry

    lax.fori_loop(0, NZ, to_neighbours, 0)

    step = min(512, width)

    def cotangents(parts):
        rows = [pl.ds(pl.multiple_of(slot * tokens + r0, n), n) for slot, r0, n in parts]
        return jnp.concatenate([jnp.concatenate([c[0, r, :], c[1, r, :]], axis=1) for r in rows], axis=0)

    def product(parts, cc, at):
        return dot(jnp.concatenate([a[slot, r0:r0 + n, at] for slot, r0, n in parts], axis=0), cc, TN)

    def accumulate(parts, first=False):
        cc = cotangents(parts)

        def body(i, carry):
            at = pl.ds(pl.multiple_of(i * step, step), step)
            g = product(parts, cc, at)
            for m in range(2):
                base = e[m, at, :].astype(F32) if first else mem[m, at, :]
                mem[m, at, :] = base + g[:, m * kv:(m + 1) * kv]
            return carry

        lax.fori_loop(0, width // step, body, 0)

    half = tokens // 2
    accumulate([(x, 0, tokens)], True)

    def over_y(zj):
        total = p[core, zj, y]
        for i in range(2):
            remote(p.at[core, zj, y], ry.at[i, zj], ys.at[i, zj], yr.at[i, zj], partner).wait_recv()
            total = total + ry[i, zj]
        q[zj] = total

    def over_y_send(j, carry):
        zj = lax.rem(z + 1 + j, NZ)
        over_y(zj)
        remote(q.at[zj], rz.at[j], zs.at[j], zr.at[j], at_z(zj)).start()
        return carry

    lax.fori_loop(0, NZ - 1, over_y_send, 0)
    over_y(z)

    total = q[z]
    for j in range(NZ - 1):
        remote(q.at[z], rz.at[j], zs.at[j], zr.at[j], partner).wait_recv()
        total = total + rz[j]
    sp[...] = total

    def over_x(k, slot):
        return remote(sp.at[lax.rem(x + k + 2 * slot, NX)], rx.at[k - 1, slot], ws.at[k - 1, slot], wr.at[k - 1, slot],
                      at_x(k))

    for k in range(1, NX):
        for slot in range(2):
            over_x(k, slot).start()
    to_right[3].start()
    to_left[3].start()
    for i in range(2):
        left_arrived([i])
        right_arrived([2 + i])
    forward_right[0].start()
    forward_left[0].start()
    accumulate([(left_x, 0, half), (right_x, half, half)])
    for slot in range(2):
        total = sp[lax.rem(x + 2 * slot, NX)]
        for k in range(1, NX):
            over_x(k, slot).wait_recv()
            total = total + rx[k - 1, slot]
        s[core, z, y, slot] = total

    own = s.at[core, z, y]

    def along_z(k):
        return lax.rem(z + NZ - k, NZ)

    def same(piece, send, recv, device):
        return remote(piece, piece, send, recv, device)

    def spread(k):
        piece = s.at[core, along_z(k), y]
        same(piece, gys.at[0, k], gyr.at[0, k], to_up).start()
        same(piece, gys.at[1, k], gyr.at[1, k], to_down).start()

    for k in range(1, NZ):
        same(own, gzs.at[k - 1], gzr.at[k - 1], at_z(lax.rem(z + k, NZ))).start()
    spread(0)

    def from_z(k, carry):
        same(s.at[core, along_z(k), y], gzs.at[k - 1], gzr.at[k - 1], partner).wait_recv()
        spread(k)
        return carry

    lax.fori_loop(1, NZ, from_z, 0)

    def to_partner(r):
        return same(s.at[core, :, lax.rem(y + r, NY)], gcs.at[r], gcr.at[r], partner)

    to_partner(0).start()

    def from_y(first):
        def body(k, carry):
            zz = along_z(k)
            lower, upper = s.at[core, zz, down], s.at[core, zz, up]
            same(lower, gys.at[0, k], gyr.at[0, k], partner).wait_recv()
            same(upper, gys.at[1, k], gyr.at[1, k], partner).wait_recv()
            if first:
                same(lower, ghs.at[k], ghr.at[k], to_up).start()
            else:
                same(upper, ghs.at[k], ghr.at[k], to_down).start()
            return carry
        return body

    lax.fori_loop(0, NZ // 2, from_y(True), 0)
    lax.fori_loop(NZ // 2, NZ, from_y(False), 0)
    to_partner(NY - 1).start()
    to_partner(1).start()

    def from_far(k, carry):
        same(s.at[core, along_z(k), far_y], ghs.at[k], ghr.at[k], partner).wait_recv()
        return carry

    lax.fori_loop(0, NZ, from_far, 0)
    to_partner(2).start()
    left_arrived([2, 3])
    right_arrived([0, 1])
    accumulate([(left_x, half, half), (right_x, 0, half)])
    for r in range(NY):
        same(s.at[other, :, lax.rem(y + r, NY)], gcs.at[r], gcr.at[r], partner).wait_recv()

    def two_terms(dst, slot):
        for m in range(2):
            for zz in range(NZ):
                for yy in range(NY):
                    d0 = (zz * NY + yy) * 128
                    high, low = split(s[m, zz, yy, slot])
                    dst[m * 64:m * 64 + 32, d0:d0 + 128] = high
                    dst[m * 64 + 32:m * 64 + 64, d0:d0 + 128] = low

    two_terms(sf, 1)
    u = dot(sf[...], a[x], NT)
    for m in range(2):
        us[m * RANK:(m + 1) * RANK, :] = u[m * 64:m * 64 + 32] + u[m * 64 + 32:m * 64 + 64]
    to_far = remote(us, uf, us_sem.at[0], ur_sem.at[0], at_x(2))
    to_far.start()
    forward_right[1].start()
    forward_left[1].start()
    two_terms(sb, 0)

    right = []
    for m in range(2):
        both = dot(sb[m * 64:m * 64 + 64, :], e[m])
        right.append(both[:RANK] + both[RANK:])

    def add_right(slot, m, um):
        tok = pl.ds(pl.multiple_of(slot * tokens, tokens), tokens)
        both = dot(jnp.concatenate(split(um), axis=0), c[m, tok, :])
        right[m] = right[m] + both[:RANK] + both[RANK:]

    for slot in (x, left_x, right_x):
        u = dot(sb[...], a[slot], NT)
        for m in range(2):
            add_right(slot, m, u[m * 64:m * 64 + 32] + u[m * 64 + 32:m * 64 + 64])
    states = []
    for m in range(2):
        both = dot(sb[m * 64:m * 64 + 64, :], sb[m * 64:m * 64 + 64, :], NT)
        states.append(elimination(
            both[:RANK, :RANK] + both[:RANK, RANK:] + both[RANK:, :RANK] + both[RANK:, RANK:]))
    to_far.wait_recv()
    for m in range(2):
        add_right(far_x, m, uf[m * RANK:(m + 1) * RANK, :])

    group = t.shape[2]
    per_row = kv // 128

    def piece(i):
        return i // group, i % group

    for m in range(2):
        for i in range(NZ * group):
            rr, kk = i // per_row, i % per_row
            t[(m,) + piece(i)] = right[m][rr * 8:rr * 8 + 8, kk * 128:kk * 128 + 128]
    for i, (d, k) in enumerate(plane):
        zk, ck = lax.rem(z + k, NZ), (core, other)[d]
        remote(t.at[ck, zk], ta.at[i], tas.at[i], tar.at[i], at_zc(zk, ck)).start()
    states = [eliminate(state, 0, 11) for state in states]
    total = t[core, z]
    for i in range(len(plane)):
        remote(t.at[core, z], ta.at[i], tas.at[i], tar.at[i], partner).wait_recv()
        total = total + ta[i]
    t2[...] = total
    for k in range(1, NY):
        remote(t2, ty.at[k - 1], tys.at[k - 1], tyr.at[k - 1], at_y(k)).start()
    states = [eliminate(state, 11, 22) for state in states]
    for k in range(1, NY):
        remote(t2, ty.at[k - 1], tys.at[k - 1], tyr.at[k - 1], partner).wait_recv()
        total = total + ty[k - 1]
    tf[core, z] = total
    own_t = tf.at[core, z]
    for i, (d, k) in enumerate(plane):
        remote(own_t, own_t, tgs.at[i], tgr.at[i], at_zc(lax.rem(z + k, NZ), (core, other)[d])).start()
    inverse = [inverse_factor(eliminate(state, 22, RANK)) for state in states]
    for m in range(2):
        high, low = split(inverse[m])
        pair = jnp.concatenate([high, low], axis=0)
        for i in range(width // step):
            at = pl.ds(i * step, step)
            both = dot(pair, sb[m * 64:m * 64 + 32, at])
            lt = both[:RANK] + both[RANK:] + dot(high, sb[m * 64 + 32:m * 64 + 64, at])
            left[m, :, at] = lt
            lh, ll = split(lt)
            stack[m * 96:m * 96 + 96, at] = jnp.concatenate([lh, ll, lh], axis=0)
    store_left = pltpu.make_async_copy(left, left_hbm, lsem.at[4])
    store_left.start()
    far_arrived()
    accumulate([(far_x, 0, tokens)])
    for i, (d, k) in enumerate(plane):
        got = tf.at[(core, other)[d], lax.rem(z + NZ - k, NZ)]
        remote(got, got, tgs.at[i], tgr.at[i], partner).wait_recv()

    means = []
    for m in range(2):
        tt = jnp.concatenate(
            [jnp.concatenate([tf[(m,) + piece(rr * per_row + kk)] for kk in range(per_row)], axis=1)
             for rr in range(RANK // 8)], axis=0)
        wh, wl = split(inverse[m])
        th, tl = split(tt)
        both = dot(jnp.concatenate([wh, wl], axis=0), th)
        mean = (both[:RANK] + both[RANK:] + dot(wh, tl)) * (1.0 / ndp)
        means_f32[m] = mean
        mh, ml = split(mean)
        means.append(jnp.concatenate([mh, mh, ml], axis=0))
    store_mean = pltpu.make_async_copy(means_f32, mean_hbm, lsem.at[5])
    store_mean.start()

    def store_new(i):
        at = pl.ds(pl.multiple_of(i * step, step), step)
        return pltpu.make_async_copy(new.at[:, at], new_hbm.at[:, at], out_sem.at[i])

    def finish(i, carry):
        at = pl.ds(pl.multiple_of(i * step, step), step)
        for m in range(2):
            approx = dot(stack[m * 96:m * 96 + 96, at], means[m], TN)
            new[m, at, :] = (mem[m, at, :] - approx).astype(BF)
        store_new(i).start()
        return carry

    lax.fori_loop(0, width // step, finish, 0)

    for copy in v_copies + to_right + to_left + forward_right + forward_left:
        copy.wait_send()

    def sent(j, carry):
        remote(p.at[other, j], rc.at[j], cs.at[j], cr.at[j], partner).wait_send()
        for i in range(2):
            remote(fy.at[i, j], fy.at[i, j], fs.at[i, j], fr.at[i, j], partner).wait_send()
            remote(p.at[core, j, y], ry.at[i, j], ys.at[i, j], yr.at[i, j], partner).wait_send()
        return carry

    lax.fori_loop(0, NZ, sent, 0)
    for j in range(NZ - 1):
        remote(q.at[j], rz.at[j], zs.at[j], zr.at[j], partner).wait_send()
        same(own, gzs.at[j], gzr.at[j], partner).wait_send()
    for k in range(1, NX):
        for slot in range(2):
            over_x(k, slot).wait_send()

    def sent_s(k, carry):
        same(own, gys.at[0, k], gyr.at[0, k], partner).wait_send()
        same(own, gys.at[1, k], gyr.at[1, k], partner).wait_send()
        same(own, ghs.at[k], ghr.at[k], partner).wait_send()
        return carry

    lax.fori_loop(0, NZ, sent_s, 0)
    for r in range(NY):
        to_partner(r).wait_send()
    to_far.wait_send()
    for i in range(len(plane)):
        remote(t2, ta.at[i], tas.at[i], tar.at[i], partner).wait_send()
        remote(own_t, own_t, tgs.at[i], tgr.at[i], partner).wait_send()
    for k in range(NY - 1):
        remote(t2, ty.at[k], tys.at[k], tyr.at[k], partner).wait_send()
    store_left.wait()
    store_mean.wait()

    def stored(i, carry):
        store_new(i).wait()
        return carry

    lax.fori_loop(0, width // step, stored, 0)


def hand_over(parts, new_hbm, left_hbm, mean_hbm, new_out, left_out, mean_out, new, left, mean, load_sem, store_sem):
    rows = new_hbm.shape[1] // parts
    at = [(m, pl.ds(i * rows, rows)) for m in range(2) for i in range(parts)]
    moves = [(new_hbm.at[w], new.at[w], new_out.at[w]) for w in at]
    moves += [(left_hbm.at[m], left.at[m], left_out.at[m]) for m in range(2)]
    moves += [(mean_hbm, mean, mean_out)]
    loads = [pltpu.make_async_copy(src, mid, load_sem.at[i]) for i, (src, mid, dst) in enumerate(moves)]
    stores = [pltpu.make_async_copy(mid, dst, store_sem.at[i]) for i, (src, mid, dst) in enumerate(moves)]
    for load in loads:
        load.start()
    for load, store in zip(loads, stores):
        load.wait()
        store.start()
    for store in stores:
        store.wait()


def shards(NY, NZ, activations, cotangent, error_memory, right_factor):
    tokens, width = activations.shape
    kv = cotangent.shape[2]
    error_memory = error_memory[:, 0]
    group = RANK * kv // (8 * 128 * NZ)
    dma = pltpu.SemaphoreType.DMA
    any_spec = pl.BlockSpec(memory_space=pl.ANY)
    new_error, left, mean = pl.pallas_call(
        functools.partial(fused, NY, NZ),
        out_shape=(
            jax.ShapeDtypeStruct((2, width, kv), BF),
            jax.ShapeDtypeStruct((2, RANK, width), F32),
            jax.ShapeDtypeStruct((2, RANK, kv), F32),
        ),
        in_specs=[any_spec] * 4,
        out_specs=(any_spec,) * 3,
        scratch_shapes=[
            pltpu.VMEM((NX, tokens, width), BF),
            pltpu.VMEM((2, NX * tokens, kv), BF),
            pltpu.VMEM((2, width, kv), BF),
            pltpu.VMEM((2, RANK, kv), F32),
            pltpu.VMEM((NX, 2 * RANK, tokens), F32),
            pltpu.VMEM((NX, 2 * RANK, tokens), F32),
            pltpu.VMEM((4 * NX * RANK, tokens), BF),
            pltpu.VMEM((2, 2 * RANK, kv), BF),
            pltpu.VMEM((2, NZ, NY, RANK, 128), F32),
            pltpu.VMEM((2, NZ, NY, NX, RANK, 128), F32),
            pltpu.VMEM((NZ, NY, NX, RANK, 128), F32),
            pltpu.VMEM((2, NZ, NX // 2, RANK, 128), F32),
            pltpu.VMEM((2, NZ, NX, RANK, 128), F32),
            pltpu.VMEM((NZ, NX, RANK, 128), F32),
            pltpu.VMEM((NZ - 1, NX, RANK, 128), F32),
            pltpu.VMEM((NX, RANK, 128), F32),
            pltpu.VMEM((NX - 1, 2, RANK, 128), F32),
            pltpu.VMEM((2, NZ, NY, 2, RANK, 128), F32),
            pltpu.VMEM((4 * RANK, width), BF),
            pltpu.VMEM((4 * RANK, width), BF),
            pltpu.VMEM((2 * RANK, tokens), F32),
            pltpu.VMEM((2 * RANK, tokens), F32),
            pltpu.VMEM((2, RANK, width), F32),
            pltpu.VMEM((6 * RANK, width), BF),
            pltpu.VMEM((2, width, kv), F32),
            pltpu.VMEM((2, width, kv), BF),
            pltpu.VMEM((2, RANK, kv), F32),
            pltpu.VMEM((2, NZ, group, 8, 128), F32),
            pltpu.VMEM((2 * NZ - 1, group, 8, 128), F32),
            pltpu.VMEM((group, 8, 128), F32),
            pltpu.VMEM((NY - 1, group, 8, 128), F32),
            pltpu.VMEM((2, NZ, group, 8, 128), F32),
            dma((6,)),
            dma((NX - 1,)), dma((NX - 1,)),
            dma((12,)), dma((12,)),
            dma((NZ,)), dma((NZ,)),
            dma((2, NZ)), dma((2, NZ)),
            dma((2, NZ)), dma((2, NZ)),
            dma((NZ - 1,)), dma((NZ - 1,)),
            dma((NX - 1, 2)), dma((NX - 1, 2)),
            dma((NZ - 1,)), dma((NZ - 1,)),
            dma((2, NZ)), dma((2, NZ)),
            dma((NZ,)), dma((NZ,)),
            dma((NY,)), dma((NY,)),
            dma((1,)), dma((1,)),
            dma((2 * NZ - 1,)), dma((2 * NZ - 1,)),
            dma((NY - 1,)), dma((NY - 1,)),
            dma((2 * NZ - 1,)), dma((2 * NZ - 1,)),
            dma((max(1, width // 512),)),
        ],
        compiler_params=pltpu.CompilerParams(
            collective_id=0, has_side_effects=True, vmem_limit_bytes=56 * 1024 * 1024),
    )(activations, cotangent, error_memory, jnp.swapaxes(right_factor, 1, 2))

    parts = 4
    new_error, left, mean = pl.pallas_call(
        functools.partial(hand_over, parts),
        out_shape=(
            jax.ShapeDtypeStruct((2, width, kv), BF),
            jax.ShapeDtypeStruct((2, RANK, width), F32),
            jax.ShapeDtypeStruct((2, RANK, kv), F32),
        ),
        in_specs=[any_spec] * 3,
        out_specs=(any_spec,) * 3,
        scratch_shapes=[
            pltpu.VMEM((2, width, kv), BF),
            pltpu.VMEM((2, RANK, width), F32),
            pltpu.VMEM((2, RANK, kv), F32),
            dma((2 * parts + 3,)),
            dma((2 * parts + 3,)),
        ],
        compiler_params=pltpu.CompilerParams(vmem_limit_bytes=56 * 1024 * 1024),
    )(new_error, left, mean)
    return (new_error[:, None], jnp.swapaxes(left, 1, 2)[:, None], jnp.swapaxes(mean, 1, 2))


def build(mesh, NY, NZ):
    return jax.shard_map(
        functools.partial(shards, NY, NZ),
        mesh=mesh,
        in_specs=(
            P(("dp", "tensor"), None),
            P(None, "dp", "tensor"),
            P(None, "dp", None, "tensor"),
            P(None, "tensor", None),
        ),
        out_specs=(
            P(None, "dp", None, "tensor"),
            P(None, "tensor", None, None),
            P(None, "tensor", None),
        ),
        check_vma=False,
    )


def solution(mesh):
    return build(mesh, 4, mesh.shape["dp"] // 8)
```

```python
import functools

import jax
import jax.numpy as jnp
from jax import lax
from jax.experimental import pallas as pl
from jax.experimental.pallas import tpu as pltpu
from jax.sharding import PartitionSpec as P

MESH = pl.DeviceIdType.MESH
BF = jnp.bfloat16
F32 = jnp.float32
NX = 4
RANK = 32
NT = (((1,), (1,)), ((), ()))
TN = (((0,), (0,)), ((), ()))


def split(value):
    high = value.astype(BF)
    return high, (value - high.astype(F32)).astype(BF)


def dot(a, b, dims=None):
    if dims is None:
        dims = (((1,), (0,)), ((), ()))
    return lax.dot_general(a, b, dims, preferred_element_type=F32)


def eliminate(state, first, last):
    wide, pivots = state
    index = lax.broadcasted_iota(jnp.int32, (RANK, 1), 0)
    for j in range(first, last):
        row = wide[j:j + 1, :]
        pivot = wide[j:j + 1, j:j + 1]
        column = wide[:, j:j + 1]
        factor = jnp.where(index > j, column * (1.0 / pivot), 0.0)
        pivots = jnp.where(index == j, pivot, pivots)
        wide = wide - factor * row
    return wide, pivots


def elimination(gram):
    rows = lax.broadcasted_iota(jnp.int32, (RANK, 2 * RANK), 0)
    cols = lax.broadcasted_iota(jnp.int32, (RANK, 2 * RANK), 1)
    eye = jnp.where(cols == rows + RANK, 1.0, 0.0).astype(F32)
    wide = jnp.concatenate([gram, jnp.zeros((RANK, RANK), F32)], axis=1) + eye
    return wide, jnp.ones((RANK, 1), F32)


def inverse_factor(state):
    wide, pivots = state
    return wide[:, RANK:] * (1.0 / jnp.sqrt(pivots))


def fused(NY, NZ, a_hbm, c_hbm, e_hbm, rt_hbm, new_hbm, left_hbm, mean_hbm,
          a, c, e, rt, v, vall, vl, rb, pe, p, rc, fy, ry, q, rz, sp, rx, s, sb, sf, us, uf, left, stack, mem, new, means_f32,
          t, ta, t2, ty, tf,
          lsem, vs, vr, xs, xr, cs, cr, fs, fr, ys, yr, zs, zr, ws, wr, gzs, gzr, gys, gyr, ghs, ghr, gcs, gcr,
          us_sem, ur_sem, tas, tar, tys, tyr, tgs, tgr, out_sem):
    dp, x = lax.axis_index("dp"), lax.axis_index("tensor")
    core, yz = lax.rem(dp, 2), lax.div(dp, 2)
    z, y = lax.rem(yz, NZ), lax.div(yz, NZ)
    other = 1 - core
    tokens = a.shape[1]
    width = a.shape[2]
    kv = c.shape[2]
    span = NY * 128
    ndp = 2 * NY * NZ

    def at_x(k):
        return {"dp": dp, "tensor": lax.rem(x + k, NX)}

    def at_y(k):
        return {"dp": (lax.rem(y + k, NY) * NZ + z) * 2 + core, "tensor": x}

    def at_zc(zz, cc):
        return {"dp": (y * NZ + zz) * 2 + cc, "tensor": x}

    def at_z(zz):
        return at_zc(zz, core)

    partner = at_zc(z, other)
    plane = [(d, k) for d in range(2) for k in range(NZ) if d + k]

    def remote(src, dst, send, recv, device):
        return pltpu.make_async_remote_copy(src_ref=src, dst_ref=dst, send_sem=send, recv_sem=recv,
                                            device_id=device, device_id_type=MESH)

    load_a = pltpu.make_async_copy(a_hbm, a.at[x], lsem.at[0])
    load_c = pltpu.make_async_copy(c_hbm, c, lsem.at[1])
    load_e = pltpu.make_async_copy(e_hbm, e, lsem.at[2])
    load_r = pltpu.make_async_copy(rt_hbm, rt, lsem.at[3])
    load_r.start()
    load_c.start()

    barrier = pltpu.get_barrier_semaphore()
    for k in range(1, NX):
        pl.semaphore_signal(barrier, inc=1, device_id=at_x(k), device_id_type=MESH)
    for k in range(1, NY):
        pl.semaphore_signal(barrier, inc=1, device_id=at_y(k), device_id_type=MESH)
    for d, k in plane:
        pl.semaphore_signal(barrier, inc=1, device_id=at_zc(lax.rem(z + k, NZ), (core, other)[d]), device_id_type=MESH)

    load_r.wait()
    load_c.wait()
    load_a.start()
    load_e.start()
    for m in range(2):
        high, low = split(rt[m])
        rb[m] = jnp.concatenate([high, low], axis=0)
        both = dot(rb[m], c[m], NT)
        vt = both[:RANK] + both[RANK:]
        for b in range(NX):
            v[b, m * RANK:(m + 1) * RANK, :] = vt[:, b * tokens:(b + 1) * tokens]

    pl.semaphore_wait(barrier, NX + NY + 2 * NZ - 3)

    v_copies = []
    for k in range(1, NX):
        copy = remote(v.at[lax.rem(x + k, NX)], vall.at[x], vs.at[k - 1], vr.at[k - 1], at_x(k))
        copy.start()
        v_copies.append(copy)

    quarter = tokens // 4
    left_x, right_x = lax.rem(x + NX - 1, NX), lax.rem(x + 1, NX)
    far_x = lax.rem(x + 2, NX)
    right_dev, left_dev = at_x(1), at_x(NX - 1)

    def quarter_copy(slot, i, sem, device):
        part = a.at[slot, pl.ds(i * quarter, quarter)]
        return remote(part, part, xs.at[sem], xr.at[sem], device)

    def own_quarter(i, sem, device):
        part = pl.ds(i * quarter, quarter)
        return remote(a_hbm.at[part], a.at[x, part], xs.at[sem], xr.at[sem], device)

    to_right = [own_quarter(i, i, right_dev) for i in range(4)]
    to_left = [own_quarter(i, 4 + i, left_dev) for i in (2, 3, 0, 1)]
    forward_right = [quarter_copy(left_x, i, 8 + i, right_dev) for i in range(2)]
    forward_left = [quarter_copy(right_x, 2 + i, 10 + i, left_dev) for i in range(2)]
    for i in range(2):
        to_right[i].start()
        to_left[i].start()

    def left_arrived(parts):
        for i in parts:
            quarter_copy(left_x, i, i, right_dev).wait_recv()

    def right_arrived(parts):
        for i in parts:
            quarter_copy(right_x, i, 4 + i, right_dev).wait_recv()

    def far_arrived():
        for i in range(2):
            quarter_copy(far_x, i, 8 + i, right_dev).wait_recv()
            quarter_copy(far_x, 2 + i, 10 + i, right_dev).wait_recv()

    load_e.wait()
    load_a.wait()

    def error_part(j, carry):
        at = pl.ds(pl.multiple_of(j * span, span), span)
        for m in range(2):
            et = dot(rb[m], e[m, at, :], NT)
            et = et[:RANK] + et[RANK:]
            for yb in range(NY):
                pe[m, j, yb] = et[:, yb * 128:(yb + 1) * 128]
        return carry

    lax.fori_loop(0, NZ, error_part, 0)

    vall[x] = v[x]
    for k in range(1, NX):
        src = lax.rem(x + NX - k, NX)
        remote(v.at[0], vall.at[src], vs.at[k - 1], vr.at[k - 1], at_x(k)).wait_recv()
    stacked = jnp.concatenate(
        [vall[b, m * RANK:(m + 1) * RANK, :] for m in range(2) for b in range(NX)], axis=0)
    high, low = split(stacked)
    block = 2 * NX * RANK
    vl[:block] = high
    vl[block:] = low

    def partials(j):
        zj = lax.rem(z + 1 + j, NZ)
        at = pl.ds(pl.multiple_of(zj * span, span), span)
        both = dot(vl[...], a[x, :, at])
        both = both[:block] + both[block:]
        for m in range(2):
            for yb in range(NY):
                for b in range(NX):
                    r0 = (m * NX + b) * RANK
                    p[m, zj, yb, b] = both[r0:r0 + RANK, yb * 128:(yb + 1) * 128]
        for m in range(2):
            for yb in range(NY):
                p[m, zj, yb, x] = p[m, zj, yb, x] + pe[m, zj, yb]
        remote(p.at[other, zj], rc.at[zj], cs.at[zj], cr.at[zj], partner).start()

    hc = NX // 2
    up, down, far_y = lax.rem(y + 1, NY), lax.rem(y + NY - 1, NY), lax.rem(y + 2, NY)
    to_up, to_down = at_y(1), at_y(NY - 1)

    def over_cores(j):
        zj = lax.rem(z + 1 + j, NZ)
        remote(p.at[other, zj], rc.at[zj], cs.at[zj], cr.at[zj], partner).wait_recv()
        p[core, zj] = p[core, zj] + rc[zj]
        remote(p.at[core, zj, far_y, pl.ds(0, hc)], fy.at[0, zj], fs.at[0, zj], fr.at[0, zj], to_up).start()
        remote(p.at[core, zj, far_y, pl.ds(hc, hc)], fy.at[1, zj], fs.at[1, zj], fr.at[1, zj], to_down).start()

    def staggered(j, carry):
        partials(j)
        over_cores(j - 1)
        return carry

    partials(0)
    lax.fori_loop(1, NZ, staggered, 0)
    over_cores(NZ - 1)

    to_right[2].start()
    to_left[2].start()

    def to_neighbours(j, carry):
        zj = lax.rem(z + 1 + j, NZ)
        for i, target, device in ((0, up, to_up), (1, down, to_down)):
            part = pl.ds(i * hc, hc)
            remote(p.at[core, zj, far_y, part], fy.at[i, zj], fs.at[i, zj], fr.at[i, zj], device).wait_recv()
            p[core, zj, target, part] = p[core, zj, target, part] + fy[i, zj]
            remote(p.at[core, zj, target], ry.at[i, zj], ys.at[i, zj], yr.at[i, zj], device).start()
        return carry

    lax.fori_loop(0, NZ, to_neighbours, 0)

    step = min(512, width)

    def cotangents(parts):
        rows = [pl.ds(pl.multiple_of(slot * tokens + r0, n), n) for slot, r0, n in parts]
        return jnp.concatenate([jnp.concatenate([c[0, r, :], c[1, r, :]], axis=1) for r in rows], axis=0)

    def product(parts, cc, at):
        return dot(jnp.concatenate([a[slot, r0:r0 + n, at] for slot, r0, n in parts], axis=0), cc, TN)

    def accumulate(parts, first=False):
        cc = cotangents(parts)

        def body(i, carry):
            at = pl.ds(pl.multiple_of(i * step, step), step)
            g = product(parts, cc, at)
            for m in range(2):
                base = e[m, at, :].astype(F32) if first else mem[m, at, :]
                mem[m, at, :] = base + g[:, m * kv:(m + 1) * kv]
            return carry

        lax.fori_loop(0, width // step, body, 0)

    half = tokens // 2
    accumulate([(x, 0, tokens)], True)

    def over_y(zj):
        total = p[core, zj, y]
        for i in range(2):
            remote(p.at[core, zj, y], ry.at[i, zj], ys.at[i, zj], yr.at[i, zj], partner).wait_recv()
            total = total + ry[i, zj]
        q[zj] = total

    def over_y_send(j, carry):
        zj = lax.rem(z + 1 + j, NZ)
        over_y(zj)
        remote(q.at[zj], rz.at[j], zs.at[j], zr.at[j], at_z(zj)).start()
        return carry

    lax.fori_loop(0, NZ - 1, over_y_send, 0)
    over_y(z)

    total = q[z]
    for j in range(NZ - 1):
        remote(q.at[z], rz.at[j], zs.at[j], zr.at[j], partner).wait_recv()
        total = total + rz[j]
    sp[...] = total

    def over_x(k, slot):
        return remote(sp.at[lax.rem(x + k + 2 * slot, NX)], rx.at[k - 1, slot], ws.at[k - 1, slot], wr.at[k - 1, slot],
                      at_x(k))

    for k in range(1, NX):
        for slot in range(2):
            over_x(k, slot).start()
    to_right[3].start()
    to_left[3].start()
    for i in range(2):
        left_arrived([i])
        right_arrived([2 + i])
    forward_right[0].start()
    forward_left[0].start()
    accumulate([(left_x, 0, half), (right_x, half, half)])
    for slot in range(2):
        total = sp[lax.rem(x + 2 * slot, NX)]
        for k in range(1, NX):
            over_x(k, slot).wait_recv()
            total = total + rx[k - 1, slot]
        s[core, z, y, slot] = total

    own = s.at[core, z, y]

    def along_z(k):
        return lax.rem(z + NZ - k, NZ)

    def same(piece, send, recv, device):
        return remote(piece, piece, send, recv, device)

    def spread(k):
        piece = s.at[core, along_z(k), y]
        same(piece, gys.at[0, k], gyr.at[0, k], to_up).start()
        same(piece, gys.at[1, k], gyr.at[1, k], to_down).start()

    for k in range(1, NZ):
        same(own, gzs.at[k - 1], gzr.at[k - 1], at_z(lax.rem(z + k, NZ))).start()
    spread(0)

    def from_z(k, carry):
        same(s.at[core, along_z(k), y], gzs.at[k - 1], gzr.at[k - 1], partner).wait_recv()
        spread(k)
        return carry

    lax.fori_loop(1, NZ, from_z, 0)

    def to_partner(r):
        return same(s.at[core, :, lax.rem(y + r, NY)], gcs.at[r], gcr.at[r], partner)

    to_partner(0).start()

    def from_y(first):
        def body(k, carry):
            zz = along_z(k)
            lower, upper = s.at[core, zz, down], s.at[core, zz, up]
            same(lower, gys.at[0, k], gyr.at[0, k], partner).wait_recv()
            same(upper, gys.at[1, k], gyr.at[1, k], partner).wait_recv()
            if first:
                same(lower, ghs.at[k], ghr.at[k], to_up).start()
            else:
                same(upper, ghs.at[k], ghr.at[k], to_down).start()
            return carry
        return body

    lax.fori_loop(0, NZ // 2, from_y(True), 0)
    lax.fori_loop(NZ // 2, NZ, from_y(False), 0)
    to_partner(NY - 1).start()
    to_partner(1).start()

    def from_far(k, carry):
        same(s.at[core, along_z(k), far_y], ghs.at[k], ghr.at[k], partner).wait_recv()
        return carry

    lax.fori_loop(0, NZ, from_far, 0)
    to_partner(2).start()
    for r in range(NY):
        same(s.at[other, :, lax.rem(y + r, NY)], gcs.at[r], gcr.at[r], partner).wait_recv()

    def two_terms(dst, slot):
        for m in range(2):
            for zz in range(NZ):
                for yy in range(NY):
                    d0 = (zz * NY + yy) * 128
                    high, low = split(s[m, zz, yy, slot])
                    dst[m * 64:m * 64 + 32, d0:d0 + 128] = high
                    dst[m * 64 + 32:m * 64 + 64, d0:d0 + 128] = low

    two_terms(sf, 1)
    u = dot(sf[...], a[x], NT)
    for m in range(2):
        us[m * RANK:(m + 1) * RANK, :] = u[m * 64:m * 64 + 32] + u[m * 64 + 32:m * 64 + 64]
    to_far = remote(us, uf, us_sem.at[0], ur_sem.at[0], at_x(2))
    to_far.start()
    forward_right[1].start()
    forward_left[1].start()
    two_terms(sb, 0)

    right = []
    for m in range(2):
        both = dot(sb[m * 64:m * 64 + 64, :], e[m])
        right.append(both[:RANK] + both[RANK:])

    def add_right(slot, m, um):
        tok = pl.ds(pl.multiple_of(slot * tokens, tokens), tokens)
        both = dot(jnp.concatenate(split(um), axis=0), c[m, tok, :])
        right[m] = right[m] + both[:RANK] + both[RANK:]

    left_arrived([2, 3])
    right_arrived([0, 1])
    for slot in (x, left_x, right_x):
        u = dot(sb[...], a[slot], NT)
        for m in range(2):
            add_right(slot, m, u[m * 64:m * 64 + 32] + u[m * 64 + 32:m * 64 + 64])
    states = []
    for m in range(2):
        both = dot(sb[m * 64:m * 64 + 64, :], sb[m * 64:m * 64 + 64, :], NT)
        states.append(elimination(
            both[:RANK, :RANK] + both[:RANK, RANK:] + both[RANK:, :RANK] + both[RANK:, RANK:]))
    to_far.wait_recv()
    for m in range(2):
        add_right(far_x, m, uf[m * RANK:(m + 1) * RANK, :])

    group = t.shape[2]
    per_row = kv // 128

    def piece(i):
        return i // group, i % group

    for m in range(2):
        for i in range(NZ * group):
            rr, kk = i // per_row, i % per_row
            t[(m,) + piece(i)] = right[m][rr * 8:rr * 8 + 8, kk * 128:kk * 128 + 128]
    for i, (d, k) in enumerate(plane):
        zk, ck = lax.rem(z + k, NZ), (core, other)[d]
        remote(t.at[ck, zk], ta.at[i], tas.at[i], tar.at[i], at_zc(zk, ck)).start()
    states = [eliminate(state, 0, 11) for state in states]
    accumulate([(left_x, half, half), (right_x, 0, half)])
    total = t[core, z]
    for i in range(len(plane)):
        remote(t.at[core, z], ta.at[i], tas.at[i], tar.at[i], partner).wait_recv()
        total = total + ta[i]
    t2[...] = total
    for k in range(1, NY):
        remote(t2, ty.at[k - 1], tys.at[k - 1], tyr.at[k - 1], at_y(k)).start()
    states = [eliminate(state, 11, 22) for state in states]
    for k in range(1, NY):
        remote(t2, ty.at[k - 1], tys.at[k - 1], tyr.at[k - 1], partner).wait_recv()
        total = total + ty[k - 1]
    tf[core, z] = total
    own_t = tf.at[core, z]
    for i, (d, k) in enumerate(plane):
        remote(own_t, own_t, tgs.at[i], tgr.at[i], at_zc(lax.rem(z + k, NZ), (core, other)[d])).start()
    inverse = [inverse_factor(eliminate(state, 22, RANK)) for state in states]
    for m in range(2):
        high, low = split(inverse[m])
        pair = jnp.concatenate([high, low], axis=0)
        for i in range(width // step):
            at = pl.ds(i * step, step)
            both = dot(pair, sb[m * 64:m * 64 + 32, at])
            lt = both[:RANK] + both[RANK:] + dot(high, sb[m * 64 + 32:m * 64 + 64, at])
            left[m, :, at] = lt
            lh, ll = split(lt)
            stack[m * 96:m * 96 + 96, at] = jnp.concatenate([lh, ll, lh], axis=0)
    store_left = pltpu.make_async_copy(left, left_hbm, lsem.at[4])
    store_left.start()
    far_arrived()
    accumulate([(far_x, 0, tokens)])
    for i, (d, k) in enumerate(plane):
        got = tf.at[(core, other)[d], lax.rem(z + NZ - k, NZ)]
        remote(got, got, tgs.at[i], tgr.at[i], partner).wait_recv()

    means = []
    for m in range(2):
        tt = jnp.concatenate(
            [jnp.concatenate([tf[(m,) + piece(rr * per_row + kk)] for kk in range(per_row)], axis=1)
             for rr in range(RANK // 8)], axis=0)
        wh, wl = split(inverse[m])
        th, tl = split(tt)
        both = dot(jnp.concatenate([wh, wl], axis=0), th)
        mean = (both[:RANK] + both[RANK:] + dot(wh, tl)) * (1.0 / ndp)
        means_f32[m] = mean
        mh, ml = split(mean)
        means.append(jnp.concatenate([mh, mh, ml], axis=0))
    store_mean = pltpu.make_async_copy(means_f32, mean_hbm, lsem.at[5])
    store_mean.start()

    def store_new(i):
        at = pl.ds(pl.multiple_of(i * step, step), step)
        return pltpu.make_async_copy(new.at[:, at], new_hbm.at[:, at], out_sem.at[i])

    def finish(i, carry):
        at = pl.ds(pl.multiple_of(i * step, step), step)
        for m in range(2):
            approx = dot(stack[m * 96:m * 96 + 96, at], means[m], TN)
            new[m, at, :] = (mem[m, at, :] - approx).astype(BF)
        store_new(i).start()
        return carry

    lax.fori_loop(0, width // step, finish, 0)

    for copy in v_copies + to_right + to_left + forward_right + forward_left:
        copy.wait_send()

    def sent(j, carry):
        remote(p.at[other, j], rc.at[j], cs.at[j], cr.at[j], partner).wait_send()
        for i in range(2):
            remote(fy.at[i, j], fy.at[i, j], fs.at[i, j], fr.at[i, j], partner).wait_send()
            remote(p.at[core, j, y], ry.at[i, j], ys.at[i, j], yr.at[i, j], partner).wait_send()
        return carry

    lax.fori_loop(0, NZ, sent, 0)
    for j in range(NZ - 1):
        remote(q.at[j], rz.at[j], zs.at[j], zr.at[j], partner).wait_send()
        same(own, gzs.at[j], gzr.at[j], partner).wait_send()
    for k in range(1, NX):
        for slot in range(2):
            over_x(k, slot).wait_send()

    def sent_s(k, carry):
        same(own, gys.at[0, k], gyr.at[0, k], partner).wait_send()
        same(own, gys.at[1, k], gyr.at[1, k], partner).wait_send()
        same(own, ghs.at[k], ghr.at[k], partner).wait_send()
        return carry

    lax.fori_loop(0, NZ, sent_s, 0)
    for r in range(NY):
        to_partner(r).wait_send()
    to_far.wait_send()
    for i in range(len(plane)):
        remote(t2, ta.at[i], tas.at[i], tar.at[i], partner).wait_send()
        remote(own_t, own_t, tgs.at[i], tgr.at[i], partner).wait_send()
    for k in range(NY - 1):
        remote(t2, ty.at[k], tys.at[k], tyr.at[k], partner).wait_send()
    store_left.wait()
    store_mean.wait()

    def stored(i, carry):
        store_new(i).wait()
        return carry

    lax.fori_loop(0, width // step, stored, 0)


def hand_over(parts, new_hbm, left_hbm, mean_hbm, new_out, left_out, mean_out, new, left, mean, load_sem, store_sem):
    rows = new_hbm.shape[1] // parts
    at = [(m, pl.ds(i * rows, rows)) for m in range(2) for i in range(parts)]
    moves = [(new_hbm.at[w], new.at[w], new_out.at[w]) for w in at]
    moves += [(left_hbm.at[m], left.at[m], left_out.at[m]) for m in range(2)]
    moves += [(mean_hbm, mean, mean_out)]
    loads = [pltpu.make_async_copy(src, mid, load_sem.at[i]) for i, (src, mid, dst) in enumerate(moves)]
    stores = [pltpu.make_async_copy(mid, dst, store_sem.at[i]) for i, (src, mid, dst) in enumerate(moves)]
    for load in loads:
        load.start()
    for load, store in zip(loads, stores):
        load.wait()
        store.start()
    for store in stores:
        store.wait()


def shards(NY, NZ, activations, cotangent, error_memory, right_factor):
    tokens, width = activations.shape
    kv = cotangent.shape[2]
    error_memory = error_memory[:, 0]
    group = RANK * kv // (8 * 128 * NZ)
    dma = pltpu.SemaphoreType.DMA
    any_spec = pl.BlockSpec(memory_space=pl.ANY)
    new_error, left, mean = pl.pallas_call(
        functools.partial(fused, NY, NZ),
        out_shape=(
            jax.ShapeDtypeStruct((2, width, kv), BF),
            jax.ShapeDtypeStruct((2, RANK, width), F32),
            jax.ShapeDtypeStruct((2, RANK, kv), F32),
        ),
        in_specs=[any_spec] * 4,
        out_specs=(any_spec,) * 3,
        scratch_shapes=[
            pltpu.VMEM((NX, tokens, width), BF),
            pltpu.VMEM((2, NX * tokens, kv), BF),
            pltpu.VMEM((2, width, kv), BF),
            pltpu.VMEM((2, RANK, kv), F32),
            pltpu.VMEM((NX, 2 * RANK, tokens), F32),
            pltpu.VMEM((NX, 2 * RANK, tokens), F32),
            pltpu.VMEM((4 * NX * RANK, tokens), BF),
            pltpu.VMEM((2, 2 * RANK, kv), BF),
            pltpu.VMEM((2, NZ, NY, RANK, 128), F32),
            pltpu.VMEM((2, NZ, NY, NX, RANK, 128), F32),
            pltpu.VMEM((NZ, NY, NX, RANK, 128), F32),
            pltpu.VMEM((2, NZ, NX // 2, RANK, 128), F32),
            pltpu.VMEM((2, NZ, NX, RANK, 128), F32),
            pltpu.VMEM((NZ, NX, RANK, 128), F32),
            pltpu.VMEM((NZ - 1, NX, RANK, 128), F32),
            pltpu.VMEM((NX, RANK, 128), F32),
            pltpu.VMEM((NX - 1, 2, RANK, 128), F32),
            pltpu.VMEM((2, NZ, NY, 2, RANK, 128), F32),
            pltpu.VMEM((4 * RANK, width), BF),
            pltpu.VMEM((4 * RANK, width), BF),
            pltpu.VMEM((2 * RANK, tokens), F32),
            pltpu.VMEM((2 * RANK, tokens), F32),
            pltpu.VMEM((2, RANK, width), F32),
            pltpu.VMEM((6 * RANK, width), BF),
            pltpu.VMEM((2, width, kv), F32),
            pltpu.VMEM((2, width, kv), BF),
            pltpu.VMEM((2, RANK, kv), F32),
            pltpu.VMEM((2, NZ, group, 8, 128), F32),
            pltpu.VMEM((2 * NZ - 1, group, 8, 128), F32),
            pltpu.VMEM((group, 8, 128), F32),
            pltpu.VMEM((NY - 1, group, 8, 128), F32),
            pltpu.VMEM((2, NZ, group, 8, 128), F32),
            dma((6,)),
            dma((NX - 1,)), dma((NX - 1,)),
            dma((12,)), dma((12,)),
            dma((NZ,)), dma((NZ,)),
            dma((2, NZ)), dma((2, NZ)),
            dma((2, NZ)), dma((2, NZ)),
            dma((NZ - 1,)), dma((NZ - 1,)),
            dma((NX - 1, 2)), dma((NX - 1, 2)),
            dma((NZ - 1,)), dma((NZ - 1,)),
            dma((2, NZ)), dma((2, NZ)),
            dma((NZ,)), dma((NZ,)),
            dma((NY,)), dma((NY,)),
            dma((1,)), dma((1,)),
            dma((2 * NZ - 1,)), dma((2 * NZ - 1,)),
            dma((NY - 1,)), dma((NY - 1,)),
            dma((2 * NZ - 1,)), dma((2 * NZ - 1,)),
            dma((max(1, width // 512),)),
        ],
        compiler_params=pltpu.CompilerParams(
            collective_id=0, has_side_effects=True, vmem_limit_bytes=56 * 1024 * 1024),
    )(activations, cotangent, error_memory, jnp.swapaxes(right_factor, 1, 2))

    parts = 4
    new_error, left, mean = pl.pallas_call(
        functools.partial(hand_over, parts),
        out_shape=(
            jax.ShapeDtypeStruct((2, width, kv), BF),
            jax.ShapeDtypeStruct((2, RANK, width), F32),
            jax.ShapeDtypeStruct((2, RANK, kv), F32),
        ),
        in_specs=[any_spec] * 3,
        out_specs=(any_spec,) * 3,
        scratch_shapes=[
            pltpu.VMEM((2, width, kv), BF),
            pltpu.VMEM((2, RANK, width), F32),
            pltpu.VMEM((2, RANK, kv), F32),
            dma((2 * parts + 3,)),
            dma((2 * parts + 3,)),
        ],
        compiler_params=pltpu.CompilerParams(vmem_limit_bytes=56 * 1024 * 1024),
    )(new_error, left, mean)
    return (new_error[:, None], jnp.swapaxes(left, 1, 2)[:, None], jnp.swapaxes(mean, 1, 2))


def build(mesh, NY, NZ):
    return jax.shard_map(
        functools.partial(shards, NY, NZ),
        mesh=mesh,
        in_specs=(
            P(("dp", "tensor"), None),
            P(None, "dp", "tensor"),
            P(None, "dp", None, "tensor"),
            P(None, "tensor", None),
        ),
        out_specs=(
            P(None, "dp", None, "tensor"),
            P(None, "tensor", None, None),
            P(None, "tensor", None),
        ),
        check_vma=False,
    )


def solution(mesh):
    return build(mesh, 4, mesh.shape["dp"] // 8)
```
